256 devices in a mesh: patch: 128 (over z_hi, y, x, core), cfg: 2 (over z_lo).
Axes of the slice: x: 4, y: 4, z: 8 (z_hi: 4, z_lo: 2; z = z_hi * 2 + z_lo), core: 2. Of those that a mesh axis runs over, the one named last changes fastest.
Arguments:
- tokens: bfloat16 [2, 32768, 1280], P('cfg', 'patch'), may hold values from -12 to 12
- stale_keys: bfloat16 [2, 2048, 2560], P('cfg', 'patch'), may hold values from -64 to 64
- norm_gain: float32 [1280], replicated, may hold values from 0.25 to 1.75
- norm_bias: float32 [1280], replicated, may hold values from -3 to 3
- query_weight: bfloat16 [1280, 1280], replicated, may hold values from -0.15625 to 0.15625
- pair_weight: bfloat16 [1280, 2560], replicated, may hold values from -0.15625 to 0.15625
Outputs:
- attended: bfloat16 [2, 32768, 1280], P('cfg', 'patch')
- fresh_keys: bfloat16 [2, 2048, 2560], P('cfg', 'patch')
The draws below stay inside these ranges and needn't reach their ends.
All inputs are finite; a program needn't handle non-finite values.
Results may differ from the reference program's by a relative error of at most 0.008.
The reference program's roundings to bfloat16 on the way (of `normed`, `pooled`, `queries`, `table` and `rounded`) count: a program that leaves them out, or rounds other values in their place, can miss the bound.
Values may be sent and summed in bfloat16 or wider, within the bound.
No kernel may reach another device: no remote copies, remote signals or barrier semaphores. Data moves between devices by JAX's collectives and lax.ppermute only.
A program may use at most 128 MiB of HBM per device.

```python
import jax
import jax.numpy as jnp
from jax import lax

D = 1280
HEADS = 20
HEAD_DIM = 64
GROUPS = 32
BRANCHES = 2
POOL = 4
GW = 64
TOK_DEV = 256
KV_DEV = 16
ROWS = 512
TOKENS = 32768
KV_TOK = 2048
N_PATCH = 128


def draw_tokens(key, part):
    key = jax.random.fold_in(key, 11)
    keys = jax.random.split(key, 3)
    shape = (BRANCHES, TOKENS, D)
    rows = (jnp.arange(TOKENS, dtype=jnp.int32) // GW).astype(jnp.float32)
    rising = jnp.exp(jnp.log(3.0) * rows / (ROWS - 1))[None, :, None]
    rough = jnp.exp(jax.random.uniform(keys[1], (BRANCHES, TOKENS, 1), jnp.float32, -0.7, 0.7))
    offset = 0.5 * jax.random.normal(keys[2], (BRANCHES, 1, D), jnp.float32)
    base = jax.random.normal(keys[0], shape, jnp.float32)
    return jnp.clip(offset + rising * rough * base, -12.0, 12.0).astype(jnp.bfloat16)


def draw_stale_keys(key, part):
    key = jax.random.fold_in(key, 23)
    keys = jax.random.split(key, 2)
    shape = (BRANCHES, KV_TOK, 2 * D)
    rough = jnp.exp(jax.random.uniform(keys[1], (BRANCHES, KV_TOK, 1), jnp.float32, -0.5, 0.5))
    base = jax.random.normal(keys[0], shape, jnp.float32) * rough
    return jnp.clip(base, -64.0, 64.0).astype(jnp.bfloat16)


def normal_values(rng, shape, width, bound, kind=jnp.bfloat16):
    result = jax.random.normal(rng, shape, jnp.float32) * width
    return jnp.minimum(jnp.maximum(result, -bound), bound).astype(kind)


def setup_inputs(seed: int = 0) -> dict:
    streams_of = jax.random.split(jax.random.key(seed), 7)
    return {
        "tokens": draw_tokens(jax.random.fold_in(streams_of[6], 71), 0),
        "stale_keys": draw_stale_keys(jax.random.fold_in(streams_of[6], 71), 0),
        "norm_gain": jnp.clip(1.0 + 0.15 * jax.random.normal(streams_of[2], (D,), jnp.float32), 0.25, 1.75),
        "norm_bias": normal_values(streams_of[3], (D,), 0.5, 3.0, jnp.float32),
        "query_weight": normal_values(streams_of[4], (D, D), D ** -0.5, 0.15625),
        "pair_weight": normal_values(streams_of[5], (D, 2 * D), D ** -0.5, 0.15625),
    }


epsilon = 1e-05

def group_norm(branch, norm_gain, norm_bias):
    values = branch.astype(jnp.float32).reshape(branch.shape[0], GROUPS, D // GROUPS)
    center = lax.optimization_barrier(jnp.mean(values, axis=(0, 2)))
    shifted = values - center[None, :, None]
    spread = lax.optimization_barrier(jnp.mean(shifted * shifted, axis=(0, 2)))
    scaled = shifted * lax.rsqrt(spread + epsilon)[None, :, None]
    return (scaled.reshape(branch.shape[0], D) * norm_gain + norm_bias).astype(jnp.bfloat16)

def pool_cells(normed):
    blocks = normed.astype(jnp.float32).reshape(ROWS // POOL, POOL, GW // POOL, POOL, D)
    return lax.optimization_barrier(jnp.mean(blocks, axis=(1, 3))).reshape(KV_TOK, D).astype(jnp.bfloat16)

def attend(queries, table):
    score_scale = HEAD_DIM ** (-0.5)
    outputs = []
    for first_head in range(0, HEADS, 4):
        head_count = min(4, HEADS - first_head)
        column_low = first_head * HEAD_DIM
        column_high = column_low + head_count * HEAD_DIM
        heads_query = queries[:, column_low:column_high].astype(jnp.float32).reshape(queries.shape[0], head_count, HEAD_DIM)
        heads_key = table[:, column_low:column_high].astype(jnp.float32).reshape(table.shape[0], head_count, HEAD_DIM)
        heads_value = table[:, D + column_low:D + column_high].astype(jnp.float32).reshape(table.shape[0], head_count, HEAD_DIM)
        scores = jnp.einsum('thd,khd->htk', heads_query, heads_key) * score_scale
        largest = lax.optimization_barrier(jnp.max(scores, axis=2))
        weights = jnp.exp(scores - largest[:, :, None])
        totals = lax.optimization_barrier(jnp.sum(weights, axis=2))
        rounded = lax.optimization_barrier(weights.astype(jnp.bfloat16)).astype(jnp.float32)
        summed = jnp.einsum('htk,khd->thd', rounded, heads_value) / jnp.transpose(totals)[:, :, None]
        outputs.append(summed.reshape(queries.shape[0], head_count * HEAD_DIM))
    return jnp.concatenate(outputs, axis=1).astype(jnp.bfloat16)

def reference(tokens, stale_keys, norm_gain, norm_bias, query_weight, pair_weight):
    attended_all = []
    fresh_all = []
    for branch_index in range(BRANCHES):
        branch = tokens[branch_index]
        normed = group_norm(branch, norm_gain, norm_bias)
        pooled = pool_cells(normed)
        fresh_pairs = jnp.dot(pooled, pair_weight, preferred_element_type=jnp.float32).astype(jnp.bfloat16)
        queries = jnp.dot(normed, query_weight, preferred_element_type=jnp.float32).astype(jnp.bfloat16)
        stale_rows = stale_keys[branch_index]

        def one_patch(patch_index):
            offset = (patch_index * KV_DEV).astype(jnp.int32)
            own_rows = lax.dynamic_slice_in_dim(fresh_pairs, offset, KV_DEV, 0)
            table = lax.dynamic_update_slice_in_dim(stale_rows, own_rows, offset, 0)
            block = lax.dynamic_slice_in_dim(queries, (patch_index * TOK_DEV).astype(jnp.int32), TOK_DEV, 0)
            return attend(block, table)
        attended = lax.map(one_patch, jnp.arange(N_PATCH, dtype=jnp.int32)).reshape(TOKENS, D)
        attended_all.append(attended)
        fresh_all.append(fresh_pairs)
    return (jnp.stack(attended_all), jnp.stack(fresh_all))
```

```python
import functools

import jax
import jax.numpy as jnp
from jax import lax
from jax.experimental import pallas as pl
from jax.experimental.pallas import tpu as pltpu
from jax.sharding import PartitionSpec as P

HEADS = 20
HEAD_DIM = 64
GROUPS = 32
POOL = 4
WIDTH = 1280
CELLS = 256
ROWS = 16
GROUP_WIDTH = WIDTH // GROUPS
LANES = 128
SET_TILES = 5
TABLE_WIDTH = SET_TILES * LANES
QUERY_WIDTH = 3 * LANES
epsilon = 1e-05

f32 = jnp.float32
bf16 = jnp.bfloat16
HIGHEST = lax.Precision.HIGHEST
VMEM = pl.BlockSpec(memory_space=pltpu.VMEM)
SMEM = pl.BlockSpec(memory_space=pltpu.SMEM)


def iota(shape, axis):
    return lax.broadcasted_iota(jnp.int32, shape, axis)


def group_of_channel():
    low = iota((WIDTH, LANES), 1) * GROUP_WIDTH
    channel = iota((WIDTH, LANES), 0)
    return ((channel >= low) & (channel < low + GROUP_WIDTH)).astype(f32)


def channel_of_group():
    low = iota((LANES, WIDTH), 0) * GROUP_WIDTH
    channel = iota((LANES, WIDTH), 1)
    return ((channel >= low) & (channel < low + GROUP_WIDTH)).astype(f32)


def exact_dot(left, right):
    return jnp.dot(left, right, precision=HIGHEST, preferred_element_type=f32)


def combine(parts, entries):
    mean = sum(part[0:1] for part in parts) / len(parts)
    squares = sum(part[1:2] for part in parts)
    apart = sum((part[0:1] - mean) * (part[0:1] - mean) for part in parts)
    return mean, squares + entries * apart


def stack_stats(mean, squares):
    row = iota((8, LANES), 0)
    return jnp.where(row == 0, mean, jnp.where(row == 1, squares, 0.0))


def encode(stats):
    high = stats.astype(bf16).astype(f32)
    rest = stats - high
    middle = rest.astype(bf16).astype(f32)
    low = rest - middle
    row = jnp.concatenate([high, middle, low], axis=1)
    return jnp.concatenate([row, jnp.zeros_like(row)], axis=0).astype(bf16)


def decode(rows):
    parts = rows.astype(f32)
    return (
        parts[0:8, 0:LANES] + parts[0:8, LANES : 2 * LANES] + parts[0:8, 2 * LANES : 3 * LANES]
    )


def head_tiles(pairs):
    lane = iota((ROWS, LANES), 1)
    even, odd = [], []
    for t in range(WIDTH // LANES):
        keys = pairs[:, t * LANES : (t + 1) * LANES].astype(f32)
        values = pairs[:, WIDTH + t * LANES : WIDTH + (t + 1) * LANES].astype(f32)
        turned = pltpu.roll(values, HEAD_DIM, 1)
        even.append(jnp.where(lane < HEAD_DIM, keys, turned).astype(bf16))
        odd.append(jnp.where(lane < HEAD_DIM, turned, keys).astype(bf16))
    sets = []
    for j in range(4):
        last = (even if j % 2 == 0 else odd)[8 + j // 2]
        sets.append(
            jnp.concatenate(
                [even[2 * j], odd[2 * j], even[2 * j + 1], odd[2 * j + 1], last], axis=1
            )
        )
    return sets


def local_kernel(tokens_ref, stale_ref, stats_ref, sets_ref):
    values = tokens_ref[...].astype(f32)
    to_group = group_of_channel()
    sums = jnp.broadcast_to(jnp.sum(values, axis=0, keepdims=True), (8, WIDTH))
    mean = exact_dot(sums, to_group) / (CELLS * GROUP_WIDTH)
    center = exact_dot(mean, channel_of_group())
    shifted = values - center[0:1]
    squares = jnp.broadcast_to(jnp.sum(shifted * shifted, axis=0, keepdims=True), (8, WIDTH))
    squares = exact_dot(squares, to_group)
    stats_ref[...] = stack_stats(mean, squares)
    for j, block in enumerate(head_tiles(stale_ref[...])):
        sets_ref[j] = block


def x_kernel(place_ref, own_ref, other_ref, sets_ref, *out_refs):
    mean, squares = combine([own_ref[...], other_ref[...]], CELLS * GROUP_WIDTH)
    coded = encode(stack_stats(mean, squares))
    place = place_ref[0]
    for k, out_ref in enumerate(out_refs):
        out_ref[0:ROWS, :] = sets_ref[lax.rem(place + k, 4)]
        out_ref[ROWS : 2 * ROWS, 0:QUERY_WIDTH] = coded
        out_ref[ROWS : 2 * ROWS, QUERY_WIDTH:] = jnp.zeros(
            (ROWS, TABLE_WIDTH - QUERY_WIDTH), bf16
        )


def z_kernel(*refs):
    *in_refs, out_ref = refs
    stats = [decode(ref[ROWS : 2 * ROWS, 0:QUERY_WIDTH]) for ref in in_refs]
    mean, squares = combine(stats, 2 * CELLS * GROUP_WIDTH)
    for k, ref in enumerate(in_refs):
        out_ref[k * ROWS : (k + 1) * ROWS, :] = ref[0:ROWS, :]
    out_ref[4 * ROWS : 5 * ROWS, 0:QUERY_WIDTH] = encode(stack_stats(mean, squares))
    out_ref[4 * ROWS : 5 * ROWS, QUERY_WIDTH:] = jnp.zeros(
        (ROWS, TABLE_WIDTH - QUERY_WIDTH), bf16
    )


def y_kernel(*refs):
    *in_refs, stats_ref, out_ref = refs
    stats = [decode(ref[4 * ROWS : 5 * ROWS, 0:QUERY_WIDTH]) for ref in in_refs]
    mean, squares = combine(stats, 8 * CELLS * GROUP_WIDTH)
    stats_ref[...] = stack_stats(mean, squares)
    for k, ref in enumerate(in_refs):
        out_ref[k * 4 * ROWS : (k + 1) * 4 * ROWS, :] = ref[0 : 4 * ROWS, :]


def project_kernel(
    place_ref, tokens_ref, s0, s1, s2, s3, gain_ref, bias_ref, query_ref, pair_ref, *refs
):
    *message_refs, fresh_ref, sets_ref, last_ref = refs
    mean, squares = combine([s0[...], s1[...], s2[...], s3[...]], 32 * CELLS * GROUP_WIDTH)
    spread = squares / (128 * CELLS * GROUP_WIDTH)
    row = iota((8, LANES), 0)
    both = jnp.where(row == 0, mean, lax.rsqrt(spread + epsilon))
    channels = exact_dot(both, channel_of_group())
    scaled = (tokens_ref[...].astype(f32) - channels[0:1]) * channels[1:2]
    normed = (scaled * gain_ref[...] + bias_ref[...]).astype(bf16)

    square = iota((ROWS, CELLS), 0)
    cell = iota((ROWS, CELLS), 1)
    cell_square = lax.shift_right_logical(lax.bitwise_and(cell, 63), 2)
    pool = jnp.where(cell_square == square, 1.0 / (POOL * POOL), 0.0).astype(bf16)
    pooled = jnp.dot(pool, normed, preferred_element_type=f32).astype(bf16)

    place = place_ref[0]
    last = jnp.dot(normed, query_ref[:, 1024:], preferred_element_type=f32).astype(bf16)
    last_ref[0] = last[:, 0:LANES]
    last_ref[1] = last[:, LANES:]
    for k in (1, 3, 2, 0):
        j = lax.rem(place + k, 4)
        columns = pl.ds(pl.multiple_of(j * 256, 256), 256)
        block = jnp.dot(normed, query_ref[:, columns], preferred_element_type=f32)
        message_refs[k][0:CELLS, 0:256] = block.astype(bf16)
        message_refs[k][0:CELLS, 256:] = last_ref[lax.shift_right_logical(j, 1)]

    fresh = jnp.dot(pooled, pair_ref[...], preferred_element_type=f32).astype(bf16)
    fresh_ref[...] = fresh
    for j, block in enumerate(head_tiles(fresh)):
        sets_ref[j] = block
    for k in range(4):
        block = sets_ref[lax.rem(place + k, 4)]
        message_refs[k][CELLS : CELLS + ROWS, :] = block[:, 0:QUERY_WIDTH]
        message_refs[k][CELLS + ROWS : CELLS + 2 * ROWS, 0:256] = block[:, QUERY_WIDTH:]
        message_refs[k][CELLS + ROWS : CELLS + 2 * ROWS, 256:] = jnp.zeros((ROWS, LANES), bf16)


def attend_kernel(source, place_ref, message_ref, *refs):
    *table_refs, out_ref, first_ref = refs
    first_ref[...] = table_refs[0][...]
    low = source * ROWS
    first_ref[low : low + ROWS, 0:QUERY_WIDTH] = message_ref[CELLS : CELLS + ROWS, :]
    first_ref[low : low + ROWS, QUERY_WIDTH:] = message_ref[CELLS + ROWS : CELLS + 2 * ROWS, 0:256]
    pieces = [first_ref] + table_refs[1:]
    lane = iota((CELLS, LANES), 1)
    low_half = lane < HEAD_DIM
    parity = lax.bitwise_and(place_ref[0], 1)
    factor = HEAD_DIM ** (-0.5) * 1.4426950408889634
    results = []
    for h in range(SET_TILES):
        queries = message_ref[0:CELLS, (h // 2) * LANES : (h // 2 + 1) * LANES]
        if h < 4:
            mask = low_half if h % 2 == 0 else jnp.logical_not(low_half)
        else:
            mask = lax.shift_right_logical(lane, 6) == parity
        queries = jnp.where(mask, queries.astype(f32), 0.0).astype(bf16)
        tiles = [ref[:, h * LANES : (h + 1) * LANES] for ref in pieces]
        scores = [
            lax.dot_general(queries, tile, (((1,), (1,)), ((), ())), preferred_element_type=f32)
            for tile in tiles
        ]
        largest = scores[0]
        for part in scores[1:]:
            largest = jnp.maximum(largest, part)
        largest = jnp.max(largest, axis=1, keepdims=True)
        total = None
        summed = None
        for part, tile in zip(scores, tiles):
            weights = jnp.exp2((part - largest) * factor)
            product = jnp.dot(weights.astype(bf16), tile, preferred_element_type=f32)
            total = weights if total is None else total + weights
            summed = product if summed is None else summed + product
        total = jnp.sum(total, axis=1, keepdims=True)
        results.append(summed / total)
    for t in range(2):
        both = jnp.where(low_half, results[2 * t + 1], results[2 * t])
        out_ref[:, t * LANES : (t + 1) * LANES] = pltpu.roll(both, HEAD_DIM, 1).astype(bf16)
    out_ref[:, 256:] = pltpu.roll(results[4], HEAD_DIM, 1).astype(bf16)


def assemble_kernel(place_ref, *refs):
    *in_refs, out_ref, pair_ref, last_ref = refs
    place = place_ref[0]
    for k, ref in enumerate(in_refs):
        j = lax.rem(place + k, 4)
        pair_ref[j] = ref[:, 0:256]
        last_ref[j] = ref[:, 256:]
    for j in range(4):
        out_ref[:, j * 256 : (j + 1) * 256] = pair_ref[j]
    low_half = iota((CELLS, LANES), 1) < HEAD_DIM
    for t in range(2):
        both = jnp.where(low_half, last_ref[2 * t].astype(f32), last_ref[2 * t + 1].astype(f32))
        out_ref[:, 1024 + t * LANES : 1024 + (t + 1) * LANES] = both.astype(bf16)


def call(kernel, ins, outs, *args, scratch=(), limit=24):
    return pl.pallas_call(
        kernel,
        in_specs=ins,
        out_specs=[VMEM] * len(outs),
        out_shape=[jax.ShapeDtypeStruct(shape, kind) for shape, kind in outs],
        scratch_shapes=list(scratch),
        compiler_params=pltpu.CompilerParams(vmem_limit_bytes=limit * 1024 * 1024),
    )(*args)


AXES = {"z": (32, 4), "y": (8, 4), "x": (2, 4), "core": (1, 2)}


def shift(array, axis, step):
    stride, size = AXES[axis]
    pairs = []
    for source in range(128):
        place = source // stride % size
        target = source + ((place + step) % size - place) * stride
        pairs.append((source, target))
    return lax.ppermute(array, "patch", pairs)


def after(array, *others):
    return lax.optimization_barrier((array, *others))[0]


def per_device(tokens, stale_keys, norm_gain, norm_bias, query_weight, pair_weight):
    tokens, stale = tokens[0], stale_keys[0]
    place = (lax.axis_index("patch") // 2 % 4).astype(jnp.int32).reshape(1)
    message = ((2 * ROWS, TABLE_WIDTH), bf16)
    stats, sets = call(
        local_kernel,
        [VMEM, VMEM],
        [((8, LANES), f32), ((4, ROWS, TABLE_WIDTH), bf16)],
        tokens,
        stale,
    )
    other = shift(stats, "core", 1)
    messages = call(
        x_kernel, [SMEM, VMEM, VMEM, VMEM], [message] * 4, place, stats, other, sets
    )
    received = [messages[0]] + [shift(messages[k], "x", k) for k in (1, 2, 3)]
    (part,) = call(z_kernel, [VMEM] * 4, [((5 * ROWS, TABLE_WIDTH), bf16)], *received)
    parts = [part] + [shift(part, "z", k) for k in (1, 2, 3)]
    stats, piece = call(
        y_kernel,
        [VMEM] * 4,
        [((8, LANES), f32), ((CELLS, TABLE_WIDTH), bf16)],
        *parts,
    )
    all_stats = [stats] + [shift(stats, "y", k) for k in (1, 2, 3)]
    pieces = [piece] + [shift(piece, "y", k) for k in (1, 3, 2)]
    pieces += [shift(block, "core", 1) for block in pieces]
    *queries, fresh = call(
        project_kernel,
        [SMEM] + [VMEM] * 9,
        [((CELLS + 2 * ROWS, QUERY_WIDTH), bf16)] * 4 + [((ROWS, 2 * WIDTH), bf16)],
        place,
        tokens,
        *all_stats,
        norm_gain.reshape(1, WIDTH),
        norm_bias.reshape(1, WIDTH),
        query_weight,
        pair_weight,
        scratch=[pltpu.VMEM((4, ROWS, TABLE_WIDTH), bf16), pltpu.VMEM((2, CELLS, LANES), bf16)],
        limit=32,
    )
    results = [None] * 4
    for k in (1, 3, 2, 0):
        asked = shift(queries[k], "x", k) if k else queries[0]
        (answer,) = call(
            functools.partial(attend_kernel, k),
            [SMEM] + [VMEM] * 9,
            [((CELLS, QUERY_WIDTH), bf16)],
            place,
            asked,
            *pieces,
            scratch=[pltpu.VMEM((CELLS, TABLE_WIDTH), bf16)],
            limit=32,
        )
        results[k] = shift(answer, "x", -k) if k else answer
    (attended,) = call(
        assemble_kernel,
        [SMEM] + [VMEM] * 4,
        [((CELLS, WIDTH), bf16)],
        place,
        *results,
        scratch=[pltpu.VMEM((4, CELLS, 256), bf16), pltpu.VMEM((4, CELLS, LANES), bf16)],
    )
    return (attended[None], fresh[None])


def solution(mesh):
    return jax.shard_map(
        per_device,
        mesh=mesh,
        in_specs=(P("cfg", "patch", None), P("cfg", "patch", None), P(), P(), P(), P()),
        out_specs=(P("cfg", "patch", None), P("cfg", "patch", None)),
        check_vma=False,
    )
```

```python
import functools

import jax
import jax.numpy as jnp
from jax import lax
from jax.experimental import pallas as pl
from jax.experimental.pallas import tpu as pltpu
from jax.sharding import PartitionSpec as P

HEADS = 20
HEAD_DIM = 64
GROUPS = 32
POOL = 4
WIDTH = 1280
CELLS = 256
ROWS = 16
GROUP_WIDTH = WIDTH // GROUPS
LANES = 128
SET_HEADS = 5
SET_ROWS = SET_HEADS * ROWS
ANSWER_ROWS = SET_HEADS * CELLS // 2
epsilon = 1e-05

f32 = jnp.float32
bf16 = jnp.bfloat16
HIGHEST = lax.Precision.HIGHEST
VMEM = pl.BlockSpec(memory_space=pltpu.VMEM)
SMEM = pl.BlockSpec(memory_space=pltpu.SMEM)
HBM = pl.BlockSpec(memory_space=pltpu.HBM)


def iota(shape, axis):
    return lax.broadcasted_iota(jnp.int32, shape, axis)


def group_of_channel():
    low = iota((WIDTH, LANES), 1) * GROUP_WIDTH
    channel = iota((WIDTH, LANES), 0)
    return ((channel >= low) & (channel < low + GROUP_WIDTH)).astype(f32)


def channel_of_group():
    low = iota((LANES, WIDTH), 0) * GROUP_WIDTH
    channel = iota((LANES, WIDTH), 1)
    return ((channel >= low) & (channel < low + GROUP_WIDTH)).astype(f32)


def exact_dot(left, right):
    return jnp.dot(left, right, precision=HIGHEST, preferred_element_type=f32)


def combine(parts, entries):
    mean = sum(part[0:1] for part in parts) / len(parts)
    squares = sum(part[1:2] for part in parts)
    apart = sum((part[0:1] - mean) * (part[0:1] - mean) for part in parts)
    return mean, squares + entries * apart


def stack_stats(mean, squares):
    row = iota((8, LANES), 0)
    return jnp.where(row == 0, mean, jnp.where(row == 1, squares, 0.0))


def encode(mean, squares):
    row = iota((ROWS, LANES), 0)
    coded = jnp.zeros((ROWS, LANES), f32)
    for i, rest in enumerate((mean, squares)):
        for part in range(3):
            rounded = rest.astype(bf16).astype(f32)
            coded = jnp.where(row == 3 * i + part, rounded, coded)
            rest = rest - rounded
    return coded.astype(bf16)


def decode(rows):
    parts = rows.astype(f32)
    return jnp.concatenate(
        [parts[0:1] + parts[1:2] + parts[2:3], parts[3:4] + parts[4:5] + parts[5:6]], axis=0
    )


def head_tiles(pairs):
    lane = iota((ROWS, LANES), 1)
    even, odd = [], []
    for t in range(WIDTH // LANES):
        keys = pairs[:, t * LANES : (t + 1) * LANES].astype(f32)
        values = pairs[:, WIDTH + t * LANES : WIDTH + (t + 1) * LANES].astype(f32)
        turned = pltpu.roll(values, HEAD_DIM, 1)
        even.append(jnp.where(lane < HEAD_DIM, keys, turned).astype(bf16))
        odd.append(jnp.where(lane < HEAD_DIM, turned, keys).astype(bf16))
    sets = []
    for j in range(4):
        last = (even if j % 2 == 0 else odd)[8 + j // 2]
        sets.append(
            jnp.concatenate(
                [even[2 * j], odd[2 * j], even[2 * j + 1], odd[2 * j + 1], last], axis=0
            )
        )
    return sets


def turn(block):
    return pltpu.roll(block.astype(f32), HEAD_DIM, 1)


def fold(block, mask):
    half = CELLS // 2
    return jnp.where(mask, block[0:half].astype(f32), turn(block[half:])).astype(bf16)


def unfold(block):
    return jnp.concatenate([block.astype(f32), turn(block)], axis=0)


def local_kernel(tokens_hbm, stale_hbm, stats_ref, sets_ref, tokens_ref, stale_ref, arrived):
    copies = [
        pltpu.make_async_copy(tokens_hbm, tokens_ref, arrived.at[0]),
        pltpu.make_async_copy(stale_hbm, stale_ref, arrived.at[1]),
    ]
    for copy in copies:
        copy.start()
    to_group, to_channel = group_of_channel(), channel_of_group()
    copies[0].wait()
    values = tokens_ref[...].astype(f32)
    sums = jnp.broadcast_to(jnp.sum(values, axis=0, keepdims=True), (8, WIDTH))
    mean = exact_dot(sums, to_group) / (CELLS * GROUP_WIDTH)
    center = exact_dot(mean, to_channel)
    shifted = values - center[0:1]
    squares = jnp.broadcast_to(jnp.sum(shifted * shifted, axis=0, keepdims=True), (8, WIDTH))
    squares = exact_dot(squares, to_group)
    stats_ref[...] = stack_stats(mean, squares)
    copies[1].wait()
    for j, block in enumerate(head_tiles(stale_ref[...])):
        sets_ref[j] = block


def x_kernel(place_ref, own_ref, other_ref, sets_ref, *out_refs):
    mean, squares = combine([own_ref[...], other_ref[...]], CELLS * GROUP_WIDTH)
    coded = encode(mean, squares)
    place = place_ref[0]
    for k, out_ref in enumerate(out_refs):
        out_ref[0:SET_ROWS, :] = sets_ref[lax.rem(place + k, 4)]
        out_ref[SET_ROWS:, :] = coded


def z_kernel(*refs):
    *in_refs, out_ref = refs
    stats = [decode(ref[SET_ROWS:, :]) for ref in in_refs]
    mean, squares = combine(stats, 2 * CELLS * GROUP_WIDTH)
    for k, ref in enumerate(in_refs):
        for h in range(SET_HEADS):
            low = h * 4 * ROWS + k * ROWS
            out_ref[low : low + ROWS, :] = ref[h * ROWS : (h + 1) * ROWS, :]
    out_ref[4 * SET_ROWS :, :] = encode(mean, squares)


def stats_kernel(*refs):
    *in_refs, stats_ref = refs
    stats = [decode(ref[4 * SET_ROWS :, :]) for ref in in_refs]
    mean, squares = combine(stats, 8 * CELLS * GROUP_WIDTH)
    stats_ref[...] = stack_stats(mean, squares)


def piece_kernel(stats_ref, *refs):
    *in_refs, out_ref = refs
    for k, ref in enumerate(in_refs):
        for h in range(SET_HEADS):
            low = h * CELLS + k * 4 * ROWS
            out_ref[low : low + 4 * ROWS, :] = ref[h * 4 * ROWS : (h + 1) * 4 * ROWS, :]


def weights_kernel(query_hbm, pair_hbm, gain_hbm, bias_hbm, *refs):
    *out_refs, arrived = refs
    copies = [
        pltpu.make_async_copy(source, target, arrived.at[i])
        for i, (source, target) in enumerate(
            zip((query_hbm, pair_hbm, gain_hbm, bias_hbm), out_refs)
        )
    ]
    for copy in copies:
        copy.start()
    for copy in copies:
        copy.wait()


def project_kernel(
    place_ref, tokens_ref, s0, s1, s2, s3, query_ref, pair_ref, gain_ref, bias_ref, *refs
):
    *message_refs, fresh_ref, sets_ref, last_ref = refs
    mean, squares = combine([s0[...], s1[...], s2[...], s3[...]], 32 * CELLS * GROUP_WIDTH)
    spread = squares / (128 * CELLS * GROUP_WIDTH)
    row = iota((8, LANES), 0)
    both = jnp.where(row == 0, mean, lax.rsqrt(spread + epsilon))
    channels = exact_dot(both, channel_of_group())
    scaled = (tokens_ref[...].astype(f32) - channels[0:1]) * channels[1:2]
    normed = (scaled * gain_ref[...] + bias_ref[...]).astype(bf16)

    square = iota((ROWS, CELLS), 0)
    cell = iota((ROWS, CELLS), 1)
    cell_square = lax.shift_right_logical(lax.bitwise_and(cell, 63), 2)
    pool = jnp.where(cell_square == square, 1.0 / (POOL * POOL), 0.0).astype(bf16)
    pooled = jnp.dot(pool, normed, preferred_element_type=f32).astype(bf16)

    place = place_ref[0]
    last = jnp.dot(normed, query_ref[:, 1024:], preferred_element_type=f32).astype(bf16)
    last_ref[0] = last[:, 0:LANES]
    last_ref[1] = last[:, LANES:]
    lane_half = lax.shift_right_logical(iota((CELLS // 2, LANES), 1), 6)
    for k in (2, 1, 3, 0):
        j = lax.rem(place + k, 4)
        columns = pl.ds(pl.multiple_of(j * 256, 256), 256)
        block = jnp.dot(normed, query_ref[:, columns], preferred_element_type=f32).astype(bf16)
        message_refs[k][0:CELLS, :] = block[:, 0:LANES]
        message_refs[k][CELLS : 2 * CELLS, :] = block[:, LANES:]
        mask = lane_half == lax.bitwise_and(j, 1)
        message_refs[k][2 * CELLS : ANSWER_ROWS, :] = fold(
            last_ref[lax.shift_right_logical(j, 1)], mask
        )

    fresh = jnp.dot(pooled, pair_ref[...], preferred_element_type=f32).astype(bf16)
    fresh_ref[...] = fresh
    for j, block in enumerate(head_tiles(fresh)):
        sets_ref[j] = block
    for k in range(4):
        message_refs[k][ANSWER_ROWS:, :] = sets_ref[lax.rem(place + k, 4)]


def attend_kernel(sources, place_ref, *refs):
    count = len(sources)
    message_refs, table_refs = refs[:count], refs[count : count + 8]
    out_refs, first_refs = refs[count + 8 : 2 * count + 8], refs[2 * count + 8 :]
    for source, message_ref, first_ref in zip(sources, message_refs, first_refs):
        first_ref[...] = table_refs[0][...]
        for h in range(SET_HEADS):
            low = h * CELLS + source * ROWS
            fresh = message_ref[ANSWER_ROWS + h * ROWS : ANSWER_ROWS + (h + 1) * ROWS, :]
            first_ref[low : low + ROWS, :] = fresh
    lane = iota((CELLS, LANES), 1)
    low_half = lane < HEAD_DIM
    parity = lax.bitwise_and(place_ref[0], 1)
    factor = HEAD_DIM ** (-0.5) * 1.4426950408889634
    against = (((1,), (1,)), ((), ()))
    results = []
    for h in range(SET_HEADS):
        if h < 4:
            mask = low_half if h % 2 == 0 else jnp.logical_not(low_half)
        else:
            mask = lax.shift_right_logical(lane, 6) == parity
        groups = []
        for message_ref in message_refs:
            if h < 4:
                queries = message_ref[(h // 2) * CELLS : (h // 2 + 1) * CELLS, :].astype(f32)
            else:
                queries = unfold(message_ref[2 * CELLS : ANSWER_ROWS, :])
            groups.append(jnp.where(mask, queries, 0.0).astype(bf16))
        queries = jnp.concatenate(groups, axis=0) if count > 1 else groups[0]
        head = slice(h * CELLS, (h + 1) * CELLS)
        firsts = [ref[head, :] for ref in first_refs]
        tiles = [ref[head, :] for ref in table_refs[1:]]
        scores = [
            jnp.concatenate(
                [
                    lax.dot_general(group, tile, against, preferred_element_type=f32)
                    for group, tile in zip(groups, firsts)
                ],
                axis=0,
            )
        ]
        for tile in tiles:
            scores.append(lax.dot_general(queries, tile, against, preferred_element_type=f32))
        largest = scores[0]
        for part in scores[1:]:
            largest = jnp.maximum(largest, part)
        largest = jnp.max(largest, axis=1, keepdims=True)
        total = summed = None
        for index, part in enumerate(scores):
            weights = jnp.exp2((part - largest) * factor)
            total = weights if total is None else total + weights
            weights = weights.astype(bf16)
            if index == 0:
                summed = jnp.concatenate(
                    [
                        jnp.dot(
                            weights[g * CELLS : (g + 1) * CELLS],
                            tile,
                            preferred_element_type=f32,
                        )
                        for g, tile in enumerate(firsts)
                    ],
                    axis=0,
                )
            else:
                summed = summed + jnp.dot(
                    weights, tiles[index - 1], preferred_element_type=f32
                )
        results.append(summed / jnp.sum(total, axis=1, keepdims=True))
    for g, out_ref in enumerate(out_refs):
        rows = slice(g * CELLS, (g + 1) * CELLS)
        for t in range(2):
            both = jnp.where(low_half, results[2 * t + 1][rows], results[2 * t][rows])
            out_ref[t * CELLS : (t + 1) * CELLS, :] = turn(both).astype(bf16)
        half = lax.shift_right_logical(iota((CELLS // 2, LANES), 1), 6)
        out_ref[2 * CELLS :, :] = fold(turn(results[4][rows]), half == parity)


def assemble_kernel(place_ref, *refs):
    *in_refs, out_ref, sets_ref = refs
    place = place_ref[0]
    for k, ref in enumerate(in_refs):
        sets_ref[lax.rem(place + k, 4)] = ref[...]
    for j in range(4):
        for t in range(2):
            low = (2 * j + t) * LANES
            out_ref[:, low : low + LANES] = sets_ref[j, t * CELLS : (t + 1) * CELLS, :]
    low_half = iota((CELLS, LANES), 1) < HEAD_DIM
    for t in range(2):
        low = (8 + t) * LANES
        both = [unfold(sets_ref[2 * t + i, 2 * CELLS :, :]) for i in range(2)]
        out_ref[:, low : low + LANES] = jnp.where(low_half, *both).astype(bf16)


def call(kernel, ins, outs, *args, scratch=(), limit=24):
    return pl.pallas_call(
        kernel,
        in_specs=ins,
        out_specs=[VMEM] * len(outs),
        out_shape=[jax.ShapeDtypeStruct(shape, kind) for shape, kind in outs],
        scratch_shapes=list(scratch),
        compiler_params=pltpu.CompilerParams(vmem_limit_bytes=limit * 1024 * 1024),
        cost_estimate=pl.CostEstimate(flops=1, bytes_accessed=1, transcendentals=0),
    )(*args)


AXES = {"z": (32, 4), "y": (8, 4), "x": (2, 4), "core": (1, 2)}


def shift(array, axis, step):
    stride, size = AXES[axis]
    pairs = []
    for source in range(128):
        place = source // stride % size
        target = source + ((place + step) % size - place) * stride
        pairs.append((source, target))
    return lax.ppermute(array, "patch", pairs)


def after(array, *others):
    return lax.optimization_barrier((array, *others))[0]


def per_device(tokens, stale_keys, norm_gain, norm_bias, query_weight, pair_weight):
    place = (lax.axis_index("patch") // 2 % 4).astype(jnp.int32).reshape(1)
    table = ((SET_HEADS * CELLS, LANES), bf16)
    answer = ((ANSWER_ROWS, LANES), bf16)
    stats, sets, tokens = call(
        local_kernel,
        [HBM, HBM],
        [((8, LANES), f32), ((4, SET_ROWS, LANES), bf16), ((CELLS, WIDTH), bf16)],
        tokens[0],
        stale_keys[0],
        scratch=[pltpu.VMEM((ROWS, 2 * WIDTH), bf16), pltpu.SemaphoreType.DMA((2,))],
    )
    other = shift(stats, "core", 1)
    messages = call(
        x_kernel,
        [SMEM, VMEM, VMEM, VMEM],
        [((SET_ROWS + ROWS, LANES), bf16)] * 4,
        place,
        stats,
        other,
        sets,
    )
    received = [messages[0]] + [shift(messages[k], "x", k) for k in (1, 2, 3)]
    (part,) = call(z_kernel, [VMEM] * 4, [((4 * SET_ROWS + ROWS, LANES), bf16)], *received)
    parts = [part] + [shift(part, "z", k) for k in (1, 2, 3)]
    query_weight, pair_weight, norm_gain, norm_bias, _ = lax.optimization_barrier(
        (query_weight, pair_weight, norm_gain, norm_bias, part)
    )
    weights = call(
        weights_kernel,
        [HBM] * 4,
        [
            ((WIDTH, WIDTH), bf16),
            ((WIDTH, 2 * WIDTH), bf16),
            ((1, WIDTH), f32),
            ((1, WIDTH), f32),
        ],
        query_weight,
        pair_weight,
        norm_gain.reshape(1, WIDTH),
        norm_bias.reshape(1, WIDTH),
        scratch=[pltpu.SemaphoreType.DMA((4,))],
    )
    parts, weights = lax.optimization_barrier((parts, weights))
    (stats,) = call(stats_kernel, [VMEM] * 4, [((8, LANES), f32)], *parts)
    all_stats = [stats] + [shift(stats, "y", k) for k in (1, 2, 3)]
    (piece,) = call(piece_kernel, [VMEM] * 5, [table], stats, *parts)
    pieces = [piece, shift(piece, "y", 1), shift(piece, "y", 3)]
    late = after(piece, *all_stats)
    pieces.append(shift(late, "y", 2))
    *queries, fresh = call(
        project_kernel,
        [SMEM] + [VMEM] * 9,
        [((ANSWER_ROWS + SET_ROWS, LANES), bf16)] * 4 + [((ROWS, 2 * WIDTH), bf16)],
        place,
        tokens,
        *all_stats,
        *weights,
        scratch=[
            pltpu.VMEM((4, SET_ROWS, LANES), bf16),
            pltpu.VMEM((2, CELLS, LANES), bf16),
        ],
    )
    asked = {0: queries[0]}
    for k in (2, 1, 3):
        asked[k] = shift(after(queries[k], pieces[1]) if k == 3 else queries[k], "x", k)
    pieces += [shift(block, "core", 1) for block in [late] + pieces[1:]]
    results = [None] * 4
    for sources in ((1, 3, 2), (0,)):
        answers = call(
            functools.partial(attend_kernel, sources),
            [SMEM] + [VMEM] * (len(sources) + 8),
            [answer] * len(sources),
            place,
            *[asked[k] for k in sources],
            *pieces,
            scratch=[pltpu.VMEM(*table)] * len(sources),
            limit=40,
        )
        for k, block in zip(sources, answers):
            results[k] = shift(block, "x", -k) if k else block
    (attended,) = call(
        assemble_kernel,
        [SMEM] + [VMEM] * 4,
        [((CELLS, WIDTH), bf16)],
        place,
        *results,
        scratch=[pltpu.VMEM((4, ANSWER_ROWS, LANES), bf16)],
    )
    return (attended[None], fresh[None])


def solution(mesh):
    return jax.shard_map(
        per_device,
        mesh=mesh,
        in_specs=(P("cfg", "patch", None), P("cfg", "patch", None), P(), P(), P(), P()),
        out_specs=(P("cfg", "patch", None), P("cfg", "patch", None)),
        check_vma=False,
    )
```

```python
import functools

import jax
import jax.numpy as jnp
from jax import lax
from jax.experimental import pallas as pl
from jax.experimental.pallas import tpu as pltpu
from jax.sharding import PartitionSpec as P

HEADS = 20
HEAD_DIM = 64
GROUPS = 32
POOL = 4
WIDTH = 1280
CELLS = 256
ROWS = 16
GROUP_WIDTH = WIDTH // GROUPS
LANES = 128
SET_HEADS = 5
SET_ROWS = SET_HEADS * ROWS
ANSWER_ROWS = SET_HEADS * CELLS // 2
epsilon = 1e-05

f32 = jnp.float32
bf16 = jnp.bfloat16
HIGHEST = lax.Precision.HIGHEST
VMEM = pl.BlockSpec(memory_space=pltpu.VMEM)
SMEM = pl.BlockSpec(memory_space=pltpu.SMEM)
HBM = pl.BlockSpec(memory_space=pltpu.HBM)


def iota(shape, axis):
    return lax.broadcasted_iota(jnp.int32, shape, axis)


def group_of_channel():
    low = iota((WIDTH, LANES), 1) * GROUP_WIDTH
    channel = iota((WIDTH, LANES), 0)
    return ((channel >= low) & (channel < low + GROUP_WIDTH)).astype(f32)


def channel_of_group():
    low = iota((LANES, WIDTH), 0) * GROUP_WIDTH
    channel = iota((LANES, WIDTH), 1)
    return ((channel >= low) & (channel < low + GROUP_WIDTH)).astype(f32)


def exact_dot(left, right):
    return jnp.dot(left, right, precision=HIGHEST, preferred_element_type=f32)


def combine(parts, entries):
    mean = sum(part[0:1] for part in parts) / len(parts)
    squares = sum(part[1:2] for part in parts)
    apart = sum((part[0:1] - mean) * (part[0:1] - mean) for part in parts)
    return mean, squares + entries * apart


def stack_stats(mean, squares):
    row = iota((8, LANES), 0)
    return jnp.where(row == 0, mean, jnp.where(row == 1, squares, 0.0))


def encode(mean, squares):
    row = iota((ROWS, LANES), 0)
    coded = jnp.zeros((ROWS, LANES), f32)
    for i, rest in enumerate((mean, squares)):
        for part in range(3):
            rounded = rest.astype(bf16).astype(f32)
            coded = jnp.where(row == 3 * i + part, rounded, coded)
            rest = rest - rounded
    return coded.astype(bf16)


def decode(rows):
    parts = rows.astype(f32)
    return jnp.concatenate(
        [parts[0:1] + parts[1:2] + parts[2:3], parts[3:4] + parts[4:5] + parts[5:6]], axis=0
    )


def head_tiles(pairs):
    lane = iota((ROWS, LANES), 1)
    even, odd = [], []
    for t in range(WIDTH // LANES):
        keys = pairs[:, t * LANES : (t + 1) * LANES].astype(f32)
        values = pairs[:, WIDTH + t * LANES : WIDTH + (t + 1) * LANES].astype(f32)
        turned = pltpu.roll(values, HEAD_DIM, 1)
        even.append(jnp.where(lane < HEAD_DIM, keys, turned).astype(bf16))
        odd.append(jnp.where(lane < HEAD_DIM, turned, keys).astype(bf16))
    sets = []
    for j in range(4):
        last = (even if j % 2 == 0 else odd)[8 + j // 2]
        sets.append(
            jnp.concatenate(
                [even[2 * j], odd[2 * j], even[2 * j + 1], odd[2 * j + 1], last], axis=0
            )
        )
    return sets


def turn(block):
    return pltpu.roll(block.astype(f32), HEAD_DIM, 1)


def fold(block, mask):
    half = CELLS // 2
    return jnp.where(mask, block[0:half].astype(f32), turn(block[half:])).astype(bf16)


def unfold(block):
    return jnp.concatenate([block.astype(f32), turn(block)], axis=0)


def local_kernel(tokens_ref, stats_ref, kept_ref):
    tokens = tokens_ref[...]
    kept_ref[...] = tokens
    values = tokens.astype(f32)
    sums = jnp.broadcast_to(jnp.sum(values, axis=0, keepdims=True), (8, WIDTH))
    mean = exact_dot(sums, group_of_channel()) / (CELLS * GROUP_WIDTH)
    center = exact_dot(mean, channel_of_group())
    shifted = values - center[0:1]
    squares = jnp.broadcast_to(jnp.sum(shifted * shifted, axis=0, keepdims=True), (8, WIDTH))
    squares = exact_dot(squares, group_of_channel())
    stats_ref[...] = stack_stats(mean, squares)


def sets_kernel(stats_ref, stale_ref, sets_ref):
    for j, block in enumerate(head_tiles(stale_ref[...])):
        sets_ref[j] = block


def x_kernel(place_ref, own_ref, other_ref, sets_ref, *out_refs):
    mean, squares = combine([own_ref[...], other_ref[...]], CELLS * GROUP_WIDTH)
    coded = encode(mean, squares)
    place = place_ref[0]
    for k, out_ref in enumerate(out_refs):
        out_ref[0:SET_ROWS, :] = sets_ref[lax.rem(place + k, 4)]
        out_ref[SET_ROWS:, :] = coded


def z_kernel(*refs):
    *in_refs, out_ref = refs
    stats = [decode(ref[SET_ROWS:, :]) for ref in in_refs]
    mean, squares = combine(stats, 2 * CELLS * GROUP_WIDTH)
    for k, ref in enumerate(in_refs):
        for h in range(SET_HEADS):
            low = h * 4 * ROWS + k * ROWS
            out_ref[low : low + ROWS, :] = ref[h * ROWS : (h + 1) * ROWS, :]
    out_ref[4 * SET_ROWS :, :] = encode(mean, squares)


def stats_kernel(*refs):
    *in_refs, stats_ref = refs
    stats = [decode(ref[4 * SET_ROWS :, :]) for ref in in_refs]
    mean, squares = combine(stats, 8 * CELLS * GROUP_WIDTH)
    stats_ref[...] = stack_stats(mean, squares)


def piece_kernel(stats_ref, *refs):
    *in_refs, out_ref = refs
    for k, ref in enumerate(in_refs):
        for h in range(SET_HEADS):
            low = h * CELLS + k * 4 * ROWS
            out_ref[low : low + 4 * ROWS, :] = ref[h * 4 * ROWS : (h + 1) * 4 * ROWS, :]


def weights_kernel(query_hbm, pair_hbm, gain_hbm, bias_hbm, *refs):
    *out_refs, arrived = refs
    copies = [
        pltpu.make_async_copy(source, target, arrived.at[i])
        for i, (source, target) in enumerate(
            zip((query_hbm, pair_hbm, gain_hbm, bias_hbm), out_refs)
        )
    ]
    for copy in copies:
        copy.start()
    for copy in copies:
        copy.wait()


def project_kernel(
    place_ref, tokens_ref, s0, s1, s2, s3, query_ref, pair_ref, gain_ref, bias_ref, *refs
):
    *message_refs, fresh_ref, sets_ref, last_ref = refs
    mean, squares = combine([s0[...], s1[...], s2[...], s3[...]], 32 * CELLS * GROUP_WIDTH)
    spread = squares / (128 * CELLS * GROUP_WIDTH)
    row = iota((8, LANES), 0)
    both = jnp.where(row == 0, mean, lax.rsqrt(spread + epsilon))
    channels = exact_dot(both, channel_of_group())
    scaled = (tokens_ref[...].astype(f32) - channels[0:1]) * channels[1:2]
    gain = gain_ref[...].reshape(1, WIDTH)
    bias = bias_ref[...].reshape(1, WIDTH)
    normed = (scaled * gain + bias).astype(bf16)

    square = iota((ROWS, CELLS), 0)
    cell = iota((ROWS, CELLS), 1)
    cell_square = lax.shift_right_logical(lax.bitwise_and(cell, 63), 2)
    pool = jnp.where(cell_square == square, 1.0 / (POOL * POOL), 0.0).astype(bf16)
    pooled = jnp.dot(pool, normed, preferred_element_type=f32).astype(bf16)

    place = place_ref[0]
    last = jnp.dot(normed, query_ref[:, 1024:], preferred_element_type=f32).astype(bf16)
    last_ref[0] = last[:, 0:LANES]
    last_ref[1] = last[:, LANES:]
    lane_half = lax.shift_right_logical(iota((CELLS // 2, LANES), 1), 6)
    for k in (2, 1, 3, 0):
        j = lax.rem(place + k, 4)
        columns = pl.ds(pl.multiple_of(j * 256, 256), 256)
        block = jnp.dot(normed, query_ref[:, columns], preferred_element_type=f32).astype(bf16)
        message_refs[k][0:CELLS, :] = block[:, 0:LANES]
        message_refs[k][CELLS : 2 * CELLS, :] = block[:, LANES:]
        mask = lane_half == lax.bitwise_and(j, 1)
        message_refs[k][2 * CELLS : ANSWER_ROWS, :] = fold(
            last_ref[lax.shift_right_logical(j, 1)], mask
        )

    fresh = jnp.dot(pooled, pair_ref[...], preferred_element_type=f32).astype(bf16)
    fresh_ref[...] = fresh
    for j, block in enumerate(head_tiles(fresh)):
        sets_ref[j] = block
    for k in range(4):
        message_refs[k][ANSWER_ROWS:, :] = sets_ref[lax.rem(place + k, 4)]


def attend_kernel(sources, place_ref, *refs):
    count = len(sources)
    message_refs, table_refs = refs[:count], refs[count : count + 8]
    out_refs, first_refs = refs[count + 8 : 2 * count + 8], refs[2 * count + 8 :]
    for source, message_ref, first_ref in zip(sources, message_refs, first_refs):
        first_ref[...] = table_refs[0][...]
        for h in range(SET_HEADS):
            low = h * CELLS + source * ROWS
            fresh = message_ref[ANSWER_ROWS + h * ROWS : ANSWER_ROWS + (h + 1) * ROWS, :]
            first_ref[low : low + ROWS, :] = fresh
    lane = iota((CELLS, LANES), 1)
    low_half = lane < HEAD_DIM
    parity = lax.bitwise_and(place_ref[0], 1)
    factor = HEAD_DIM ** (-0.5) * 1.4426950408889634
    against = (((1,), (1,)), ((), ()))
    ones = jnp.ones((CELLS, LANES), bf16)

    def head_scores(h):
        if h < 4:
            mask = low_half if h % 2 == 0 else jnp.logical_not(low_half)
        else:
            mask = lax.shift_right_logical(lane, 6) == parity
        groups = []
        for message_ref in message_refs:
            if h < 4:
                queries = message_ref[(h // 2) * CELLS : (h // 2 + 1) * CELLS, :].astype(f32)
            else:
                queries = unfold(message_ref[2 * CELLS : ANSWER_ROWS, :])
            groups.append(jnp.where(mask, queries, 0.0).astype(bf16))
        queries = jnp.concatenate(groups, axis=0) if count > 1 else groups[0]
        head = slice(h * CELLS, (h + 1) * CELLS)
        firsts = [
            lax.dot_general(group, ref[head, :], against, preferred_element_type=f32)
            for group, ref in zip(groups, first_refs)
        ]
        scores = [jnp.concatenate(firsts, axis=0)]
        for ref in table_refs[1:]:
            keys = ref[head, :]
            scores.append(lax.dot_general(queries, keys, against, preferred_element_type=f32))
        return scores

    def head_result(h, scores):
        head = slice(h * CELLS, (h + 1) * CELLS)
        largest = scores[0]
        for part in scores[1:]:
            largest = jnp.maximum(largest, part)
        largest = jnp.max(largest, axis=1, keepdims=True)
        summed = None
        for index, part in enumerate(scores):
            weights = jnp.exp2((part - largest) * factor).astype(bf16)
            if index == 0:
                products = []
                for g, ref in enumerate(first_refs):
                    values = jnp.concatenate([ref[head, :], ones], axis=1)
                    rows = weights[g * CELLS : (g + 1) * CELLS]
                    products.append(jnp.dot(rows, values, preferred_element_type=f32))
                summed = jnp.concatenate(products, axis=0)
            else:
                values = jnp.concatenate([table_refs[index][head, :], ones], axis=1)
                summed = summed + jnp.dot(weights, values, preferred_element_type=f32)
        return summed[:, 0:LANES] / summed[:, LANES:]

    results = []
    scores = head_scores(0)
    for h in range(SET_HEADS):
        following = head_scores(h + 1) if h + 1 < SET_HEADS else None
        results.append(head_result(h, scores))
        scores = following
    for g, out_ref in enumerate(out_refs):
        rows = slice(g * CELLS, (g + 1) * CELLS)
        for t in range(2):
            both = jnp.where(low_half, results[2 * t + 1][rows], results[2 * t][rows])
            out_ref[t * CELLS : (t + 1) * CELLS, :] = turn(both).astype(bf16)
        half = lax.shift_right_logical(iota((CELLS // 2, LANES), 1), 6)
        out_ref[2 * CELLS :, :] = fold(turn(results[4][rows]), half == parity)


def assemble_kernel(place_ref, *refs):
    *in_refs, out_ref, sets_ref = refs
    place = place_ref[0]
    for k, ref in enumerate(in_refs):
        sets_ref[lax.rem(place + k, 4)] = ref[...]
    for j in range(4):
        for t in range(2):
            low = (2 * j + t) * LANES
            out_ref[:, low : low + LANES] = sets_ref[j, t * CELLS : (t + 1) * CELLS, :]
    low_half = iota((CELLS, LANES), 1) < HEAD_DIM
    for t in range(2):
        low = (8 + t) * LANES
        both = [unfold(sets_ref[2 * t + i, 2 * CELLS :, :]) for i in range(2)]
        out_ref[:, low : low + LANES] = jnp.where(low_half, *both).astype(bf16)


def call(kernel, ins, outs, *args, scratch=(), limit=24):
    return pl.pallas_call(
        kernel,
        in_specs=ins,
        out_specs=[VMEM] * len(outs),
        out_shape=[jax.ShapeDtypeStruct(shape, kind) for shape, kind in outs],
        scratch_shapes=list(scratch),
        compiler_params=pltpu.CompilerParams(vmem_limit_bytes=limit * 1024 * 1024),
        cost_estimate=pl.CostEstimate(flops=1, bytes_accessed=1, transcendentals=0),
    )(*args)


def permute(array, place):
    pairs = []
    for source in range(128):
        z, y, x, core = place(source // 32, source // 8 % 4, source // 2 % 4, source % 2)
        pairs.append((source, z % 4 * 32 + y % 4 * 8 + x % 4 * 2 + core % 2))
    return lax.ppermute(array, "patch", pairs)


def shift(array, axis, step):
    def place(*places):
        return [at + step * (name == axis) for at, name in zip(places, ("z", "y", "x", "core"))]

    return permute(array, place)


def after(array, *others):
    return lax.optimization_barrier((array, *others))[0]


def per_device(tokens, stale_keys, norm_gain, norm_bias, query_weight, pair_weight):
    place = (lax.axis_index("patch") // 2 % 4).astype(jnp.int32).reshape(1)
    table = ((SET_HEADS * CELLS, LANES), bf16)
    answer = ((ANSWER_ROWS, LANES), bf16)
    stats, tokens = call(
        local_kernel,
        [VMEM],
        [((8, LANES), f32), ((CELLS, WIDTH), bf16)],
        tokens[0],
    )
    (sets,) = call(
        sets_kernel, [VMEM, VMEM], [((4, SET_ROWS, LANES), bf16)], stats, stale_keys[0]
    )
    other = shift(stats, "core", 1)
    messages = call(
        x_kernel,
        [SMEM, VMEM, VMEM, VMEM],
        [((SET_ROWS + ROWS, LANES), bf16)] * 4,
        place,
        stats,
        other,
        sets,
    )
    received = [messages[0]] + [shift(messages[k], "x", k) for k in (1, 2, 3)]
    (part,) = call(z_kernel, [VMEM] * 4, [((4 * SET_ROWS + ROWS, LANES), bf16)], *received)
    parts = [part] + [shift(part, "z", k) for k in (1, 2, 3)]
    query_weight, pair_weight, norm_gain, norm_bias, _ = lax.optimization_barrier(
        (query_weight, pair_weight, norm_gain, norm_bias, part)
    )
    weights = call(
        weights_kernel,
        [HBM] * 4,
        [
            ((WIDTH, WIDTH), bf16),
            ((WIDTH, 2 * WIDTH), bf16),
            ((WIDTH,), f32),
            ((WIDTH,), f32),
        ],
        query_weight,
        pair_weight,
        norm_gain,
        norm_bias,
        scratch=[pltpu.SemaphoreType.DMA((4,))],
    )
    parts, weights = lax.optimization_barrier((parts, weights))
    (stats,) = call(stats_kernel, [VMEM] * 4, [((8, LANES), f32)], *parts)
    all_stats = [stats] + [shift(stats, "y", k) for k in (1, 2, 3)]
    (piece,) = call(piece_kernel, [VMEM] * 5, [table], stats, *parts)
    pieces = [piece, shift(piece, "y", 1), shift(piece, "y", 3)]
    pieces.append(shift(after(piece, *all_stats), "y", 2))
    *queries, fresh = call(
        project_kernel,
        [SMEM] + [VMEM] * 9,
        [((ANSWER_ROWS + SET_ROWS, LANES), bf16)] * 4 + [((ROWS, 2 * WIDTH), bf16)],
        place,
        tokens,
        *all_stats,
        *weights,
        scratch=[
            pltpu.VMEM((4, SET_ROWS, LANES), bf16),
            pltpu.VMEM((2, CELLS, LANES), bf16),
        ],
    )
    asked = {0: queries[0]}
    for k in (2, 1, 3):
        asked[k] = shift(after(queries[k], pieces[1]) if k == 3 else queries[k], "x", k)
    tables = pieces + [shift(after(block, asked[2]), "core", 1) for block in pieces]
    results = [None] * 4
    for sources in ((2, 1), (3,), (0,)):
        answers = call(
            functools.partial(attend_kernel, sources),
            [SMEM] + [VMEM] * (len(sources) + 8),
            [answer] * len(sources),
            place,
            *[asked[k] for k in sources],
            *tables,
            scratch=[pltpu.VMEM(*table)] * len(sources),
            limit=40,
        )
        for k, block in zip(sources, answers):
            results[k] = shift(block, "x", -k) if k else block
    (attended,) = call(
        assemble_kernel,
        [SMEM] + [VMEM] * 4,
        [((CELLS, WIDTH), bf16)],
        place,
        *results,
        scratch=[pltpu.VMEM((4, ANSWER_ROWS, LANES), bf16)],
    )
    return (attended[None], fresh[None])


def solution(mesh):
    return jax.shard_map(
        per_device,
        mesh=mesh,
        in_specs=(P("cfg", "patch", None), P("cfg", "patch", None), P(), P(), P(), P()),
        out_specs=(P("cfg", "patch", None), P("cfg", "patch", None)),
        check_vma=False,
    )
```

```python
import functools

import jax
import jax.numpy as jnp
from jax import lax
from jax.experimental import pallas as pl
from jax.experimental.pallas import tpu as pltpu
from jax.sharding import PartitionSpec as P

HEADS = 20
HEAD_DIM = 64
GROUPS = 32
POOL = 4
WIDTH = 1280
CELLS = 256
ROWS = 16
GROUP_WIDTH = WIDTH // GROUPS
LANES = 128
SET_HEADS = 5
SET_ROWS = SET_HEADS * ROWS
ANSWER_ROWS = SET_HEADS * CELLS // 2
epsilon = 1e-05

f32 = jnp.float32
bf16 = jnp.bfloat16
HIGHEST = lax.Precision.HIGHEST
VMEM = pl.BlockSpec(memory_space=pltpu.VMEM)
SMEM = pl.BlockSpec(memory_space=pltpu.SMEM)
HBM = pl.BlockSpec(memory_space=pltpu.HBM)


def iota(shape, axis):
    return lax.broadcasted_iota(jnp.int32, shape, axis)


def group_of_channel():
    low = iota((WIDTH, LANES), 1) * GROUP_WIDTH
    channel = iota((WIDTH, LANES), 0)
    return ((channel >= low) & (channel < low + GROUP_WIDTH)).astype(f32)


def channel_of_group():
    low = iota((LANES, WIDTH), 0) * GROUP_WIDTH
    channel = iota((LANES, WIDTH), 1)
    return ((channel >= low) & (channel < low + GROUP_WIDTH)).astype(f32)


def exact_dot(left, right):
    return jnp.dot(left, right, precision=HIGHEST, preferred_element_type=f32)


def combine(parts, entries):
    mean = sum(part[0:1] for part in parts) / len(parts)
    squares = sum(part[1:2] for part in parts)
    apart = sum((part[0:1] - mean) * (part[0:1] - mean) for part in parts)
    return mean, squares + entries * apart


def stack_stats(mean, squares):
    row = iota((8, LANES), 0)
    return jnp.where(row == 0, mean, jnp.where(row == 1, squares, 0.0))


def encode(mean, squares):
    row = iota((ROWS, LANES), 0)
    coded = jnp.zeros((ROWS, LANES), f32)
    for i, rest in enumerate((mean, squares)):
        for part in range(3):
            rounded = rest.astype(bf16).astype(f32)
            coded = jnp.where(row == 3 * i + part, rounded, coded)
            rest = rest - rounded
    return coded.astype(bf16)


def decode(rows):
    parts = rows.astype(f32)
    return jnp.concatenate(
        [parts[0:1] + parts[1:2] + parts[2:3], parts[3:4] + parts[4:5] + parts[5:6]], axis=0
    )


def head_tiles(pairs):
    lane = iota((ROWS, LANES), 1)
    even, odd = [], []
    for t in range(WIDTH // LANES):
        keys = pairs[:, t * LANES : (t + 1) * LANES].astype(f32)
        values = pairs[:, WIDTH + t * LANES : WIDTH + (t + 1) * LANES].astype(f32)
        turned = pltpu.roll(values, HEAD_DIM, 1)
        even.append(jnp.where(lane < HEAD_DIM, keys, turned).astype(bf16))
        odd.append(jnp.where(lane < HEAD_DIM, turned, keys).astype(bf16))
    sets = []
    for j in range(4):
        last = (even if j % 2 == 0 else odd)[8 + j // 2]
        sets.append(
            jnp.concatenate(
                [even[2 * j], odd[2 * j], even[2 * j + 1], odd[2 * j + 1], last], axis=0
            )
        )
    return sets


def turn(block):
    return pltpu.roll(block.astype(f32), HEAD_DIM, 1)


def fold(block, mask):
    half = CELLS // 2
    return jnp.where(mask, block[0:half].astype(f32), turn(block[half:])).astype(bf16)


def unfold(block):
    return jnp.concatenate([block.astype(f32), turn(block)], axis=0)


def local_kernel(tokens_ref, stats_ref, kept_ref):
    tokens = tokens_ref[...]
    kept_ref[...] = tokens
    values = tokens.astype(f32)
    sums = jnp.broadcast_to(jnp.sum(values, axis=0, keepdims=True), (8, WIDTH))
    mean = exact_dot(sums, group_of_channel()) / (CELLS * GROUP_WIDTH)
    center = exact_dot(mean, channel_of_group())
    shifted = values - center[0:1]
    squares = jnp.broadcast_to(jnp.sum(shifted * shifted, axis=0, keepdims=True), (8, WIDTH))
    squares = exact_dot(squares, group_of_channel())
    stats_ref[...] = stack_stats(mean, squares)


def sets_kernel(stats_ref, stale_ref, sets_ref):
    for j, block in enumerate(head_tiles(stale_ref[...])):
        sets_ref[j] = block


def x_kernel(place_ref, own_ref, other_ref, sets_ref, *out_refs):
    mean, squares = combine([own_ref[...], other_ref[...]], CELLS * GROUP_WIDTH)
    coded = encode(mean, squares)
    place = place_ref[0]
    for k, out_ref in enumerate(out_refs):
        out_ref[0:SET_ROWS, :] = sets_ref[lax.rem(place + k, 4)]
        out_ref[SET_ROWS:, :] = coded


def affine_kernel(gain_ref, bias_ref, out_ref):
    out_ref[0:1, :] = gain_ref[...].reshape(1, WIDTH)
    out_ref[1:2, :] = bias_ref[...].reshape(1, WIDTH)


def z_kernel(*refs):
    *in_refs, out_ref = refs
    stats = [decode(ref[SET_ROWS:, :]) for ref in in_refs]
    mean, squares = combine(stats, 2 * CELLS * GROUP_WIDTH)
    for k, ref in enumerate(in_refs):
        for h in range(SET_HEADS):
            low = h * 4 * ROWS + k * ROWS
            out_ref[low : low + ROWS, :] = ref[h * ROWS : (h + 1) * ROWS, :]
    out_ref[4 * SET_ROWS :, :] = encode(mean, squares)


def stats_kernel(*refs):
    *in_refs, stats_ref = refs
    stats = [decode(ref[4 * SET_ROWS :, :]) for ref in in_refs]
    mean, squares = combine(stats, 8 * CELLS * GROUP_WIDTH)
    stats_ref[...] = stack_stats(mean, squares)


def piece_kernel(stats_ref, *refs):
    *in_refs, out_ref = refs
    for k, ref in enumerate(in_refs):
        for h in range(SET_HEADS):
            low = h * CELLS + k * 4 * ROWS
            out_ref[low : low + 4 * ROWS, :] = ref[h * 4 * ROWS : (h + 1) * 4 * ROWS, :]


def load_kernel(source_hbm, target_ref, arrived):
    copy = pltpu.make_async_copy(source_hbm, target_ref, arrived)
    copy.start()
    copy.wait()


def project_kernel(
    place_ref, tokens_ref, s0, s1, s2, s3, affine_ref, query_ref, pair_ref, *refs
):
    *message_refs, fresh_ref, sets_ref, last_ref = refs
    mean, squares = combine([s0[...], s1[...], s2[...], s3[...]], 32 * CELLS * GROUP_WIDTH)
    spread = squares / (128 * CELLS * GROUP_WIDTH)
    row = iota((8, LANES), 0)
    both = jnp.where(row == 0, mean, lax.rsqrt(spread + epsilon))
    channels = exact_dot(both, channel_of_group())
    scaled = (tokens_ref[...].astype(f32) - channels[0:1]) * channels[1:2]
    normed = (scaled * affine_ref[0:1] + affine_ref[1:2]).astype(bf16)

    square = iota((ROWS, CELLS), 0)
    cell = iota((ROWS, CELLS), 1)
    cell_square = lax.shift_right_logical(lax.bitwise_and(cell, 63), 2)
    pool = jnp.where(cell_square == square, 1.0 / (POOL * POOL), 0.0).astype(bf16)
    pooled = jnp.dot(pool, normed, preferred_element_type=f32).astype(bf16)

    place = place_ref[0]
    last = jnp.dot(normed, query_ref[:, 1024:], preferred_element_type=f32).astype(bf16)
    last_ref[0] = last[:, 0:LANES]
    last_ref[1] = last[:, LANES:]
    lane_half = lax.shift_right_logical(iota((CELLS // 2, LANES), 1), 6)
    for k in (2, 1, 3, 0):
        j = lax.rem(place + k, 4)
        columns = pl.ds(pl.multiple_of(j * 256, 256), 256)
        block = jnp.dot(normed, query_ref[:, columns], preferred_element_type=f32).astype(bf16)
        message_refs[k][0:CELLS, :] = block[:, 0:LANES]
        message_refs[k][CELLS : 2 * CELLS, :] = block[:, LANES:]
        mask = lane_half == lax.bitwise_and(j, 1)
        message_refs[k][2 * CELLS : ANSWER_ROWS, :] = fold(
            last_ref[lax.shift_right_logical(j, 1)], mask
        )

    fresh = jnp.dot(pooled, pair_ref[...], preferred_element_type=f32).astype(bf16)
    fresh_ref[...] = fresh
    for j, block in enumerate(head_tiles(fresh)):
        sets_ref[j] = block
    for k in range(4):
        message_refs[k][ANSWER_ROWS:, :] = sets_ref[lax.rem(place + k, 4)]


def attend_kernel(sources, place_ref, *refs):
    count = len(sources)
    message_refs, table_refs = refs[:count], refs[count : count + 8]
    out_refs, first_refs = refs[count + 8 : 2 * count + 8], refs[2 * count + 8 :]
    for source, message_ref, first_ref in zip(sources, message_refs, first_refs):
        first_ref[...] = table_refs[0][...]
        for h in range(SET_HEADS):
            low = h * CELLS + source * ROWS
            fresh = message_ref[ANSWER_ROWS + h * ROWS : ANSWER_ROWS + (h + 1) * ROWS, :]
            first_ref[low : low + ROWS, :] = fresh
    lane = iota((CELLS, LANES), 1)
    low_half = lane < HEAD_DIM
    parity = lax.bitwise_and(place_ref[0], 1)
    factor = HEAD_DIM ** (-0.5) * 1.4426950408889634
    against = (((1,), (1,)), ((), ()))
    ones = jnp.ones((CELLS, LANES), bf16)

    def head_scores(h):
        if h < 4:
            mask = low_half if h % 2 == 0 else jnp.logical_not(low_half)
        else:
            mask = lax.shift_right_logical(lane, 6) == parity
        groups = []
        for message_ref in message_refs:
            if h < 4:
                queries = message_ref[(h // 2) * CELLS : (h // 2 + 1) * CELLS, :].astype(f32)
            else:
                queries = unfold(message_ref[2 * CELLS : ANSWER_ROWS, :])
            groups.append(jnp.where(mask, queries, 0.0).astype(bf16))
        queries = jnp.concatenate(groups, axis=0) if count > 1 else groups[0]
        head = slice(h * CELLS, (h + 1) * CELLS)
        firsts = [
            lax.dot_general(group, ref[head, :], against, preferred_element_type=f32)
            for group, ref in zip(groups, first_refs)
        ]
        scores = [jnp.concatenate(firsts, axis=0)]
        for ref in table_refs[1:]:
            keys = ref[head, :]
            scores.append(lax.dot_general(queries, keys, against, preferred_element_type=f32))
        return scores

    def head_result(h, scores):
        head = slice(h * CELLS, (h + 1) * CELLS)
        largest = scores[0]
        for part in scores[1:]:
            largest = jnp.maximum(largest, part)
        largest = jnp.max(largest, axis=1, keepdims=True)
        summed = None
        for index, part in enumerate(scores):
            weights = jnp.exp2((part - largest) * factor).astype(bf16)
            if index == 0:
                products = []
                for g, ref in enumerate(first_refs):
                    values = jnp.concatenate([ref[head, :], ones], axis=1)
                    rows = weights[g * CELLS : (g + 1) * CELLS]
                    products.append(jnp.dot(rows, values, preferred_element_type=f32))
                summed = jnp.concatenate(products, axis=0)
            else:
                values = jnp.concatenate([table_refs[index][head, :], ones], axis=1)
                summed = summed + jnp.dot(weights, values, preferred_element_type=f32)
        return summed[:, 0:LANES] / summed[:, LANES:]

    results = []
    scores = head_scores(0)
    for h in range(SET_HEADS):
        following = head_scores(h + 1) if h + 1 < SET_HEADS else None
        results.append(head_result(h, scores))
        scores = following
    for g, out_ref in enumerate(out_refs):
        rows = slice(g * CELLS, (g + 1) * CELLS)
        for t in range(2):
            both = jnp.where(low_half, results[2 * t + 1][rows], results[2 * t][rows])
            out_ref[t * CELLS : (t + 1) * CELLS, :] = turn(both).astype(bf16)
        half = lax.shift_right_logical(iota((CELLS // 2, LANES), 1), 6)
        out_ref[2 * CELLS :, :] = fold(turn(results[4][rows]), half == parity)


def assemble_kernel(place_ref, *refs):
    *in_refs, out_ref, sets_ref = refs
    place = place_ref[0]
    for k, ref in enumerate(in_refs):
        sets_ref[lax.rem(place + k, 4)] = ref[...]
    for j in range(4):
        for t in range(2):
            low = (2 * j + t) * LANES
            out_ref[:, low : low + LANES] = sets_ref[j, t * CELLS : (t + 1) * CELLS, :]
    low_half = iota((CELLS, LANES), 1) < HEAD_DIM
    for t in range(2):
        low = (8 + t) * LANES
        both = [unfold(sets_ref[2 * t + i, 2 * CELLS :, :]) for i in range(2)]
        out_ref[:, low : low + LANES] = jnp.where(low_half, *both).astype(bf16)


def call(kernel, ins, outs, *args, scratch=(), limit=24):
    return pl.pallas_call(
        kernel,
        in_specs=ins,
        out_specs=[VMEM] * len(outs),
        out_shape=[jax.ShapeDtypeStruct(shape, kind) for shape, kind in outs],
        scratch_shapes=list(scratch),
        compiler_params=pltpu.CompilerParams(vmem_limit_bytes=limit * 1024 * 1024),
        cost_estimate=pl.CostEstimate(flops=1, bytes_accessed=1, transcendentals=0),
    )(*args)


def permute(array, place):
    pairs = []
    for source in range(128):
        z, y, x, core = place(source // 32, source // 8 % 4, source // 2 % 4, source % 2)
        pairs.append((source, z % 4 * 32 + y % 4 * 8 + x % 4 * 2 + core % 2))
    return lax.ppermute(array, "patch", pairs)


def shift(array, axis, step):
    def place(*places):
        return [at + step * (name == axis) for at, name in zip(places, ("z", "y", "x", "core"))]

    return permute(array, place)


def after(array, *others):
    return lax.optimization_barrier((array, *others))[0]


def per_device(tokens, stale_keys, norm_gain, norm_bias, query_weight, pair_weight):
    place = (lax.axis_index("patch") // 2 % 4).astype(jnp.int32).reshape(1)
    table = ((SET_HEADS * CELLS, LANES), bf16)
    answer = ((ANSWER_ROWS, LANES), bf16)
    stats, tokens = call(
        local_kernel,
        [VMEM],
        [((8, LANES), f32), ((CELLS, WIDTH), bf16)],
        tokens[0],
    )
    (sets,) = call(
        sets_kernel, [VMEM, VMEM], [((4, SET_ROWS, LANES), bf16)], stats, stale_keys[0]
    )
    other = shift(stats, "core", 1)
    messages = call(
        x_kernel,
        [SMEM, VMEM, VMEM, VMEM],
        [((SET_ROWS + ROWS, LANES), bf16)] * 4,
        place,
        stats,
        other,
        sets,
    )
    received = [messages[0]] + [shift(messages[k], "x", k) for k in (1, 2, 3)]
    norm_gain, norm_bias, _ = lax.optimization_barrier((norm_gain, norm_bias, messages[0]))
    (affine,) = call(affine_kernel, [VMEM] * 2, [((2, WIDTH), f32)], norm_gain, norm_bias)
    received, affine = lax.optimization_barrier((received, affine))
    (part,) = call(z_kernel, [VMEM] * 4, [((4 * SET_ROWS + ROWS, LANES), bf16)], *received)
    parts = [part] + [shift(part, "z", k) for k in (1, 2, 3)]
    weights = [part]
    for weight, limit in ((query_weight, 49), (pair_weight, 43)):
        weight = after(weight, weights[0])
        weights = list(call(
            load_kernel,
            [HBM],
            [(weight.shape, bf16)],
            weight,
            scratch=[pltpu.SemaphoreType.DMA],
            limit=limit,
        )) + weights
    weights = weights[1::-1]
    parts, weights = lax.optimization_barrier((parts, weights))
    (stats,) = call(stats_kernel, [VMEM] * 4, [((8, LANES), f32)], *parts)
    all_stats = [stats] + [shift(stats, "y", k) for k in (1, 2, 3)]
    (piece,) = call(piece_kernel, [VMEM] * 5, [table], stats, *parts)
    pieces = [piece, shift(piece, "y", 1), shift(piece, "y", 3)]
    pieces.append(shift(after(piece, *all_stats), "y", 2))
    *queries, fresh = call(
        project_kernel,
        [SMEM] + [VMEM] * 8,
        [((ANSWER_ROWS + SET_ROWS, LANES), bf16)] * 4 + [((ROWS, 2 * WIDTH), bf16)],
        place,
        tokens,
        *all_stats,
        affine,
        *weights,
        scratch=[
            pltpu.VMEM((4, SET_ROWS, LANES), bf16),
            pltpu.VMEM((2, CELLS, LANES), bf16),
        ],
    )
    asked = {0: queries[0]}
    for k in (2, 1, 3):
        asked[k] = shift(after(queries[k], pieces[1]) if k == 3 else queries[k], "x", k)
    tables = pieces + [shift(after(block, asked[2]), "core", 1) for block in pieces]
    results = [None] * 4
    for sources in ((2, 1), (3,), (0,)):
        answers = call(
            functools.partial(attend_kernel, sources),
            [SMEM] + [VMEM] * (len(sources) + 8),
            [answer] * len(sources),
            place,
            *[asked[k] for k in sources],
            *tables,
            scratch=[pltpu.VMEM(*table)] * len(sources),
            limit=40,
        )
        for k, block in zip(sources, answers):
            results[k] = shift(block, "x", -k) if k else block
    (attended,) = call(
        assemble_kernel,
        [SMEM] + [VMEM] * 4,
        [((CELLS, WIDTH), bf16)],
        place,
        *results,
        scratch=[pltpu.VMEM((4, ANSWER_ROWS, LANES), bf16)],
    )
    return (attended[None], fresh[None])


def solution(mesh):
    return jax.shard_map(
        per_device,
        mesh=mesh,
        in_specs=(P("cfg", "patch", None), P("cfg", "patch", None), P(), P(), P(), P()),
        out_specs=(P("cfg", "patch", None), P("cfg", "patch", None)),
        check_vma=False,
    )
```

```python
import functools

import jax
import jax.numpy as jnp
from jax import lax
from jax.experimental import pallas as pl
from jax.experimental.pallas import tpu as pltpu
from jax.sharding import PartitionSpec as P

HEADS = 20
HEAD_DIM = 64
GROUPS = 32
POOL = 4
WIDTH = 1280
CELLS = 256
ROWS = 16
GROUP_WIDTH = WIDTH // GROUPS
LANES = 128
SET_HEADS = 5
SET_ROWS = SET_HEADS * ROWS
ANSWER_ROWS = SET_HEADS * CELLS // 2
epsilon = 1e-05

f32 = jnp.float32
bf16 = jnp.bfloat16
VMEM = pl.BlockSpec(memory_space=pltpu.VMEM)
SMEM = pl.BlockSpec(memory_space=pltpu.SMEM)
HBM = pl.BlockSpec(memory_space=pltpu.HBM)


def iota(shape, axis):
    return lax.broadcasted_iota(jnp.int32, shape, axis)


def group_of_channel():
    low = iota((WIDTH, LANES), 1) * GROUP_WIDTH
    channel = iota((WIDTH, LANES), 0)
    return ((channel >= low) & (channel < low + GROUP_WIDTH)).astype(f32).astype(bf16)


def channel_of_group():
    low = iota((LANES, WIDTH), 0) * GROUP_WIDTH
    channel = iota((LANES, WIDTH), 1)
    return ((channel >= low) & (channel < low + GROUP_WIDTH)).astype(f32).astype(bf16)


def split_rows(*rows):
    width = rows[0].shape[1]
    row = iota((ROWS, width), 0)
    split = jnp.zeros((ROWS, width), f32)
    for i, rest in enumerate(rows):
        for part in range(3):
            rounded = rest.astype(bf16).astype(f32)
            split = jnp.where(row == 3 * i + part, rounded, split)
            rest = rest - rounded
    return split.astype(bf16)


def join_rows(split, i):
    parts = split[3 * i : 3 * i + 3].astype(f32)
    return parts[0:1] + parts[1:2] + parts[2:3]


def select_dot(matrix, *rows):
    products = jnp.dot(split_rows(*rows), matrix, preferred_element_type=f32)
    return [join_rows(products, i) for i in range(len(rows))]


def combine(parts, entries):
    mean = sum(part[0:1] for part in parts) / len(parts)
    squares = sum(part[1:2] for part in parts)
    apart = sum((part[0:1] - mean) * (part[0:1] - mean) for part in parts)
    return mean, squares + entries * apart


def stack_stats(mean, squares):
    row = iota((8, LANES), 0)
    return jnp.where(row == 0, mean, jnp.where(row == 1, squares, 0.0))


def decode(rows):
    split = rows.astype(f32)
    return jnp.concatenate([join_rows(split, 0), join_rows(split, 1)], axis=0)


def head_tiles(pairs):
    lane = iota((ROWS, LANES), 1)
    even, odd = [], []
    for t in range(WIDTH // LANES):
        keys = pairs[:, t * LANES : (t + 1) * LANES].astype(f32)
        values = pairs[:, WIDTH + t * LANES : WIDTH + (t + 1) * LANES].astype(f32)
        turned = pltpu.roll(values, HEAD_DIM, 1)
        even.append(jnp.where(lane < HEAD_DIM, keys, turned).astype(bf16))
        odd.append(jnp.where(lane < HEAD_DIM, turned, keys).astype(bf16))
    sets = []
    for j in range(4):
        last = (even if j % 2 == 0 else odd)[8 + j // 2]
        sets.append(
            jnp.concatenate(
                [even[2 * j], odd[2 * j], even[2 * j + 1], odd[2 * j + 1], last], axis=0
            )
        )
    return sets


def turn(block):
    return pltpu.roll(block.astype(f32), HEAD_DIM, 1)


def fold(block, mask):
    half = CELLS // 2
    return jnp.where(mask, block[0:half].astype(f32), turn(block[half:])).astype(bf16)


def unfold(block):
    return jnp.concatenate([block.astype(f32), turn(block)], axis=0)


def local_kernel(tokens_ref, stats_ref, kept_ref):
    tokens = tokens_ref[...]
    kept_ref[...] = tokens
    values = tokens.astype(f32)
    (mean,) = select_dot(group_of_channel(), jnp.sum(values, axis=0, keepdims=True))
    mean = mean / (CELLS * GROUP_WIDTH)
    (center,) = select_dot(channel_of_group(), mean)
    shifted = values - center
    (squares,) = select_dot(
        group_of_channel(), jnp.sum(shifted * shifted, axis=0, keepdims=True)
    )
    stats_ref[...] = stack_stats(mean, squares)


def sets_kernel(stats_ref, stale_ref, sets_ref):
    for j, block in enumerate(head_tiles(stale_ref[...])):
        sets_ref[j] = block


def x_kernel(place_ref, own_ref, other_ref, sets_ref, *out_refs):
    mean, squares = combine([own_ref[...], other_ref[...]], CELLS * GROUP_WIDTH)
    coded = split_rows(mean, squares)
    place = place_ref[0]
    for k, out_ref in enumerate(out_refs):
        out_ref[0:SET_ROWS, :] = sets_ref[lax.rem(place + k, 4)]
        out_ref[SET_ROWS:, :] = coded


def affine_kernel(gain_ref, bias_ref, out_ref):
    out_ref[0:1, :] = gain_ref[...].reshape(1, WIDTH)
    out_ref[1:2, :] = bias_ref[...].reshape(1, WIDTH)


def z_kernel(*refs):
    *in_refs, out_ref = refs
    stats = [decode(ref[SET_ROWS:, :]) for ref in in_refs]
    mean, squares = combine(stats, 2 * CELLS * GROUP_WIDTH)
    for k, ref in enumerate(in_refs):
        for h in range(SET_HEADS):
            low = h * 4 * ROWS + k * ROWS
            out_ref[low : low + ROWS, :] = ref[h * ROWS : (h + 1) * ROWS, :]
    out_ref[4 * SET_ROWS :, :] = split_rows(mean, squares)


def stats_kernel(*refs):
    *in_refs, stats_ref = refs
    stats = [decode(ref[4 * SET_ROWS :, :]) for ref in in_refs]
    mean, squares = combine(stats, 8 * CELLS * GROUP_WIDTH)
    stats_ref[...] = stack_stats(mean, squares)


def piece_kernel(stats_ref, *refs):
    *in_refs, out_ref = refs
    for k, ref in enumerate(in_refs):
        for h in range(SET_HEADS):
            low = h * CELLS + k * 4 * ROWS
            out_ref[low : low + 4 * ROWS, :] = ref[h * 4 * ROWS : (h + 1) * 4 * ROWS, :]


def load_kernel(source_hbm, target_ref, arrived):
    copy = pltpu.make_async_copy(source_hbm, target_ref, arrived)
    copy.start()
    copy.wait()


def project_kernel(
    place_ref, tokens_ref, s0, s1, s2, s3, affine_ref, query_ref, pair_ref, *refs
):
    *message_refs, fresh_ref, sets_ref, last_ref = refs
    mean, squares = combine([s0[...], s1[...], s2[...], s3[...]], 32 * CELLS * GROUP_WIDTH)
    spread = squares / (128 * CELLS * GROUP_WIDTH)
    center, inverse = select_dot(channel_of_group(), mean, lax.rsqrt(spread + epsilon))
    scaled = (tokens_ref[...].astype(f32) - center) * inverse
    normed = (scaled * affine_ref[0:1] + affine_ref[1:2]).astype(bf16)

    square = iota((ROWS, CELLS), 0)
    cell = iota((ROWS, CELLS), 1)
    cell_square = lax.shift_right_logical(lax.bitwise_and(cell, 63), 2)
    pool = jnp.where(cell_square == square, 1.0 / (POOL * POOL), 0.0).astype(bf16)
    pooled = jnp.dot(pool, normed, preferred_element_type=f32).astype(bf16)

    place = place_ref[0]
    last = jnp.dot(normed, query_ref[:, 1024:], preferred_element_type=f32).astype(bf16)
    last_ref[0] = last[:, 0:LANES]
    last_ref[1] = last[:, LANES:]
    lane_half = lax.shift_right_logical(iota((CELLS // 2, LANES), 1), 6)
    for k in (2, 1, 3, 0):
        j = lax.rem(place + k, 4)
        columns = pl.ds(pl.multiple_of(j * 256, 256), 256)
        block = jnp.dot(normed, query_ref[:, columns], preferred_element_type=f32).astype(bf16)
        message_refs[k][0:CELLS, :] = block[:, 0:LANES]
        message_refs[k][CELLS : 2 * CELLS, :] = block[:, LANES:]
        mask = lane_half == lax.bitwise_and(j, 1)
        message_refs[k][2 * CELLS : ANSWER_ROWS, :] = fold(
            last_ref[lax.shift_right_logical(j, 1)], mask
        )

    fresh = jnp.dot(pooled, pair_ref[...], preferred_element_type=f32).astype(bf16)
    fresh_ref[...] = fresh
    for j, block in enumerate(head_tiles(fresh)):
        sets_ref[j] = block
    for k in range(4):
        message_refs[k][ANSWER_ROWS:, :] = sets_ref[lax.rem(place + k, 4)]


def attend_kernel(sources, place_ref, *refs):
    count = len(sources)
    message_refs, table_refs = refs[:count], refs[count : count + 8]
    out_refs, first_refs = refs[count + 8 : 2 * count + 8], refs[2 * count + 8 :]
    for source, message_ref, first_ref in zip(sources, message_refs, first_refs):
        first_ref[...] = table_refs[0][...]
        for h in range(SET_HEADS):
            low = h * CELLS + source * ROWS
            fresh = message_ref[ANSWER_ROWS + h * ROWS : ANSWER_ROWS + (h + 1) * ROWS, :]
            first_ref[low : low + ROWS, :] = fresh
    lane = iota((CELLS, LANES), 1)
    low_half = lane < HEAD_DIM
    parity = lax.bitwise_and(place_ref[0], 1)
    factor = HEAD_DIM ** (-0.5) * 1.4426950408889634
    against = (((1,), (1,)), ((), ()))
    ones = jnp.ones((CELLS, LANES), bf16)

    def head_scores(h):
        if h < 4:
            mask = low_half if h % 2 == 0 else jnp.logical_not(low_half)
        else:
            mask = lax.shift_right_logical(lane, 6) == parity
        groups = []
        for message_ref in message_refs:
            if h < 4:
                queries = message_ref[(h // 2) * CELLS : (h // 2 + 1) * CELLS, :].astype(f32)
            else:
                queries = unfold(message_ref[2 * CELLS : ANSWER_ROWS, :])
            groups.append(jnp.where(mask, queries, 0.0).astype(bf16))
        queries = jnp.concatenate(groups, axis=0) if count > 1 else groups[0]
        head = slice(h * CELLS, (h + 1) * CELLS)
        firsts = [
            lax.dot_general(group, ref[head, :], against, preferred_element_type=f32)
            for group, ref in zip(groups, first_refs)
        ]
        scores = [jnp.concatenate(firsts, axis=0)]
        for ref in table_refs[1:]:
            keys = ref[head, :]
            scores.append(lax.dot_general(queries, keys, against, preferred_element_type=f32))
        return scores

    def head_result(h, scores):
        head = slice(h * CELLS, (h + 1) * CELLS)
        largest = scores[0]
        for part in scores[1:]:
            largest = jnp.maximum(largest, part)
        largest = jnp.max(largest, axis=1, keepdims=True)
        summed = None
        for index, part in enumerate(scores):
            weights = jnp.exp2((part - largest) * factor).astype(bf16)
            if index == 0:
                products = []
                for g, ref in enumerate(first_refs):
                    values = jnp.concatenate([ref[head, :], ones], axis=1)
                    rows = weights[g * CELLS : (g + 1) * CELLS]
                    products.append(jnp.dot(rows, values, preferred_element_type=f32))
                summed = jnp.concatenate(products, axis=0)
            else:
                values = jnp.concatenate([table_refs[index][head, :], ones], axis=1)
                summed = summed + jnp.dot(weights, values, preferred_element_type=f32)
        return summed[:, 0:LANES] / summed[:, LANES:]

    results = []
    scores = head_scores(0)
    for h in range(SET_HEADS):
        following = head_scores(h + 1) if h + 1 < SET_HEADS else None
        results.append(head_result(h, scores))
        scores = following
    for g, out_ref in enumerate(out_refs):
        rows = slice(g * CELLS, (g + 1) * CELLS)
        for t in range(2):
            both = jnp.where(low_half, results[2 * t + 1][rows], results[2 * t][rows])
            out_ref[t * CELLS : (t + 1) * CELLS, :] = turn(both).astype(bf16)
        half = lax.shift_right_logical(iota((CELLS // 2, LANES), 1), 6)
        out_ref[2 * CELLS :, :] = fold(turn(results[4][rows]), half == parity)


def assemble_kernel(place_ref, *refs):
    *in_refs, out_ref, sets_ref = refs
    place = place_ref[0]
    for k, ref in enumerate(in_refs):
        sets_ref[lax.rem(place + k, 4)] = ref[...]
    for j in range(4):
        for t in range(2):
            low = (2 * j + t) * LANES
            out_ref[:, low : low + LANES] = sets_ref[j, t * CELLS : (t + 1) * CELLS, :]
    low_half = iota((CELLS, LANES), 1) < HEAD_DIM
    for t in range(2):
        low = (8 + t) * LANES
        both = [unfold(sets_ref[2 * t + i, 2 * CELLS :, :]) for i in range(2)]
        out_ref[:, low : low + LANES] = jnp.where(low_half, *both).astype(bf16)


def call(kernel, ins, outs, *args, scratch=(), limit=24):
    return pl.pallas_call(
        kernel,
        in_specs=ins,
        out_specs=[VMEM] * len(outs),
        out_shape=[jax.ShapeDtypeStruct(shape, kind) for shape, kind in outs],
        scratch_shapes=list(scratch),
        compiler_params=pltpu.CompilerParams(vmem_limit_bytes=limit * 1024 * 1024),
        cost_estimate=pl.CostEstimate(flops=1, bytes_accessed=1, transcendentals=0),
    )(*args)


def permute(array, place):
    pairs = []
    for source in range(128):
        z, y, x, core = place(source // 32, source // 8 % 4, source // 2 % 4, source % 2)
        pairs.append((source, z % 4 * 32 + y % 4 * 8 + x % 4 * 2 + core % 2))
    return lax.ppermute(array, "patch", pairs)


def shift(array, axis, step):
    def place(*places):
        return [at + step * (name == axis) for at, name in zip(places, ("z", "y", "x", "core"))]

    return permute(array, place)


def after(array, *others):
    return lax.optimization_barrier((array, *others))[0]


def per_device(tokens, stale_keys, norm_gain, norm_bias, query_weight, pair_weight):
    place = (lax.axis_index("patch") // 2 % 4).astype(jnp.int32).reshape(1)
    table = ((SET_HEADS * CELLS, LANES), bf16)
    answer = ((ANSWER_ROWS, LANES), bf16)
    stats, tokens = call(
        local_kernel,
        [VMEM],
        [((8, LANES), f32), ((CELLS, WIDTH), bf16)],
        tokens[0],
    )
    (sets,) = call(
        sets_kernel, [VMEM, VMEM], [((4, SET_ROWS, LANES), bf16)], stats, stale_keys[0]
    )
    other = shift(stats, "core", 1)
    messages = call(
        x_kernel,
        [SMEM, VMEM, VMEM, VMEM],
        [((SET_ROWS + ROWS, LANES), bf16)] * 4,
        place,
        stats,
        other,
        sets,
    )
    received = [messages[0]] + [shift(messages[k], "x", k) for k in (1, 2, 3)]
    norm_gain, norm_bias, _ = lax.optimization_barrier((norm_gain, norm_bias, messages[0]))
    (affine,) = call(affine_kernel, [VMEM] * 2, [((2, WIDTH), f32)], norm_gain, norm_bias)
    received, affine = lax.optimization_barrier((received, affine))
    (part,) = call(z_kernel, [VMEM] * 4, [((4 * SET_ROWS + ROWS, LANES), bf16)], *received)
    parts = [part] + [shift(part, "z", k) for k in (2, 3, 1)]
    weights = [part]
    for weight, limit in ((query_weight, 49), (pair_weight, 43)):
        weight = after(weight, weights[0])
        loaded = call(
            load_kernel,
            [HBM],
            [(weight.shape, bf16)],
            weight,
            scratch=[pltpu.SemaphoreType.DMA],
            limit=limit,
        )
        weights = [*loaded, *weights]
    weights = weights[1::-1]
    parts, weights = lax.optimization_barrier((parts, weights))
    (stats,) = call(stats_kernel, [VMEM] * 4, [((8, LANES), f32)], *parts)
    all_stats = [stats] + [shift(stats, "y", k) for k in (1, 2, 3)]
    (piece,) = call(piece_kernel, [VMEM] * 5, [table], stats, *parts)
    pieces = [piece, shift(piece, "y", 1), shift(piece, "y", 3)]
    pieces.append(shift(after(piece, *all_stats), "y", 2))
    *queries, fresh = call(
        project_kernel,
        [SMEM] + [VMEM] * 8,
        [((ANSWER_ROWS + SET_ROWS, LANES), bf16)] * 4 + [((ROWS, 2 * WIDTH), bf16)],
        place,
        tokens,
        *all_stats,
        affine,
        *weights,
        scratch=[
            pltpu.VMEM((4, SET_ROWS, LANES), bf16),
            pltpu.VMEM((2, CELLS, LANES), bf16),
        ],
    )
    asked = {0: queries[0]}
    for k in (1, 2, 3):
        asked[k] = shift(after(queries[k], pieces[1]) if k == 3 else queries[k], "x", k)
    tables = pieces + [shift(after(block, asked[1]), "core", 1) for block in pieces]
    results = [None] * 4
    for sources in ((2, 1), (3,), (0,)):
        answers = call(
            functools.partial(attend_kernel, sources),
            [SMEM] + [VMEM] * (len(sources) + 8),
            [answer] * len(sources),
            place,
            *[asked[k] for k in sources],
            *tables,
            scratch=[pltpu.VMEM(*table)] * len(sources),
            limit=40,
        )
        for k, block in zip(sources, answers):
            results[k] = shift(block, "x", -k) if k else block
    (attended,) = call(
        assemble_kernel,
        [SMEM] + [VMEM] * 4,
        [((CELLS, WIDTH), bf16)],
        place,
        *results,
        scratch=[pltpu.VMEM((4, ANSWER_ROWS, LANES), bf16)],
    )
    return (attended[None], fresh[None])


def solution(mesh):
    return jax.shard_map(
        per_device,
        mesh=mesh,
        in_specs=(P("cfg", "patch", None), P("cfg", "patch", None), P(), P(), P(), P()),
        out_specs=(P("cfg", "patch", None), P("cfg", "patch", None)),
        check_vma=False,
    )
```

```python
import functools

import jax
import jax.numpy as jnp
from jax import lax
from jax.experimental import pallas as pl
from jax.experimental.pallas import tpu as pltpu
from jax.sharding import PartitionSpec as P

HEADS = 20
HEAD_DIM = 64
GROUPS = 32
POOL = 4
WIDTH = 1280
CELLS = 256
ROWS = 16
GROUP_WIDTH = WIDTH // GROUPS
LANES = 128
SET_HEADS = 5
SET_ROWS = SET_HEADS * ROWS
ANSWER_ROWS = SET_HEADS * CELLS // 2
epsilon = 1e-05

f32 = jnp.float32
bf16 = jnp.bfloat16
VMEM = pl.BlockSpec(memory_space=pltpu.VMEM)
SMEM = pl.BlockSpec(memory_space=pltpu.SMEM)
HBM = pl.BlockSpec(memory_space=pltpu.HBM)


def iota(shape, axis):
    return lax.broadcasted_iota(jnp.int32, shape, axis)


def x_place(place_ref):
    return lax.bitwise_and(lax.shift_right_logical(place_ref[0], 1), 3)


def group_of_channel():
    low = iota((WIDTH, LANES), 1) * GROUP_WIDTH
    channel = iota((WIDTH, LANES), 0)
    return ((channel >= low) & (channel < low + GROUP_WIDTH)).astype(f32).astype(bf16)


def channel_of_group():
    low = iota((LANES, WIDTH), 0) * GROUP_WIDTH
    channel = iota((LANES, WIDTH), 1)
    return ((channel >= low) & (channel < low + GROUP_WIDTH)).astype(f32).astype(bf16)


def split_rows(*rows):
    width = rows[0].shape[1]
    row = iota((ROWS, width), 0)
    split = jnp.zeros((ROWS, width), f32)
    for i, rest in enumerate(rows):
        for part in range(3):
            rounded = rest.astype(bf16).astype(f32)
            split = jnp.where(row == 3 * i + part, rounded, split)
            rest = rest - rounded
    return split.astype(bf16)


def join_rows(split, i):
    parts = split[3 * i : 3 * i + 3].astype(f32)
    return parts[0:1] + parts[1:2] + parts[2:3]


def select_dot(matrix, *rows):
    products = jnp.dot(split_rows(*rows), matrix, preferred_element_type=f32)
    return [join_rows(products, i) for i in range(len(rows))]


def combine(parts, entries):
    mean = sum(part[0:1] for part in parts) / len(parts)
    squares = sum(part[1:2] for part in parts)
    apart = sum((part[0:1] - mean) * (part[0:1] - mean) for part in parts)
    return mean, squares + entries * apart


def stack_stats(mean, squares):
    row = iota((8, LANES), 0)
    return jnp.where(row == 0, mean, jnp.where(row == 1, squares, 0.0))


def decode(rows):
    split = rows.astype(f32)
    return jnp.concatenate([join_rows(split, 0), join_rows(split, 1)], axis=0)


def head_tiles(pairs):
    lane = iota((ROWS, LANES), 1)
    even, odd = [], []
    for t in range(WIDTH // LANES):
        keys = pairs[:, t * LANES : (t + 1) * LANES].astype(f32)
        values = pairs[:, WIDTH + t * LANES : WIDTH + (t + 1) * LANES].astype(f32)
        turned = pltpu.roll(values, HEAD_DIM, 1)
        even.append(jnp.where(lane < HEAD_DIM, keys, turned).astype(bf16))
        odd.append(jnp.where(lane < HEAD_DIM, turned, keys).astype(bf16))
    sets = []
    for j in range(4):
        last = (even if j % 2 == 0 else odd)[8 + j // 2]
        sets.append(
            jnp.concatenate(
                [even[2 * j], odd[2 * j], even[2 * j + 1], odd[2 * j + 1], last], axis=0
            )
        )
    return sets


def turn(block):
    return pltpu.roll(block.astype(f32), HEAD_DIM, 1)


def fold(block, mask):
    half = CELLS // 2
    return jnp.where(mask, block[0:half].astype(f32), turn(block[half:])).astype(bf16)


def unfold(block):
    return jnp.concatenate([block.astype(f32), turn(block)], axis=0)


def local_kernel(tokens_ref, stats_ref, kept_ref):
    tokens = tokens_ref[...]
    kept_ref[...] = tokens
    values = tokens.astype(f32)
    (mean,) = select_dot(group_of_channel(), jnp.sum(values, axis=0, keepdims=True))
    mean = mean / (CELLS * GROUP_WIDTH)
    (center,) = select_dot(channel_of_group(), mean)
    shifted = values - center
    (squares,) = select_dot(
        group_of_channel(), jnp.sum(shifted * shifted, axis=0, keepdims=True)
    )
    stats_ref[...] = stack_stats(mean, squares)


def sets_kernel(stats_ref, stale_ref, sets_ref):
    for j, block in enumerate(head_tiles(stale_ref[...])):
        sets_ref[j] = block


def x_kernel(place_ref, own_ref, other_ref, sets_ref, *out_refs):
    mean, squares = combine([own_ref[...], other_ref[...]], CELLS * GROUP_WIDTH)
    coded = split_rows(mean, squares)
    place = x_place(place_ref)
    for k, out_ref in enumerate(out_refs):
        out_ref[0:SET_ROWS, :] = sets_ref[lax.rem(place + k, 4)]
        out_ref[SET_ROWS:, :] = coded


def affine_kernel(gain_ref, bias_ref, out_ref):
    out_ref[0:1, :] = gain_ref[...].reshape(1, WIDTH)
    out_ref[1:2, :] = bias_ref[...].reshape(1, WIDTH)


def z_kernel(*refs):
    *in_refs, out_ref = refs
    stats = [decode(ref[SET_ROWS:, :]) for ref in in_refs]
    mean, squares = combine(stats, 2 * CELLS * GROUP_WIDTH)
    for k, ref in enumerate(in_refs):
        for h in range(SET_HEADS):
            low = h * 4 * ROWS + k * ROWS
            out_ref[low : low + ROWS, :] = ref[h * ROWS : (h + 1) * ROWS, :]
    out_ref[4 * SET_ROWS :, :] = split_rows(mean, squares)


def stats_kernel(*refs):
    *in_refs, stats_ref = refs
    stats = [decode(ref[4 * SET_ROWS :, :]) for ref in in_refs]
    mean, squares = combine(stats, 8 * CELLS * GROUP_WIDTH)
    stats_ref[...] = stack_stats(mean, squares)


def all_stats_kernel(s0, s1, s2, s3, stats_ref):
    mean, squares = combine([s0[...], s1[...], s2[...], s3[...]], 32 * CELLS * GROUP_WIDTH)
    stats_ref[...] = stack_stats(mean, squares)


def piece_kernel(stats_ref, *refs):
    *in_refs, out_ref = refs
    for k, ref in enumerate(in_refs):
        for h in range(SET_HEADS):
            low = h * CELLS + k * 4 * ROWS
            out_ref[low : low + 4 * ROWS, :] = ref[h * 4 * ROWS : (h + 1) * 4 * ROWS, :]


def load_kernel(source_hbm, target_ref, arrived):
    copy = pltpu.make_async_copy(source_hbm, target_ref, arrived)
    copy.start()
    copy.wait()


def project_kernel(
    place_ref, tokens_ref, own_ref, other_ref, affine_ref, query_ref, pair_ref, *refs
):
    *message_refs, fresh_ref, sets_ref, last_ref = refs
    stats = jnp.where(lax.bitwise_and(place_ref[0], 1) == 1, own_ref[...], other_ref[...])
    mean, squares = stats[0:1], stats[1:2]
    spread = squares / (128 * CELLS * GROUP_WIDTH)
    center, inverse = select_dot(channel_of_group(), mean, lax.rsqrt(spread + epsilon))
    scaled = (tokens_ref[...].astype(f32) - center) * inverse
    normed = (scaled * affine_ref[0:1] + affine_ref[1:2]).astype(bf16)

    square = iota((ROWS, CELLS), 0)
    cell = iota((ROWS, CELLS), 1)
    cell_square = lax.shift_right_logical(lax.bitwise_and(cell, 63), 2)
    pool = jnp.where(cell_square == square, 1.0 / (POOL * POOL), 0.0).astype(bf16)
    pooled = jnp.dot(pool, normed, preferred_element_type=f32).astype(bf16)

    place = x_place(place_ref)
    last = jnp.dot(normed, query_ref[:, 1024:], preferred_element_type=f32).astype(bf16)
    last_ref[0] = last[:, 0:LANES]
    last_ref[1] = last[:, LANES:]
    lane_half = lax.shift_right_logical(iota((CELLS // 2, LANES), 1), 6)
    for k in (2, 1, 3, 0):
        j = lax.rem(place + k, 4)
        columns = pl.ds(pl.multiple_of(j * 256, 256), 256)
        block = jnp.dot(normed, query_ref[:, columns], preferred_element_type=f32).astype(bf16)
        message_refs[k][0:CELLS, :] = block[:, 0:LANES]
        message_refs[k][CELLS : 2 * CELLS, :] = block[:, LANES:]
        mask = lane_half == lax.bitwise_and(j, 1)
        message_refs[k][2 * CELLS : ANSWER_ROWS, :] = fold(
            last_ref[lax.shift_right_logical(j, 1)], mask
        )

    fresh = jnp.dot(pooled, pair_ref[...], preferred_element_type=f32).astype(bf16)
    fresh_ref[...] = fresh
    for j, block in enumerate(head_tiles(fresh)):
        sets_ref[j] = block
    for k in range(4):
        message_refs[k][ANSWER_ROWS:, :] = sets_ref[lax.rem(place + k, 4)]


def attend_kernel(sources, place_ref, *refs):
    count = len(sources)
    message_refs, table_refs = refs[:count], refs[count : count + 8]
    out_refs, first_refs = refs[count + 8 : 2 * count + 8], refs[2 * count + 8 :]
    for source, message_ref, first_ref in zip(sources, message_refs, first_refs):
        first_ref[...] = table_refs[0][...]
        for h in range(SET_HEADS):
            low = h * CELLS + source * ROWS
            fresh = message_ref[ANSWER_ROWS + h * ROWS : ANSWER_ROWS + (h + 1) * ROWS, :]
            first_ref[low : low + ROWS, :] = fresh
    lane = iota((CELLS, LANES), 1)
    low_half = lane < HEAD_DIM
    parity = lax.bitwise_and(x_place(place_ref), 1)
    factor = HEAD_DIM ** (-0.5) * 1.4426950408889634
    against = (((1,), (1,)), ((), ()))
    ones = jnp.ones((CELLS, LANES), bf16)

    def head_scores(h):
        if h < 4:
            mask = low_half if h % 2 == 0 else jnp.logical_not(low_half)
        else:
            mask = lax.shift_right_logical(lane, 6) == parity
        groups = []
        for message_ref in message_refs:
            if h < 4:
                queries = message_ref[(h // 2) * CELLS : (h // 2 + 1) * CELLS, :].astype(f32)
            else:
                queries = unfold(message_ref[2 * CELLS : ANSWER_ROWS, :])
            groups.append(jnp.where(mask, queries, 0.0).astype(bf16))
        queries = jnp.concatenate(groups, axis=0) if count > 1 else groups[0]
        head = slice(h * CELLS, (h + 1) * CELLS)
        firsts = [
            lax.dot_general(group, ref[head, :], against, preferred_element_type=f32)
            for group, ref in zip(groups, first_refs)
        ]
        scores = [jnp.concatenate(firsts, axis=0)]
        for ref in table_refs[1:]:
            keys = ref[head, :]
            scores.append(lax.dot_general(queries, keys, against, preferred_element_type=f32))
        return scores

    def head_result(h, scores):
        head = slice(h * CELLS, (h + 1) * CELLS)
        largest = scores[0]
        for part in scores[1:]:
            largest = jnp.maximum(largest, part)
        largest = jnp.max(largest, axis=1, keepdims=True)
        summed = None
        for index, part in enumerate(scores):
            weights = jnp.exp2((part - largest) * factor).astype(bf16)
            if index == 0:
                products = []
                for g, ref in enumerate(first_refs):
                    values = jnp.concatenate([ref[head, :], ones], axis=1)
                    rows = weights[g * CELLS : (g + 1) * CELLS]
                    products.append(jnp.dot(rows, values, preferred_element_type=f32))
                summed = jnp.concatenate(products, axis=0)
            else:
                values = jnp.concatenate([table_refs[index][head, :], ones], axis=1)
                summed = summed + jnp.dot(weights, values, preferred_element_type=f32)
        return summed[:, 0:LANES] / summed[:, LANES:]

    results = []
    scores = head_scores(0)
    for h in range(SET_HEADS):
        following = head_scores(h + 1) if h + 1 < SET_HEADS else None
        results.append(head_result(h, scores))
        scores = following
    for g, out_ref in enumerate(out_refs):
        rows = slice(g * CELLS, (g + 1) * CELLS)
        for t in range(2):
            both = jnp.where(low_half, results[2 * t + 1][rows], results[2 * t][rows])
            out_ref[t * CELLS : (t + 1) * CELLS, :] = turn(both).astype(bf16)
        half = lax.shift_right_logical(iota((CELLS // 2, LANES), 1), 6)
        out_ref[2 * CELLS :, :] = fold(turn(results[4][rows]), half == parity)


def assemble_kernel(place_ref, *refs):
    *in_refs, out_ref, sets_ref = refs
    place = x_place(place_ref)
    for k, ref in enumerate(in_refs):
        sets_ref[lax.rem(place + k, 4)] = ref[...]
    for j in range(4):
        for t in range(2):
            low = (2 * j + t) * LANES
            out_ref[:, low : low + LANES] = sets_ref[j, t * CELLS : (t + 1) * CELLS, :]
    low_half = iota((CELLS, LANES), 1) < HEAD_DIM
    for t in range(2):
        low = (8 + t) * LANES
        both = [unfold(sets_ref[2 * t + i, 2 * CELLS :, :]) for i in range(2)]
        out_ref[:, low : low + LANES] = jnp.where(low_half, *both).astype(bf16)


def call(kernel, ins, outs, *args, scratch=(), limit=24):
    return pl.pallas_call(
        kernel,
        in_specs=ins,
        out_specs=[VMEM] * len(outs),
        out_shape=[jax.ShapeDtypeStruct(shape, kind) for shape, kind in outs],
        scratch_shapes=list(scratch),
        compiler_params=pltpu.CompilerParams(vmem_limit_bytes=limit * 1024 * 1024),
        cost_estimate=pl.CostEstimate(flops=1, bytes_accessed=1, transcendentals=0),
    )(*args)


AXES = {"z": (32, 4), "y": (8, 4), "x": (2, 4), "core": (1, 2)}


def shift(array, axis, step, cores=(0, 1)):
    stride, size = AXES[axis]
    pairs = []
    for source in range(128):
        place = source // stride % size
        if source % 2 in cores:
            pairs.append((source, source + ((place + step) % size - place) * stride))
    return lax.ppermute(array, "patch", pairs)


def after(array, *others):
    return lax.optimization_barrier((array, *others))[0]


def per_device(tokens, stale_keys, norm_gain, norm_bias, query_weight, pair_weight):
    place = lax.axis_index("patch").astype(jnp.int32).reshape(1)
    table = ((SET_HEADS * CELLS, LANES), bf16)
    answer = ((ANSWER_ROWS, LANES), bf16)
    stats, tokens = call(
        local_kernel,
        [VMEM],
        [((8, LANES), f32), ((CELLS, WIDTH), bf16)],
        tokens[0],
    )
    (sets,) = call(
        sets_kernel, [VMEM, VMEM], [((4, SET_ROWS, LANES), bf16)], stats, stale_keys[0]
    )
    other = shift(stats, "core", 1)
    messages = call(
        x_kernel,
        [SMEM, VMEM, VMEM, VMEM],
        [((SET_ROWS + ROWS, LANES), bf16)] * 4,
        place,
        stats,
        other,
        sets,
    )
    received = [messages[0]] + [shift(messages[k], "x", k) for k in (1, 2, 3)]
    norm_gain, norm_bias, _ = lax.optimization_barrier((norm_gain, norm_bias, messages[0]))
    (affine,) = call(affine_kernel, [VMEM] * 2, [((2, WIDTH), f32)], norm_gain, norm_bias)
    received, affine = lax.optimization_barrier((received, affine))
    (part,) = call(z_kernel, [VMEM] * 4, [((4 * SET_ROWS + ROWS, LANES), bf16)], *received)
    parts = [part] + [shift(part, "z", k) for k in (2, 3, 1)]
    weights = [part]
    for weight, limit in ((query_weight, 49), (pair_weight, 43)):
        weight = after(weight, weights[0])
        loaded = call(
            load_kernel,
            [HBM],
            [(weight.shape, bf16)],
            weight,
            scratch=[pltpu.SemaphoreType.DMA],
            limit=limit,
        )
        weights = [*loaded, *weights]
    weights = weights[1::-1]
    parts, weights = lax.optimization_barrier((parts, weights))
    (stats,) = call(stats_kernel, [VMEM] * 4, [((8, LANES), f32)], *parts)
    y_stats = [stats] + [shift(stats, "y", k, cores=(1,)) for k in (1, 2, 3)]
    (piece,) = call(piece_kernel, [VMEM] * 5, [table], stats, *parts)
    pieces = [piece, shift(piece, "y", 1), shift(piece, "y", 3)]
    (stats,) = call(all_stats_kernel, [VMEM] * 4, [((8, LANES), f32)], *y_stats)
    pieces.append(shift(after(piece, stats), "y", 2))
    both_stats = [stats, shift(stats, "core", 1, cores=(1,))]
    *queries, fresh = call(
        project_kernel,
        [SMEM] + [VMEM] * 6,
        [((ANSWER_ROWS + SET_ROWS, LANES), bf16)] * 4 + [((ROWS, 2 * WIDTH), bf16)],
        place,
        tokens,
        *both_stats,
        affine,
        *weights,
        scratch=[
            pltpu.VMEM((4, SET_ROWS, LANES), bf16),
            pltpu.VMEM((2, CELLS, LANES), bf16),
        ],
    )
    asked = {0: queries[0]}
    for k in (1, 2, 3):
        asked[k] = shift(after(queries[k], pieces[1]) if k == 3 else queries[k], "x", k)
    tables = pieces + [shift(after(block, asked[1]), "core", 1) for block in pieces]
    results = [None] * 4
    for sources in ((2, 1), (3,), (0,)):
        answers = call(
            functools.partial(attend_kernel, sources),
            [SMEM] + [VMEM] * (len(sources) + 8),
            [answer] * len(sources),
            place,
            *[asked[k] for k in sources],
            *tables,
            scratch=[pltpu.VMEM(*table)] * len(sources),
            limit=40,
        )
        for k, block in zip(sources, answers):
            results[k] = shift(block, "x", -k) if k else block
    (attended,) = call(
        assemble_kernel,
        [SMEM] + [VMEM] * 4,
        [((CELLS, WIDTH), bf16)],
        place,
        *results,
        scratch=[pltpu.VMEM((4, ANSWER_ROWS, LANES), bf16)],
    )
    return (attended[None], fresh[None])


def solution(mesh):
    return jax.shard_map(
        per_device,
        mesh=mesh,
        in_specs=(P("cfg", "patch", None), P("cfg", "patch", None), P(), P(), P(), P()),
        out_specs=(P("cfg", "patch", None), P("cfg", "patch", None)),
        check_vma=False,
    )
```

```python
import functools

import jax
import jax.numpy as jnp
from jax import lax
from jax.experimental import pallas as pl
from jax.experimental.pallas import tpu as pltpu
from jax.sharding import PartitionSpec as P

HEADS = 20
HEAD_DIM = 64
GROUPS = 32
POOL = 4
WIDTH = 1280
CELLS = 256
ROWS = 16
GROUP_WIDTH = WIDTH // GROUPS
LANES = 128
SET_HEADS = 5
SET_ROWS = SET_HEADS * ROWS
ANSWER_ROWS = SET_HEADS * CELLS // 2
epsilon = 1e-05

f32 = jnp.float32
bf16 = jnp.bfloat16
VMEM = pl.BlockSpec(memory_space=pltpu.VMEM)
SMEM = pl.BlockSpec(memory_space=pltpu.SMEM)
HBM = pl.BlockSpec(memory_space=pltpu.HBM)


def iota(shape, axis):
    return lax.broadcasted_iota(jnp.int32, shape, axis)


def x_peer(place_ref, k):
    place = place_ref[0]
    step = k * (1 - 2 * lax.bitwise_and(place, 1))
    return lax.bitwise_and(lax.shift_right_logical(place, 1) + step, 3)


def group_of_channel():
    low = iota((WIDTH, LANES), 1) * GROUP_WIDTH
    channel = iota((WIDTH, LANES), 0)
    return ((channel >= low) & (channel < low + GROUP_WIDTH)).astype(f32).astype(bf16)


def channel_of_group():
    low = iota((LANES, WIDTH), 0) * GROUP_WIDTH
    channel = iota((LANES, WIDTH), 1)
    return ((channel >= low) & (channel < low + GROUP_WIDTH)).astype(f32).astype(bf16)


def split_rows(*rows):
    width = rows[0].shape[1]
    row = iota((ROWS, width), 0)
    split = jnp.zeros((ROWS, width), f32)
    for i, rest in enumerate(rows):
        for part in range(3):
            rounded = rest.astype(bf16).astype(f32)
            split = jnp.where(row == 3 * i + part, rounded, split)
            rest = rest - rounded
    return split.astype(bf16)


def join_rows(split, i):
    parts = split[3 * i : 3 * i + 3].astype(f32)
    return parts[0:1] + parts[1:2] + parts[2:3]


def select_dot(matrix, *rows):
    products = jnp.dot(split_rows(*rows), matrix, preferred_element_type=f32)
    return [join_rows(products, i) for i in range(len(rows))]


def combine(parts, entries):
    mean = sum(part[0:1] for part in parts) / len(parts)
    squares = sum(part[1:2] for part in parts)
    apart = sum((part[0:1] - mean) * (part[0:1] - mean) for part in parts)
    return mean, squares + entries * apart


def stack_stats(mean, squares):
    row = iota((8, LANES), 0)
    return jnp.where(row == 0, mean, jnp.where(row == 1, squares, 0.0))


def decode(rows):
    split = rows.astype(f32)
    return jnp.concatenate([join_rows(split, 0), join_rows(split, 1)], axis=0)


def head_tiles(pairs):
    lane = iota((ROWS, LANES), 1)
    even, odd = [], []
    for t in range(WIDTH // LANES):
        keys = pairs[:, t * LANES : (t + 1) * LANES].astype(f32)
        values = pairs[:, WIDTH + t * LANES : WIDTH + (t + 1) * LANES].astype(f32)
        turned = pltpu.roll(values, HEAD_DIM, 1)
        even.append(jnp.where(lane < HEAD_DIM, keys, turned).astype(bf16))
        odd.append(jnp.where(lane < HEAD_DIM, turned, keys).astype(bf16))
    sets = []
    for j in range(4):
        last = (even if j % 2 == 0 else odd)[8 + j // 2]
        sets.append(
            jnp.concatenate(
                [even[2 * j], odd[2 * j], even[2 * j + 1], odd[2 * j + 1], last], axis=0
            )
        )
    return sets


def turn(block):
    return pltpu.roll(block.astype(f32), HEAD_DIM, 1)


def fold(block, mask):
    half = CELLS // 2
    return jnp.where(mask, block[0:half].astype(f32), turn(block[half:])).astype(bf16)


def unfold(block):
    return jnp.concatenate([block.astype(f32), turn(block)], axis=0)


def local_kernel(tokens_ref, stats_ref, kept_ref):
    tokens = tokens_ref[...]
    kept_ref[...] = tokens
    values = tokens.astype(f32)
    (mean,) = select_dot(group_of_channel(), jnp.sum(values, axis=0, keepdims=True))
    mean = mean / (CELLS * GROUP_WIDTH)
    (center,) = select_dot(channel_of_group(), mean)
    shifted = values - center
    (squares,) = select_dot(
        group_of_channel(), jnp.sum(shifted * shifted, axis=0, keepdims=True)
    )
    stats_ref[...] = stack_stats(mean, squares)


def sets_kernel(stats_ref, stale_ref, sets_ref):
    for j, block in enumerate(head_tiles(stale_ref[...])):
        sets_ref[j] = block


def x_kernel(place_ref, own_ref, other_ref, sets_ref, *out_refs):
    mean, squares = combine([own_ref[...], other_ref[...]], CELLS * GROUP_WIDTH)
    coded = split_rows(mean, squares)
    for k, out_ref in enumerate(out_refs):
        out_ref[0:SET_ROWS, :] = sets_ref[x_peer(place_ref, k)]
        out_ref[SET_ROWS:, :] = coded


def affine_kernel(gain_ref, bias_ref, out_ref):
    out_ref[0:1, :] = gain_ref[...].reshape(1, WIDTH)
    out_ref[1:2, :] = bias_ref[...].reshape(1, WIDTH)


def z_kernel(*refs):
    *in_refs, out_ref = refs
    stats = [decode(ref[SET_ROWS:, :]) for ref in in_refs]
    mean, squares = combine(stats, 2 * CELLS * GROUP_WIDTH)
    for k, ref in enumerate(in_refs):
        for h in range(SET_HEADS):
            low = h * 4 * ROWS + k * ROWS
            out_ref[low : low + ROWS, :] = ref[h * ROWS : (h + 1) * ROWS, :]
    out_ref[4 * SET_ROWS :, :] = split_rows(mean, squares)


def stats_kernel(*refs):
    *in_refs, stats_ref = refs
    stats = [decode(ref[4 * SET_ROWS :, :]) for ref in in_refs]
    mean, squares = combine(stats, 8 * CELLS * GROUP_WIDTH)
    stats_ref[...] = stack_stats(mean, squares)


def piece_kernel(stats_ref, *refs):
    *in_refs, out_ref = refs
    for k, ref in enumerate(in_refs):
        for h in range(SET_HEADS):
            low = h * CELLS + k * 4 * ROWS
            out_ref[low : low + 4 * ROWS, :] = ref[h * 4 * ROWS : (h + 1) * 4 * ROWS, :]


def load_kernel(source_hbm, target_ref, arrived):
    copy = pltpu.make_async_copy(source_hbm, target_ref, arrived)
    copy.start()
    copy.wait()


def project_kernel(
    place_ref, tokens_ref, s0, s1, s2, s3, affine_ref, query_ref, pair_ref, *refs
):
    *message_refs, fresh_ref, sets_ref, last_ref = refs
    mean, squares = combine([s0[...], s1[...], s2[...], s3[...]], 32 * CELLS * GROUP_WIDTH)
    spread = squares / (128 * CELLS * GROUP_WIDTH)
    center, inverse = select_dot(channel_of_group(), mean, lax.rsqrt(spread + epsilon))
    scaled = (tokens_ref[...].astype(f32) - center) * inverse
    normed = (scaled * affine_ref[0:1] + affine_ref[1:2]).astype(bf16)

    square = iota((ROWS, CELLS), 0)
    cell = iota((ROWS, CELLS), 1)
    cell_square = lax.shift_right_logical(lax.bitwise_and(cell, 63), 2)
    pool = jnp.where(cell_square == square, 1.0 / (POOL * POOL), 0.0).astype(bf16)
    pooled = jnp.dot(pool, normed, preferred_element_type=f32).astype(bf16)

    last = jnp.dot(normed, query_ref[:, 1024:], preferred_element_type=f32).astype(bf16)
    last_ref[0] = last[:, 0:LANES]
    last_ref[1] = last[:, LANES:]
    lane_half = lax.shift_right_logical(iota((CELLS // 2, LANES), 1), 6)
    for k in (2, 1, 3, 0):
        j = x_peer(place_ref, k)
        columns = pl.ds(pl.multiple_of(j * 256, 256), 256)
        block = jnp.dot(normed, query_ref[:, columns], preferred_element_type=f32).astype(bf16)
        message_refs[k][0:CELLS, :] = block[:, 0:LANES]
        message_refs[k][CELLS : 2 * CELLS, :] = block[:, LANES:]
        mask = lane_half == lax.bitwise_and(j, 1)
        message_refs[k][2 * CELLS : ANSWER_ROWS, :] = fold(
            last_ref[lax.shift_right_logical(j, 1)], mask
        )

    fresh = jnp.dot(pooled, pair_ref[...], preferred_element_type=f32).astype(bf16)
    fresh_ref[...] = fresh
    for j, block in enumerate(head_tiles(fresh)):
        sets_ref[j] = block
    for k in range(4):
        message_refs[k][ANSWER_ROWS:, :] = sets_ref[x_peer(place_ref, k)]


def attend_kernel(sources, place_ref, *refs):
    count = len(sources)
    message_refs, table_refs = refs[:count], refs[count : count + 8]
    out_refs, first_refs = refs[count + 8 : 2 * count + 8], refs[2 * count + 8 :]
    for source, message_ref, first_ref in zip(sources, message_refs, first_refs):
        first_ref[...] = table_refs[0][...]
        for h in range(SET_HEADS):
            low = h * CELLS + source * ROWS
            fresh = message_ref[ANSWER_ROWS + h * ROWS : ANSWER_ROWS + (h + 1) * ROWS, :]
            first_ref[low : low + ROWS, :] = fresh
    lane = iota((CELLS, LANES), 1)
    low_half = lane < HEAD_DIM
    parity = lax.bitwise_and(x_peer(place_ref, 0), 1)
    factor = HEAD_DIM ** (-0.5) * 1.4426950408889634
    against = (((1,), (1,)), ((), ()))
    ones = jnp.ones((CELLS, LANES), bf16)

    def head_scores(h):
        if h < 4:
            mask = low_half if h % 2 == 0 else jnp.logical_not(low_half)
        else:
            mask = lax.shift_right_logical(lane, 6) == parity
        groups = []
        for message_ref in message_refs:
            if h < 4:
                queries = message_ref[(h // 2) * CELLS : (h // 2 + 1) * CELLS, :].astype(f32)
            else:
                queries = unfold(message_ref[2 * CELLS : ANSWER_ROWS, :])
            groups.append(jnp.where(mask, queries, 0.0).astype(bf16))
        queries = jnp.concatenate(groups, axis=0) if count > 1 else groups[0]
        head = slice(h * CELLS, (h + 1) * CELLS)
        firsts = [
            lax.dot_general(group, ref[head, :], against, preferred_element_type=f32)
            for group, ref in zip(groups, first_refs)
        ]
        scores = [jnp.concatenate(firsts, axis=0)]
        for ref in table_refs[1:]:
            keys = ref[head, :]
            scores.append(lax.dot_general(queries, keys, against, preferred_element_type=f32))
        return scores

    def head_result(h, scores):
        head = slice(h * CELLS, (h + 1) * CELLS)
        largest = scores[0]
        for part in scores[1:]:
            largest = jnp.maximum(largest, part)
        largest = jnp.max(largest, axis=1, keepdims=True)
        summed = None
        for index, part in enumerate(scores):
            weights = jnp.exp2((part - largest) * factor).astype(bf16)
            if index == 0:
                products = []
                for g, ref in enumerate(first_refs):
                    values = jnp.concatenate([ref[head, :], ones], axis=1)
                    rows = weights[g * CELLS : (g + 1) * CELLS]
                    products.append(jnp.dot(rows, values, preferred_element_type=f32))
                summed = jnp.concatenate(products, axis=0)
            else:
                values = jnp.concatenate([table_refs[index][head, :], ones], axis=1)
                summed = summed + jnp.dot(weights, values, preferred_element_type=f32)
        return summed[:, 0:LANES] / summed[:, LANES:]

    results = []
    scores = head_scores(0)
    for h in range(SET_HEADS):
        following = head_scores(h + 1) if h + 1 < SET_HEADS else None
        results.append(head_result(h, scores))
        scores = following
    for g, out_ref in enumerate(out_refs):
        rows = slice(g * CELLS, (g + 1) * CELLS)
        for t in range(2):
            both = jnp.where(low_half, results[2 * t + 1][rows], results[2 * t][rows])
            out_ref[t * CELLS : (t + 1) * CELLS, :] = turn(both).astype(bf16)
        half = lax.shift_right_logical(iota((CELLS // 2, LANES), 1), 6)
        out_ref[2 * CELLS :, :] = fold(turn(results[4][rows]), half == parity)


def assemble_kernel(place_ref, *refs):
    *in_refs, out_ref, sets_ref = refs
    for k, ref in enumerate(in_refs):
        sets_ref[x_peer(place_ref, k)] = ref[...]
    for j in range(4):
        for t in range(2):
            low = (2 * j + t) * LANES
            out_ref[:, low : low + LANES] = sets_ref[j, t * CELLS : (t + 1) * CELLS, :]
    low_half = iota((CELLS, LANES), 1) < HEAD_DIM
    for t in range(2):
        low = (8 + t) * LANES
        both = [unfold(sets_ref[2 * t + i, 2 * CELLS :, :]) for i in range(2)]
        out_ref[:, low : low + LANES] = jnp.where(low_half, *both).astype(bf16)


def call(kernel, ins, outs, *args, scratch=(), limit=24):
    return pl.pallas_call(
        kernel,
        in_specs=ins,
        out_specs=[VMEM] * len(outs),
        out_shape=[jax.ShapeDtypeStruct(shape, kind) for shape, kind in outs],
        scratch_shapes=list(scratch),
        compiler_params=pltpu.CompilerParams(vmem_limit_bytes=limit * 1024 * 1024),
        cost_estimate=pl.CostEstimate(flops=1, bytes_accessed=1, transcendentals=0),
    )(*args)


AXES = {"z": (32, 4), "y": (8, 4), "x": (2, 4), "core": (1, 2)}


def shift(array, axis, step):
    stride, size = AXES[axis]
    pairs = []
    for source in range(128):
        place = source // stride % size
        target = (place + step * (1 - 2 * (source % 2))) % size
        pairs.append((source, source + (target - place) * stride))
    return lax.ppermute(array, "patch", pairs)


def after(array, *others):
    return lax.optimization_barrier((array, *others))[0]


def per_device(tokens, stale_keys, norm_gain, norm_bias, query_weight, pair_weight):
    place = lax.axis_index("patch").astype(jnp.int32).reshape(1)
    table = ((SET_HEADS * CELLS, LANES), bf16)
    answer = ((ANSWER_ROWS, LANES), bf16)
    stats, tokens = call(
        local_kernel,
        [VMEM],
        [((8, LANES), f32), ((CELLS, WIDTH), bf16)],
        tokens[0],
    )
    (sets,) = call(
        sets_kernel, [VMEM, VMEM], [((4, SET_ROWS, LANES), bf16)], stats, stale_keys[0]
    )
    other = shift(stats, "core", 1)
    messages = call(
        x_kernel,
        [SMEM, VMEM, VMEM, VMEM],
        [((SET_ROWS + ROWS, LANES), bf16)] * 4,
        place,
        stats,
        other,
        sets,
    )
    received = [messages[0]] + [shift(messages[k], "x", k) for k in (1, 2, 3)]
    norm_gain, norm_bias, _ = lax.optimization_barrier((norm_gain, norm_bias, messages[0]))
    (affine,) = call(affine_kernel, [VMEM] * 2, [((2, WIDTH), f32)], norm_gain, norm_bias)
    received, affine = lax.optimization_barrier((received, affine))
    (part,) = call(z_kernel, [VMEM] * 4, [((4 * SET_ROWS + ROWS, LANES), bf16)], *received)
    parts = [part] + [shift(part, "z", k) for k in (2, 3, 1)]
    weights = [part]
    for weight, limit in ((query_weight, 49), (pair_weight, 43)):
        weight = after(weight, weights[0])
        loaded = call(
            load_kernel,
            [HBM],
            [(weight.shape, bf16)],
            weight,
            scratch=[pltpu.SemaphoreType.DMA],
            limit=limit,
        )
        weights = [*loaded, *weights]
    weights = weights[1::-1]
    parts, weights = lax.optimization_barrier((parts, weights))
    (stats,) = call(stats_kernel, [VMEM] * 4, [((8, LANES), f32)], *parts)
    all_stats = [stats] + [shift(stats, "y", k) for k in (1, 2, 3)]
    (piece,) = call(piece_kernel, [VMEM] * 5, [table], stats, *parts)
    pieces = [piece, shift(piece, "y", 1), shift(piece, "y", 3)]
    pieces.append(shift(after(piece, *all_stats), "y", 2))
    *queries, fresh = call(
        project_kernel,
        [SMEM] + [VMEM] * 8,
        [((ANSWER_ROWS + SET_ROWS, LANES), bf16)] * 4 + [((ROWS, 2 * WIDTH), bf16)],
        place,
        tokens,
        *all_stats,
        affine,
        *weights,
        scratch=[
            pltpu.VMEM((4, SET_ROWS, LANES), bf16),
            pltpu.VMEM((2, CELLS, LANES), bf16),
        ],
    )
    asked = {0: queries[0]}
    for k in (1, 2, 3):
        asked[k] = shift(after(queries[k], pieces[1]) if k == 3 else queries[k], "x", k)
    tables = pieces + [shift(after(block, asked[1]), "core", 1) for block in pieces]
    results = [None] * 4
    for sources in ((2, 1), (3,), (0,)):
        answers = call(
            functools.partial(attend_kernel, sources),
            [SMEM] + [VMEM] * (len(sources) + 8),
            [answer] * len(sources),
            place,
            *[asked[k] for k in sources],
            *tables,
            scratch=[pltpu.VMEM(*table)] * len(sources),
            limit=40,
        )
        for k, block in zip(sources, answers):
            results[k] = shift(block, "x", -k) if k else block
    (attended,) = call(
        assemble_kernel,
        [SMEM] + [VMEM] * 4,
        [((CELLS, WIDTH), bf16)],
        place,
        *results,
        scratch=[pltpu.VMEM((4, ANSWER_ROWS, LANES), bf16)],
    )
    return (attended[None], fresh[None])


def solution(mesh):
    return jax.shard_map(
        per_device,
        mesh=mesh,
        in_specs=(P("cfg", "patch", None), P("cfg", "patch", None), P(), P(), P(), P()),
        out_specs=(P("cfg", "patch", None), P("cfg", "patch", None)),
        check_vma=False,
    )
```

```python
import functools

import jax
import jax.numpy as jnp
from jax import lax
from jax.experimental import pallas as pl
from jax.experimental.pallas import tpu as pltpu
from jax.sharding import PartitionSpec as P

HEADS = 20
HEAD_DIM = 64
GROUPS = 32
POOL = 4
WIDTH = 1280
CELLS = 256
ROWS = 16
GROUP_WIDTH = WIDTH // GROUPS
LANES = 128
SET_HEADS = 5
SET_ROWS = SET_HEADS * ROWS
ANSWER_ROWS = SET_HEADS * CELLS // 2
epsilon = 1e-05

f32 = jnp.float32
bf16 = jnp.bfloat16
VMEM = pl.BlockSpec(memory_space=pltpu.VMEM)
SMEM = pl.BlockSpec(memory_space=pltpu.SMEM)
HBM = pl.BlockSpec(memory_space=pltpu.HBM)


def iota(shape, axis):
    return lax.broadcasted_iota(jnp.int32, shape, axis)


def x_place(place_ref):
    return lax.bitwise_and(lax.shift_right_logical(place_ref[0], 1), 3)


def group_of_channel():
    low = iota((WIDTH, LANES), 1) * GROUP_WIDTH
    channel = iota((WIDTH, LANES), 0)
    return ((channel >= low) & (channel < low + GROUP_WIDTH)).astype(f32).astype(bf16)


def channel_of_group():
    low = iota((LANES, WIDTH), 0) * GROUP_WIDTH
    channel = iota((LANES, WIDTH), 1)
    return ((channel >= low) & (channel < low + GROUP_WIDTH)).astype(f32).astype(bf16)


def split_rows(*rows):
    width = rows[0].shape[1]
    row = iota((ROWS, width), 0)
    split = jnp.zeros((ROWS, width), f32)
    for i, rest in enumerate(rows):
        for part in range(3):
            rounded = rest.astype(bf16).astype(f32)
            split = jnp.where(row == 3 * i + part, rounded, split)
            rest = rest - rounded
    return split.astype(bf16)


def join_rows(split, i):
    parts = split[3 * i : 3 * i + 3].astype(f32)
    return parts[0:1] + parts[1:2] + parts[2:3]


def select_dot(matrix, *rows):
    products = jnp.dot(split_rows(*rows), matrix, preferred_element_type=f32)
    return [join_rows(products, i) for i in range(len(rows))]


def combine(parts, entries):
    mean = sum(part[0:1] for part in parts) / len(parts)
    squares = sum(part[1:2] for part in parts)
    apart = sum((part[0:1] - mean) * (part[0:1] - mean) for part in parts)
    return mean, squares + entries * apart


def stack_stats(mean, squares):
    row = iota((8, LANES), 0)
    return jnp.where(row == 0, mean, jnp.where(row == 1, squares, 0.0))


def decode(rows):
    split = rows.astype(f32)
    return jnp.concatenate([join_rows(split, 0), join_rows(split, 1)], axis=0)


def head_tiles(pairs):
    lane = iota((ROWS, LANES), 1)
    even, odd = [], []
    for t in range(WIDTH // LANES):
        keys = pairs[:, t * LANES : (t + 1) * LANES].astype(f32)
        values = pairs[:, WIDTH + t * LANES : WIDTH + (t + 1) * LANES].astype(f32)
        turned = pltpu.roll(values, HEAD_DIM, 1)
        even.append(jnp.where(lane < HEAD_DIM, keys, turned).astype(bf16))
        odd.append(jnp.where(lane < HEAD_DIM, turned, keys).astype(bf16))
    sets = []
    for j in range(4):
        last = (even if j % 2 == 0 else odd)[8 + j // 2]
        sets.append(
            jnp.concatenate(
                [even[2 * j], odd[2 * j], even[2 * j + 1], odd[2 * j + 1], last], axis=0
            )
        )
    return sets


def turn(block):
    return pltpu.roll(block.astype(f32), HEAD_DIM, 1)


def fold(block, mask):
    half = CELLS // 2
    return jnp.where(mask, block[0:half].astype(f32), turn(block[half:])).astype(bf16)


def unfold(block):
    return jnp.concatenate([block.astype(f32), turn(block)], axis=0)


def local_kernel(tokens_ref, stats_ref, kept_ref):
    tokens = tokens_ref[...]
    kept_ref[...] = tokens
    values = tokens.astype(f32)
    (mean,) = select_dot(group_of_channel(), jnp.sum(values, axis=0, keepdims=True))
    mean = mean / (CELLS * GROUP_WIDTH)
    (center,) = select_dot(channel_of_group(), mean)
    shifted = values - center
    (squares,) = select_dot(
        group_of_channel(), jnp.sum(shifted * shifted, axis=0, keepdims=True)
    )
    stats_ref[...] = stack_stats(mean, squares)


def sets_kernel(stats_ref, stale_ref, sets_ref):
    for j, block in enumerate(head_tiles(stale_ref[...])):
        sets_ref[j] = block


def x_kernel(place_ref, own_ref, other_ref, sets_ref, *out_refs):
    mean, squares = combine([own_ref[...], other_ref[...]], CELLS * GROUP_WIDTH)
    coded = split_rows(mean, squares)
    place = x_place(place_ref)
    for k, out_ref in enumerate(out_refs):
        out_ref[0:SET_ROWS, :] = sets_ref[lax.rem(place + k, 4)]
        out_ref[SET_ROWS:, :] = coded


def affine_kernel(gain_ref, bias_ref, out_ref):
    out_ref[0:1, :] = gain_ref[...].reshape(1, WIDTH)
    out_ref[1:2, :] = bias_ref[...].reshape(1, WIDTH)


def z_kernel(*refs):
    *in_refs, out_ref = refs
    stats = [decode(ref[SET_ROWS:, :]) for ref in in_refs]
    mean, squares = combine(stats, 2 * CELLS * GROUP_WIDTH)
    for k, ref in enumerate(in_refs):
        for h in range(SET_HEADS):
            low = h * 4 * ROWS + k * ROWS
            out_ref[low : low + ROWS, :] = ref[h * ROWS : (h + 1) * ROWS, :]
    out_ref[4 * SET_ROWS :, :] = split_rows(mean, squares)


def stats_kernel(*refs):
    *in_refs, stats_ref = refs
    stats = [decode(ref[4 * SET_ROWS :, :]) for ref in in_refs]
    mean, squares = combine(stats, 8 * CELLS * GROUP_WIDTH)
    stats_ref[...] = stack_stats(mean, squares)


def all_stats_kernel(s0, s1, s2, s3, stats_ref):
    mean, squares = combine([s0[...], s1[...], s2[...], s3[...]], 32 * CELLS * GROUP_WIDTH)
    stats_ref[...] = stack_stats(mean, squares)


def piece_kernel(stats_ref, *refs):
    *in_refs, out_ref = refs
    for k, ref in enumerate(in_refs):
        for h in range(SET_HEADS):
            low = h * CELLS + k * 4 * ROWS
            out_ref[low : low + 4 * ROWS, :] = ref[h * 4 * ROWS : (h + 1) * 4 * ROWS, :]


def load_kernel(source_hbm, target_ref, arrived):
    copy = pltpu.make_async_copy(source_hbm, target_ref, arrived)
    copy.start()
    copy.wait()


def project_kernel(
    place_ref, tokens_ref, own_ref, other_ref, affine_ref, query_ref, pair_ref, *refs
):
    *message_refs, fresh_ref, sets_ref, last_ref = refs
    stats = jnp.where(lax.bitwise_and(place_ref[0], 1) == 1, own_ref[...], other_ref[...])
    mean, squares = stats[0:1], stats[1:2]
    spread = squares / (128 * CELLS * GROUP_WIDTH)
    center, inverse = select_dot(channel_of_group(), mean, lax.rsqrt(spread + epsilon))
    scaled = (tokens_ref[...].astype(f32) - center) * inverse
    normed = (scaled * affine_ref[0:1] + affine_ref[1:2]).astype(bf16)

    square = iota((ROWS, CELLS), 0)
    cell = iota((ROWS, CELLS), 1)
    cell_square = lax.shift_right_logical(lax.bitwise_and(cell, 63), 2)
    pool = jnp.where(cell_square == square, 1.0 / (POOL * POOL), 0.0).astype(bf16)
    pooled = jnp.dot(pool, normed, preferred_element_type=f32).astype(bf16)

    place = x_place(place_ref)
    last = jnp.dot(normed, query_ref[:, 1024:], preferred_element_type=f32).astype(bf16)
    last_ref[0] = last[:, 0:LANES]
    last_ref[1] = last[:, LANES:]
    lane_half = lax.shift_right_logical(iota((CELLS // 2, LANES), 1), 6)
    for k in (2, 1, 3, 0):
        j = lax.rem(place + k, 4)
        columns = pl.ds(pl.multiple_of(j * 256, 256), 256)
        block = jnp.dot(normed, query_ref[:, columns], preferred_element_type=f32).astype(bf16)
        message_refs[k][0:CELLS, :] = block[:, 0:LANES]
        message_refs[k][CELLS : 2 * CELLS, :] = block[:, LANES:]
        mask = lane_half == lax.bitwise_and(j, 1)
        message_refs[k][2 * CELLS : ANSWER_ROWS, :] = fold(
            last_ref[lax.shift_right_logical(j, 1)], mask
        )

    fresh = jnp.dot(pooled, pair_ref[...], preferred_element_type=f32).astype(bf16)
    fresh_ref[...] = fresh
    for j, block in enumerate(head_tiles(fresh)):
        sets_ref[j] = block
    for k in range(4):
        message_refs[k][ANSWER_ROWS:, :] = sets_ref[lax.rem(place + k, 4)]


def attend_kernel(sources, place_ref, *refs):
    count = len(sources)
    message_refs, table_refs = refs[:count], refs[count : count + 8]
    out_refs, first_refs = refs[count + 8 : 2 * count + 8], refs[2 * count + 8 :]
    for source, message_ref, first_ref in zip(sources, message_refs, first_refs):
        first_ref[...] = table_refs[0][...]
        for h in range(SET_HEADS):
            low = h * CELLS + source * ROWS
            fresh = message_ref[ANSWER_ROWS + h * ROWS : ANSWER_ROWS + (h + 1) * ROWS, :]
            first_ref[low : low + ROWS, :] = fresh
    lane = iota((CELLS, LANES), 1)
    low_half = lane < HEAD_DIM
    parity = lax.bitwise_and(x_place(place_ref), 1)
    factor = HEAD_DIM ** (-0.5) * 1.4426950408889634
    against = (((1,), (1,)), ((), ()))
    ones = jnp.ones((CELLS, LANES), bf16)

    def head_scores(h):
        if h < 4:
            mask = low_half if h % 2 == 0 else jnp.logical_not(low_half)
        else:
            mask = lax.shift_right_logical(lane, 6) == parity
        groups = []
        for message_ref in message_refs:
            if h < 4:
                queries = message_ref[(h // 2) * CELLS : (h // 2 + 1) * CELLS, :].astype(f32)
            else:
                queries = unfold(message_ref[2 * CELLS : ANSWER_ROWS, :])
            groups.append(jnp.where(mask, queries, 0.0).astype(bf16))
        queries = jnp.concatenate(groups, axis=0) if count > 1 else groups[0]
        head = slice(h * CELLS, (h + 1) * CELLS)
        firsts = [
            lax.dot_general(group, ref[head, :], against, preferred_element_type=f32)
            for group, ref in zip(groups, first_refs)
        ]
        scores = [jnp.concatenate(firsts, axis=0)]
        for ref in table_refs[1:]:
            keys = ref[head, :]
            scores.append(lax.dot_general(queries, keys, against, preferred_element_type=f32))
        return scores

    def head_result(h, scores):
        head = slice(h * CELLS, (h + 1) * CELLS)
        largest = scores[0]
        for part in scores[1:]:
            largest = jnp.maximum(largest, part)
        largest = jnp.max(largest, axis=1, keepdims=True)
        summed = None
        for index, part in enumerate(scores):
            weights = jnp.exp2((part - largest) * factor).astype(bf16)
            if index == 0:
                products = []
                for g, ref in enumerate(first_refs):
                    values = jnp.concatenate([ref[head, :], ones], axis=1)
                    rows = weights[g * CELLS : (g + 1) * CELLS]
                    products.append(jnp.dot(rows, values, preferred_element_type=f32))
                summed = jnp.concatenate(products, axis=0)
            else:
                values = jnp.concatenate([table_refs[index][head, :], ones], axis=1)
                summed = summed + jnp.dot(weights, values, preferred_element_type=f32)
        return summed[:, 0:LANES] / summed[:, LANES:]

    results = []
    scores = head_scores(0)
    for h in range(SET_HEADS):
        following = head_scores(h + 1) if h + 1 < SET_HEADS else None
        results.append(head_result(h, scores))
        scores = following
    for g, out_ref in enumerate(out_refs):
        rows = slice(g * CELLS, (g + 1) * CELLS)
        for t in range(2):
            both = jnp.where(low_half, results[2 * t + 1][rows], results[2 * t][rows])
            out_ref[t * CELLS : (t + 1) * CELLS, :] = turn(both).astype(bf16)
        half = lax.shift_right_logical(iota((CELLS // 2, LANES), 1), 6)
        out_ref[2 * CELLS :, :] = fold(turn(results[4][rows]), half == parity)


def assemble_kernel(place_ref, *refs):
    *in_refs, out_ref, sets_ref = refs
    place = x_place(place_ref)
    for k, ref in enumerate(in_refs):
        sets_ref[lax.rem(place + k, 4)] = ref[...]
    for j in range(4):
        for t in range(2):
            low = (2 * j + t) * LANES
            out_ref[:, low : low + LANES] = sets_ref[j, t * CELLS : (t + 1) * CELLS, :]
    low_half = iota((CELLS, LANES), 1) < HEAD_DIM
    for t in range(2):
        low = (8 + t) * LANES
        both = [unfold(sets_ref[2 * t + i, 2 * CELLS :, :]) for i in range(2)]
        out_ref[:, low : low + LANES] = jnp.where(low_half, *both).astype(bf16)


def call(kernel, ins, outs, *args, scratch=(), limit=24):
    return pl.pallas_call(
        kernel,
        in_specs=ins,
        out_specs=[VMEM] * len(outs),
        out_shape=[jax.ShapeDtypeStruct(shape, kind) for shape, kind in outs],
        scratch_shapes=list(scratch),
        compiler_params=pltpu.CompilerParams(vmem_limit_bytes=limit * 1024 * 1024),
        cost_estimate=pl.CostEstimate(flops=1, bytes_accessed=1, transcendentals=0),
    )(*args)


AXES = {"z": (32, 4), "y": (8, 4), "x": (2, 4), "core": (1, 2)}


def shift(array, axis, step, cores=(0, 1)):
    stride, size = AXES[axis]
    pairs = []
    for source in range(128):
        place = source // stride % size
        if source % 2 in cores:
            pairs.append((source, source + ((place + step) % size - place) * stride))
    return lax.ppermute(array, "patch", pairs)


def after(array, *others):
    return lax.optimization_barrier((array, *others))[0]


def per_device(tokens, stale_keys, norm_gain, norm_bias, query_weight, pair_weight):
    place = lax.axis_index("patch").astype(jnp.int32).reshape(1)
    table = ((SET_HEADS * CELLS, LANES), bf16)
    answer = ((ANSWER_ROWS, LANES), bf16)
    stats, tokens = call(
        local_kernel,
        [VMEM],
        [((8, LANES), f32), ((CELLS, WIDTH), bf16)],
        tokens[0],
    )
    (sets,) = call(
        sets_kernel, [VMEM, VMEM], [((4, SET_ROWS, LANES), bf16)], stats, stale_keys[0]
    )
    other = shift(stats, "core", 1)
    messages = call(
        x_kernel,
        [SMEM, VMEM, VMEM, VMEM],
        [((SET_ROWS + ROWS, LANES), bf16)] * 4,
        place,
        stats,
        other,
        sets,
    )
    received = [messages[0]] + [shift(messages[k], "x", k) for k in (1, 2, 3)]
    norm_gain, norm_bias, _ = lax.optimization_barrier((norm_gain, norm_bias, messages[0]))
    (affine,) = call(affine_kernel, [VMEM] * 2, [((2, WIDTH), f32)], norm_gain, norm_bias)
    received, affine = lax.optimization_barrier((received, affine))
    (part,) = call(z_kernel, [VMEM] * 4, [((4 * SET_ROWS + ROWS, LANES), bf16)], *received)
    parts = [part] + [shift(part, "z", k) for k in (2, 3, 1)]
    weights = [part]
    for weight, limit in ((query_weight, 49), (pair_weight, 43)):
        weight = after(weight, weights[0])
        loaded = call(
            load_kernel,
            [HBM],
            [(weight.shape, bf16)],
            weight,
            scratch=[pltpu.SemaphoreType.DMA],
            limit=limit,
        )
        weights = [*loaded, *weights]
    weights = weights[1::-1]
    parts, weights = lax.optimization_barrier((parts, weights))
    (stats,) = call(stats_kernel, [VMEM] * 4, [((8, LANES), f32)], *parts)
    y_stats = [stats] + [shift(stats, "y", k, cores=(1,)) for k in (1, 2, 3)]
    (piece,) = call(piece_kernel, [VMEM] * 5, [table], stats, *parts)
    (stats,) = call(all_stats_kernel, [VMEM] * 4, [((8, LANES), f32)], *y_stats)
    late = after(piece, stats)
    pieces = [piece] + [shift(late, "y", k) for k in (1, 3, 2)]
    both_stats = [stats, shift(stats, "core", 1)]
    *queries, fresh = call(
        project_kernel,
        [SMEM] + [VMEM] * 6,
        [((ANSWER_ROWS + SET_ROWS, LANES), bf16)] * 4 + [((ROWS, 2 * WIDTH), bf16)],
        place,
        tokens,
        *both_stats,
        affine,
        *weights,
        scratch=[
            pltpu.VMEM((4, SET_ROWS, LANES), bf16),
            pltpu.VMEM((2, CELLS, LANES), bf16),
        ],
    )
    asked = {0: queries[0]}
    for k in (1, 2, 3):
        asked[k] = shift(after(queries[k], pieces[1]) if k == 3 else queries[k], "x", k)
    tables = pieces + [shift(after(block, asked[1]), "core", 1) for block in pieces]
    results = [None] * 4
    for sources in ((2, 1), (3,), (0,)):
        answers = call(
            functools.partial(attend_kernel, sources),
            [SMEM] + [VMEM] * (len(sources) + 8),
            [answer] * len(sources),
            place,
            *[asked[k] for k in sources],
            *tables,
            scratch=[pltpu.VMEM(*table)] * len(sources),
            limit=40,
        )
        for k, block in zip(sources, answers):
            results[k] = shift(block, "x", -k) if k else block
    (attended,) = call(
        assemble_kernel,
        [SMEM] + [VMEM] * 4,
        [((CELLS, WIDTH), bf16)],
        place,
        *results,
        scratch=[pltpu.VMEM((4, ANSWER_ROWS, LANES), bf16)],
    )
    return (attended[None], fresh[None])


def solution(mesh):
    return jax.shard_map(
        per_device,
        mesh=mesh,
        in_specs=(P("cfg", "patch", None), P("cfg", "patch", None), P(), P(), P(), P()),
        out_specs=(P("cfg", "patch", None), P("cfg", "patch", None)),
        check_vma=False,
    )
```

```python
import functools

import jax
import jax.numpy as jnp
from jax import lax
from jax.experimental import pallas as pl
from jax.experimental.pallas import tpu as pltpu
from jax.sharding import PartitionSpec as P

HEADS = 20
HEAD_DIM = 64
GROUPS = 32
POOL = 4
WIDTH = 1280
CELLS = 256
ROWS = 16
GROUP_WIDTH = WIDTH // GROUPS
LANES = 128
SET_HEADS = 5
SET_ROWS = SET_HEADS * ROWS
ANSWER_ROWS = SET_HEADS * CELLS // 2
epsilon = 1e-05
X_ORDER = (0, 1, 3, 2)

f32 = jnp.float32
bf16 = jnp.bfloat16
VMEM = pl.BlockSpec(memory_space=pltpu.VMEM)
SMEM = pl.BlockSpec(memory_space=pltpu.SMEM)
HBM = pl.BlockSpec(memory_space=pltpu.HBM)


def iota(shape, axis):
    return lax.broadcasted_iota(jnp.int32, shape, axis)


def group_of_channel():
    low = iota((WIDTH, LANES), 1) * GROUP_WIDTH
    channel = iota((WIDTH, LANES), 0)
    return ((channel >= low) & (channel < low + GROUP_WIDTH)).astype(f32).astype(bf16)


def channel_of_group():
    low = iota((LANES, WIDTH), 0) * GROUP_WIDTH
    channel = iota((LANES, WIDTH), 1)
    return ((channel >= low) & (channel < low + GROUP_WIDTH)).astype(f32).astype(bf16)


def split_rows(*rows):
    width = rows[0].shape[1]
    row = iota((ROWS, width), 0)
    split = jnp.zeros((ROWS, width), f32)
    for i, rest in enumerate(rows):
        for part in range(3):
            rounded = rest.astype(bf16).astype(f32)
            split = jnp.where(row == 3 * i + part, rounded, split)
            rest = rest - rounded
    return split.astype(bf16)


def join_rows(split, i):
    parts = split[3 * i : 3 * i + 3].astype(f32)
    return parts[0:1] + parts[1:2] + parts[2:3]


def select_dot(matrix, *rows):
    products = jnp.dot(split_rows(*rows), matrix, preferred_element_type=f32)
    return [join_rows(products, i) for i in range(len(rows))]


def combine(parts, entries):
    mean = sum(part[0:1] for part in parts) / len(parts)
    squares = sum(part[1:2] for part in parts)
    apart = sum((part[0:1] - mean) * (part[0:1] - mean) for part in parts)
    return mean, squares + entries * apart


def stack_stats(mean, squares):
    row = iota((8, LANES), 0)
    return jnp.where(row == 0, mean, jnp.where(row == 1, squares, 0.0))


def decode(rows):
    split = rows.astype(f32)
    return jnp.concatenate([join_rows(split, 0), join_rows(split, 1)], axis=0)


def head_tiles(pairs):
    lane = iota((ROWS, LANES), 1)
    even, odd = [], []
    for t in range(WIDTH // LANES):
        keys = pairs[:, t * LANES : (t + 1) * LANES].astype(f32)
        values = pairs[:, WIDTH + t * LANES : WIDTH + (t + 1) * LANES].astype(f32)
        turned = pltpu.roll(values, HEAD_DIM, 1)
        even.append(jnp.where(lane < HEAD_DIM, keys, turned).astype(bf16))
        odd.append(jnp.where(lane < HEAD_DIM, turned, keys).astype(bf16))
    sets = []
    for j in range(4):
        last = (even if j % 2 == 0 else odd)[8 + j // 2]
        sets.append(
            jnp.concatenate(
                [even[2 * j], odd[2 * j], even[2 * j + 1], odd[2 * j + 1], last], axis=0
            )
        )
    return sets


def turn(block):
    return pltpu.roll(block.astype(f32), HEAD_DIM, 1)


def fold(block, mask):
    half = CELLS // 2
    return jnp.where(mask, block[0:half].astype(f32), turn(block[half:])).astype(bf16)


def unfold(block):
    return jnp.concatenate([block.astype(f32), turn(block)], axis=0)


def local_kernel(tokens_ref, stats_ref, kept_ref):
    tokens = tokens_ref[...]
    kept_ref[...] = tokens
    values = tokens.astype(f32)
    (mean,) = select_dot(group_of_channel(), jnp.sum(values, axis=0, keepdims=True))
    mean = mean / (CELLS * GROUP_WIDTH)
    (center,) = select_dot(channel_of_group(), mean)
    shifted = values - center
    (squares,) = select_dot(
        group_of_channel(), jnp.sum(shifted * shifted, axis=0, keepdims=True)
    )
    stats_ref[...] = stack_stats(mean, squares)


def sets_kernel(stats_ref, stale_ref, sets_ref):
    for j, block in enumerate(head_tiles(stale_ref[...])):
        sets_ref[j] = block


def x_kernel(place_ref, own_ref, other_ref, sets_ref, *out_refs):
    mean, squares = combine([own_ref[...], other_ref[...]], CELLS * GROUP_WIDTH)
    coded = split_rows(mean, squares)
    place = place_ref[0]
    for k, out_ref in enumerate(out_refs):
        out_ref[0:SET_ROWS, :] = sets_ref[lax.rem(place + k, 4)]
        out_ref[SET_ROWS:, :] = coded


def affine_kernel(gain_ref, bias_ref, out_ref):
    out_ref[0:1, :] = gain_ref[...].reshape(1, WIDTH)
    out_ref[1:2, :] = bias_ref[...].reshape(1, WIDTH)


def z_kernel(*refs):
    *in_refs, out_ref = refs
    stats = [decode(ref[SET_ROWS:, :]) for ref in in_refs]
    mean, squares = combine(stats, 2 * CELLS * GROUP_WIDTH)
    for k, ref in zip(X_ORDER, in_refs):
        for h in range(SET_HEADS):
            low = h * 4 * ROWS + k * ROWS
            out_ref[low : low + ROWS, :] = ref[h * ROWS : (h + 1) * ROWS, :]
    out_ref[4 * SET_ROWS :, :] = split_rows(mean, squares)


def stats_kernel(*refs):
    *in_refs, stats_ref = refs
    stats = [decode(ref[4 * SET_ROWS :, :]) for ref in in_refs]
    mean, squares = combine(stats, 8 * CELLS * GROUP_WIDTH)
    stats_ref[...] = stack_stats(mean, squares)


def piece_kernel(stats_ref, *refs):
    *in_refs, out_ref = refs
    for k, ref in enumerate(in_refs):
        for h in range(SET_HEADS):
            low = h * CELLS + k * 4 * ROWS
            out_ref[low : low + 4 * ROWS, :] = ref[h * 4 * ROWS : (h + 1) * 4 * ROWS, :]


def load_kernel(source_hbm, target_ref, arrived):
    copy = pltpu.make_async_copy(source_hbm, target_ref, arrived)
    copy.start()
    copy.wait()


def project_kernel(
    place_ref, tokens_ref, s0, s1, s2, s3, affine_ref, query_ref, pair_ref, *refs
):
    *message_refs, fresh_ref, sets_ref, last_ref = refs
    mean, squares = combine([s0[...], s1[...], s2[...], s3[...]], 32 * CELLS * GROUP_WIDTH)
    spread = squares / (128 * CELLS * GROUP_WIDTH)
    center, inverse = select_dot(channel_of_group(), mean, lax.rsqrt(spread + epsilon))
    scaled = (tokens_ref[...].astype(f32) - center) * inverse
    normed = (scaled * affine_ref[0:1] + affine_ref[1:2]).astype(bf16)

    square = iota((ROWS, CELLS), 0)
    cell = iota((ROWS, CELLS), 1)
    cell_square = lax.shift_right_logical(lax.bitwise_and(cell, 63), 2)
    pool = jnp.where(cell_square == square, 1.0 / (POOL * POOL), 0.0).astype(bf16)
    pooled = jnp.dot(pool, normed, preferred_element_type=f32).astype(bf16)

    place = place_ref[0]
    last = jnp.dot(normed, query_ref[:, 1024:], preferred_element_type=f32).astype(bf16)
    last_ref[0] = last[:, 0:LANES]
    last_ref[1] = last[:, LANES:]
    lane_half = lax.shift_right_logical(iota((CELLS // 2, LANES), 1), 6)
    for k in (2, 1, 3, 0):
        j = lax.rem(place + k, 4)
        columns = pl.ds(pl.multiple_of(j * 256, 256), 256)
        block = jnp.dot(normed, query_ref[:, columns], preferred_element_type=f32).astype(bf16)
        message_refs[k][0:CELLS, :] = block[:, 0:LANES]
        message_refs[k][CELLS : 2 * CELLS, :] = block[:, LANES:]
        mask = lane_half == lax.bitwise_and(j, 1)
        message_refs[k][2 * CELLS : ANSWER_ROWS, :] = fold(
            last_ref[lax.shift_right_logical(j, 1)], mask
        )

    fresh = jnp.dot(pooled, pair_ref[...], preferred_element_type=f32).astype(bf16)
    fresh_ref[...] = fresh
    for j, block in enumerate(head_tiles(fresh)):
        sets_ref[j] = block
    for k in range(4):
        message_refs[k][ANSWER_ROWS:, :] = sets_ref[lax.rem(place + k, 4)]


def attend_kernel(sources, place_ref, *refs):
    count = len(sources)
    message_refs, table_refs = refs[:count], refs[count : count + 8]
    out_refs, first_refs = refs[count + 8 : 2 * count + 8], refs[2 * count + 8 :]
    for source, message_ref, first_ref in zip(sources, message_refs, first_refs):
        first_ref[...] = table_refs[0][...]
        for h in range(SET_HEADS):
            low = h * CELLS + source * ROWS
            fresh = message_ref[ANSWER_ROWS + h * ROWS : ANSWER_ROWS + (h + 1) * ROWS, :]
            first_ref[low : low + ROWS, :] = fresh
    lane = iota((CELLS, LANES), 1)
    low_half = lane < HEAD_DIM
    parity = lax.bitwise_and(place_ref[0], 1)
    factor = HEAD_DIM ** (-0.5) * 1.4426950408889634
    against = (((1,), (1,)), ((), ()))
    ones = jnp.ones((CELLS, LANES), bf16)

    def head_scores(h):
        if h < 4:
            mask = low_half if h % 2 == 0 else jnp.logical_not(low_half)
        else:
            mask = lax.shift_right_logical(lane, 6) == parity
        groups = []
        for message_ref in message_refs:
            if h < 4:
                queries = message_ref[(h // 2) * CELLS : (h // 2 + 1) * CELLS, :].astype(f32)
            else:
                queries = unfold(message_ref[2 * CELLS : ANSWER_ROWS, :])
            groups.append(jnp.where(mask, queries, 0.0).astype(bf16))
        queries = jnp.concatenate(groups, axis=0) if count > 1 else groups[0]
        head = slice(h * CELLS, (h + 1) * CELLS)
        firsts = [
            lax.dot_general(group, ref[head, :], against, preferred_element_type=f32)
            for group, ref in zip(groups, first_refs)
        ]
        scores = [jnp.concatenate(firsts, axis=0)]
        for ref in table_refs[1:]:
            keys = ref[head, :]
            scores.append(lax.dot_general(queries, keys, against, preferred_element_type=f32))
        return scores

    def head_result(h, scores):
        head = slice(h * CELLS, (h + 1) * CELLS)
        largest = scores[0]
        for part in scores[1:]:
            largest = jnp.maximum(largest, part)
        largest = jnp.max(largest, axis=1, keepdims=True)
        summed = None
        for index, part in enumerate(scores):
            weights = jnp.exp2((part - largest) * factor).astype(bf16)
            if index == 0:
                products = []
                for g, ref in enumerate(first_refs):
                    values = jnp.concatenate([ref[head, :], ones], axis=1)
                    rows = weights[g * CELLS : (g + 1) * CELLS]
                    products.append(jnp.dot(rows, values, preferred_element_type=f32))
                summed = jnp.concatenate(products, axis=0)
            else:
                values = jnp.concatenate([table_refs[index][head, :], ones], axis=1)
                summed = summed + jnp.dot(weights, values, preferred_element_type=f32)
        return summed[:, 0:LANES] / summed[:, LANES:]

    results = []
    scores = head_scores(0)
    for h in range(SET_HEADS):
        following = head_scores(h + 1) if h + 1 < SET_HEADS else None
        results.append(head_result(h, scores))
        scores = following
    for g, out_ref in enumerate(out_refs):
        rows = slice(g * CELLS, (g + 1) * CELLS)
        for t in range(2):
            both = jnp.where(low_half, results[2 * t + 1][rows], results[2 * t][rows])
            out_ref[t * CELLS : (t + 1) * CELLS, :] = turn(both).astype(bf16)
        half = lax.shift_right_logical(iota((CELLS // 2, LANES), 1), 6)
        out_ref[2 * CELLS :, :] = fold(turn(results[4][rows]), half == parity)


def assemble_kernel(place_ref, *refs):
    *in_refs, out_ref, sets_ref = refs
    place = place_ref[0]
    for k, ref in enumerate(in_refs):
        sets_ref[lax.rem(place + k, 4)] = ref[...]
    for j in range(4):
        for t in range(2):
            low = (2 * j + t) * LANES
            out_ref[:, low : low + LANES] = sets_ref[j, t * CELLS : (t + 1) * CELLS, :]
    low_half = iota((CELLS, LANES), 1) < HEAD_DIM
    for t in range(2):
        low = (8 + t) * LANES
        both = [unfold(sets_ref[2 * t + i, 2 * CELLS :, :]) for i in range(2)]
        out_ref[:, low : low + LANES] = jnp.where(low_half, *both).astype(bf16)


def call(kernel, ins, outs, *args, scratch=(), limit=24):
    return pl.pallas_call(
        kernel,
        in_specs=ins,
        out_specs=[VMEM] * len(outs),
        out_shape=[jax.ShapeDtypeStruct(shape, kind) for shape, kind in outs],
        scratch_shapes=list(scratch),
        compiler_params=pltpu.CompilerParams(vmem_limit_bytes=limit * 1024 * 1024),
        cost_estimate=pl.CostEstimate(flops=1, bytes_accessed=1, transcendentals=0),
    )(*args)


def permute(array, place):
    pairs = []
    for source in range(128):
        z, y, x, core = place(source // 32, source // 8 % 4, source // 2 % 4, source % 2)
        pairs.append((source, z % 4 * 32 + y % 4 * 8 + x % 4 * 2 + core % 2))
    return lax.ppermute(array, "patch", pairs)


def shift(array, axis, step):
    def place(*places):
        return [at + step * (name == axis) for at, name in zip(places, ("z", "y", "x", "core"))]

    return permute(array, place)


def after(array, *others):
    return lax.optimization_barrier((array, *others))[0]


def per_device(tokens, stale_keys, norm_gain, norm_bias, query_weight, pair_weight):
    place = (lax.axis_index("patch") // 2 % 4).astype(jnp.int32).reshape(1)
    table = ((SET_HEADS * CELLS, LANES), bf16)
    answer = ((ANSWER_ROWS, LANES), bf16)
    stats, tokens = call(
        local_kernel,
        [VMEM],
        [((8, LANES), f32), ((CELLS, WIDTH), bf16)],
        tokens[0],
    )
    (sets,) = call(
        sets_kernel, [VMEM, VMEM], [((4, SET_ROWS, LANES), bf16)], stats, stale_keys[0]
    )
    other = shift(stats, "core", 1)
    messages = call(
        x_kernel,
        [SMEM, VMEM, VMEM, VMEM],
        [((SET_ROWS + ROWS, LANES), bf16)] * 4,
        place,
        stats,
        other,
        sets,
    )
    received = [messages[0]] + [shift(messages[k], "x", k) for k in X_ORDER[1:]]
    norm_gain, norm_bias, _ = lax.optimization_barrier((norm_gain, norm_bias, messages[0]))
    (affine,) = call(affine_kernel, [VMEM] * 2, [((2, WIDTH), f32)], norm_gain, norm_bias)
    received, affine = lax.optimization_barrier((received, affine))
    (part,) = call(z_kernel, [VMEM] * 4, [((4 * SET_ROWS + ROWS, LANES), bf16)], *received)
    parts = [part] + [shift(part, "z", k) for k in (2, 3, 1)]
    weights = [part]
    for weight, limit in ((query_weight, 49), (pair_weight, 43)):
        weight = after(weight, weights[0])
        loaded = call(
            load_kernel,
            [HBM],
            [(weight.shape, bf16)],
            weight,
            scratch=[pltpu.SemaphoreType.DMA],
            limit=limit,
        )
        weights = [*loaded, *weights]
    weights = weights[1::-1]
    parts, weights = lax.optimization_barrier((parts, weights))
    (stats,) = call(stats_kernel, [VMEM] * 4, [((8, LANES), f32)], *parts)
    all_stats = [stats] + [shift(stats, "y", k) for k in (2, 3, 1)]
    (piece,) = call(piece_kernel, [VMEM] * 5, [table], stats, *parts)
    pieces = [piece, shift(piece, "y", 1), shift(piece, "y", 3)]
    pieces.append(shift(after(piece, *all_stats), "y", 2))
    *queries, fresh = call(
        project_kernel,
        [SMEM] + [VMEM] * 8,
        [((ANSWER_ROWS + SET_ROWS, LANES), bf16)] * 4 + [((ROWS, 2 * WIDTH), bf16)],
        place,
        tokens,
        *all_stats,
        affine,
        *weights,
        scratch=[
            pltpu.VMEM((4, SET_ROWS, LANES), bf16),
            pltpu.VMEM((2, CELLS, LANES), bf16),
        ],
    )
    asked = {0: queries[0]}
    for k in (1, 2, 3):
        asked[k] = shift(after(queries[k], pieces[1]) if k == 3 else queries[k], "x", k)
    tables = pieces + [shift(after(block, asked[1]), "core", 1) for block in pieces]
    results = [None] * 4
    for sources in ((2, 1), (3,), (0,)):
        answers = call(
            functools.partial(attend_kernel, sources),
            [SMEM] + [VMEM] * (len(sources) + 8),
            [answer] * len(sources),
            place,
            *[asked[k] for k in sources],
            *tables,
            scratch=[pltpu.VMEM(*table)] * len(sources),
            limit=40,
        )
        for k, block in zip(sources, answers):
            results[k] = shift(block, "x", -k) if k else block
    (attended,) = call(
        assemble_kernel,
        [SMEM] + [VMEM] * 4,
        [((CELLS, WIDTH), bf16)],
        place,
        *results,
        scratch=[pltpu.VMEM((4, ANSWER_ROWS, LANES), bf16)],
    )
    return (attended[None], fresh[None])


def solution(mesh):
    return jax.shard_map(
        per_device,
        mesh=mesh,
        in_specs=(P("cfg", "patch", None), P("cfg", "patch", None), P(), P(), P(), P()),
        out_specs=(P("cfg", "patch", None), P("cfg", "patch", None)),
        check_vma=False,
    )
```

```python
import functools

import jax
import jax.numpy as jnp
from jax import lax
from jax.experimental import pallas as pl
from jax.experimental.pallas import tpu as pltpu
from jax.sharding import PartitionSpec as P

HEADS = 20
HEAD_DIM = 64
GROUPS = 32
POOL = 4
WIDTH = 1280
CELLS = 256
ROWS = 16
GROUP_WIDTH = WIDTH // GROUPS
LANES = 128
SET_HEADS = 5
SET_ROWS = SET_HEADS * ROWS
ANSWER_ROWS = SET_HEADS * CELLS // 2
epsilon = 1e-05
X_ORDER = (0, 2, 1, 3)

f32 = jnp.float32
bf16 = jnp.bfloat16
VMEM = pl.BlockSpec(memory_space=pltpu.VMEM)
SMEM = pl.BlockSpec(memory_space=pltpu.SMEM)
HBM = pl.BlockSpec(memory_space=pltpu.HBM)


def iota(shape, axis):
    return lax.broadcasted_iota(jnp.int32, shape, axis)


def group_of_channel():
    low = iota((WIDTH, LANES), 1) * GROUP_WIDTH
    channel = iota((WIDTH, LANES), 0)
    return ((channel >= low) & (channel < low + GROUP_WIDTH)).astype(f32).astype(bf16)


def channel_of_group():
    low = iota((LANES, WIDTH), 0) * GROUP_WIDTH
    channel = iota((LANES, WIDTH), 1)
    return ((channel >= low) & (channel < low + GROUP_WIDTH)).astype(f32).astype(bf16)


def split_rows(*rows):
    width = rows[0].shape[1]
    row = iota((ROWS, width), 0)
    split = jnp.zeros((ROWS, width), f32)
    for i, rest in enumerate(rows):
        for part in range(3):
            rounded = rest.astype(bf16).astype(f32)
            split = jnp.where(row == 3 * i + part, rounded, split)
            rest = rest - rounded
    return split.astype(bf16)


def join_rows(split, i):
    parts = split[3 * i : 3 * i + 3].astype(f32)
    return parts[0:1] + parts[1:2] + parts[2:3]


def select_dot(matrix, *rows):
    products = jnp.dot(split_rows(*rows), matrix, preferred_element_type=f32)
    return [join_rows(products, i) for i in range(len(rows))]


def combine(parts, entries):
    mean = sum(part[0:1] for part in parts) / len(parts)
    squares = sum(part[1:2] for part in parts)
    apart = sum((part[0:1] - mean) * (part[0:1] - mean) for part in parts)
    return mean, squares + entries * apart


def stack_stats(mean, squares):
    row = iota((8, LANES), 0)
    return jnp.where(row == 0, mean, jnp.where(row == 1, squares, 0.0))


def decode(rows):
    split = rows.astype(f32)
    return jnp.concatenate([join_rows(split, 0), join_rows(split, 1)], axis=0)


def head_tiles(pairs):
    lane = iota((ROWS, LANES), 1)
    even, odd = [], []
    for t in range(WIDTH // LANES):
        keys = pairs[:, t * LANES : (t + 1) * LANES].astype(f32)
        values = pairs[:, WIDTH + t * LANES : WIDTH + (t + 1) * LANES].astype(f32)
        turned = pltpu.roll(values, HEAD_DIM, 1)
        even.append(jnp.where(lane < HEAD_DIM, keys, turned).astype(bf16))
        odd.append(jnp.where(lane < HEAD_DIM, turned, keys).astype(bf16))
    sets = []
    for j in range(4):
        last = (even if j % 2 == 0 else odd)[8 + j // 2]
        sets.append(
            jnp.concatenate(
                [even[2 * j], odd[2 * j], even[2 * j + 1], odd[2 * j + 1], last], axis=0
            )
        )
    return sets


def turn(block):
    return pltpu.roll(block.astype(f32), HEAD_DIM, 1)


def fold(block, mask):
    half = CELLS // 2
    return jnp.where(mask, block[0:half].astype(f32), turn(block[half:])).astype(bf16)


def unfold(block):
    return jnp.concatenate([block.astype(f32), turn(block)], axis=0)


def local_kernel(tokens_ref, stats_ref, kept_ref):
    tokens = tokens_ref[...]
    kept_ref[...] = tokens
    values = tokens.astype(f32)
    (mean,) = select_dot(group_of_channel(), jnp.sum(values, axis=0, keepdims=True))
    mean = mean / (CELLS * GROUP_WIDTH)
    (center,) = select_dot(channel_of_group(), mean)
    shifted = values - center
    (squares,) = select_dot(
        group_of_channel(), jnp.sum(shifted * shifted, axis=0, keepdims=True)
    )
    stats_ref[...] = stack_stats(mean, squares)


def sets_kernel(stats_ref, stale_ref, sets_ref):
    for j, block in enumerate(head_tiles(stale_ref[...])):
        sets_ref[j] = block


def x_kernel(place_ref, own_ref, other_ref, sets_ref, *out_refs):
    mean, squares = combine([own_ref[...], other_ref[...]], CELLS * GROUP_WIDTH)
    coded = split_rows(mean, squares)
    place = place_ref[0]
    for k, out_ref in enumerate(out_refs):
        out_ref[0:SET_ROWS, :] = sets_ref[lax.rem(place + k, 4)]
        out_ref[SET_ROWS:, :] = coded


def affine_kernel(gain_ref, bias_ref, out_ref):
    out_ref[0:1, :] = gain_ref[...].reshape(1, WIDTH)
    out_ref[1:2, :] = bias_ref[...].reshape(1, WIDTH)


def z_kernel(*refs):
    *in_refs, out_ref = refs
    stats = [decode(ref[SET_ROWS:, :]) for ref in in_refs]
    mean, squares = combine(stats, 2 * CELLS * GROUP_WIDTH)
    for k, ref in zip(X_ORDER, in_refs):
        for h in range(SET_HEADS):
            low = h * 4 * ROWS + k * ROWS
            out_ref[low : low + ROWS, :] = ref[h * ROWS : (h + 1) * ROWS, :]
    out_ref[4 * SET_ROWS :, :] = split_rows(mean, squares)


def stats_kernel(*refs):
    *in_refs, stats_ref = refs
    stats = [decode(ref[4 * SET_ROWS :, :]) for ref in in_refs]
    mean, squares = combine(stats, 8 * CELLS * GROUP_WIDTH)
    stats_ref[...] = stack_stats(mean, squares)


def piece_kernel(stats_ref, *refs):
    *in_refs, out_ref = refs
    for k, ref in enumerate(in_refs):
        for h in range(SET_HEADS):
            low = h * CELLS + k * 4 * ROWS
            out_ref[low : low + 4 * ROWS, :] = ref[h * 4 * ROWS : (h + 1) * 4 * ROWS, :]


def load_kernel(source_hbm, target_ref, arrived):
    copy = pltpu.make_async_copy(source_hbm, target_ref, arrived)
    copy.start()
    copy.wait()


def project_kernel(
    place_ref, tokens_ref, s0, s1, s2, s3, affine_ref, query_ref, pair_ref, *refs
):
    *message_refs, fresh_ref, sets_ref, last_ref = refs
    mean, squares = combine([s0[...], s1[...], s2[...], s3[...]], 32 * CELLS * GROUP_WIDTH)
    spread = squares / (128 * CELLS * GROUP_WIDTH)
    center, inverse = select_dot(channel_of_group(), mean, lax.rsqrt(spread + epsilon))
    scaled = (tokens_ref[...].astype(f32) - center) * inverse
    normed = (scaled * affine_ref[0:1] + affine_ref[1:2]).astype(bf16)

    square = iota((ROWS, CELLS), 0)
    cell = iota((ROWS, CELLS), 1)
    cell_square = lax.shift_right_logical(lax.bitwise_and(cell, 63), 2)
    pool = jnp.where(cell_square == square, 1.0 / (POOL * POOL), 0.0).astype(bf16)
    pooled = jnp.dot(pool, normed, preferred_element_type=f32).astype(bf16)

    place = place_ref[0]
    last = jnp.dot(normed, query_ref[:, 1024:], preferred_element_type=f32).astype(bf16)
    last_ref[0] = last[:, 0:LANES]
    last_ref[1] = last[:, LANES:]
    lane_half = lax.shift_right_logical(iota((CELLS // 2, LANES), 1), 6)
    for k in (2, 1, 3, 0):
        j = lax.rem(place + k, 4)
        columns = pl.ds(pl.multiple_of(j * 256, 256), 256)
        block = jnp.dot(normed, query_ref[:, columns], preferred_element_type=f32).astype(bf16)
        message_refs[k][0:CELLS, :] = block[:, 0:LANES]
        message_refs[k][CELLS : 2 * CELLS, :] = block[:, LANES:]
        mask = lane_half == lax.bitwise_and(j, 1)
        message_refs[k][2 * CELLS : ANSWER_ROWS, :] = fold(
            last_ref[lax.shift_right_logical(j, 1)], mask
        )

    fresh = jnp.dot(pooled, pair_ref[...], preferred_element_type=f32).astype(bf16)
    fresh_ref[...] = fresh
    for j, block in enumerate(head_tiles(fresh)):
        sets_ref[j] = block
    for k in range(4):
        message_refs[k][ANSWER_ROWS:, :] = sets_ref[lax.rem(place + k, 4)]


def attend_kernel(sources, place_ref, *refs):
    count = len(sources)
    message_refs, table_refs = refs[:count], refs[count : count + 8]
    out_refs, first_refs = refs[count + 8 : 2 * count + 8], refs[2 * count + 8 :]
    for source, message_ref, first_ref in zip(sources, message_refs, first_refs):
        first_ref[...] = table_refs[0][...]
        for h in range(SET_HEADS):
            low = h * CELLS + source * ROWS
            fresh = message_ref[ANSWER_ROWS + h * ROWS : ANSWER_ROWS + (h + 1) * ROWS, :]
            first_ref[low : low + ROWS, :] = fresh
    lane = iota((CELLS, LANES), 1)
    low_half = lane < HEAD_DIM
    parity = lax.bitwise_and(place_ref[0], 1)
    factor = HEAD_DIM ** (-0.5) * 1.4426950408889634
    against = (((1,), (1,)), ((), ()))
    ones = jnp.ones((CELLS, LANES), bf16)

    def head_scores(h):
        if h < 4:
            mask = low_half if h % 2 == 0 else jnp.logical_not(low_half)
        else:
            mask = lax.shift_right_logical(lane, 6) == parity
        groups = []
        for message_ref in message_refs:
            if h < 4:
                queries = message_ref[(h // 2) * CELLS : (h // 2 + 1) * CELLS, :].astype(f32)
            else:
                queries = unfold(message_ref[2 * CELLS : ANSWER_ROWS, :])
            groups.append(jnp.where(mask, queries, 0.0).astype(bf16))
        queries = jnp.concatenate(groups, axis=0) if count > 1 else groups[0]
        head = slice(h * CELLS, (h + 1) * CELLS)
        firsts = [
            lax.dot_general(group, ref[head, :], against, preferred_element_type=f32)
            for group, ref in zip(groups, first_refs)
        ]
        scores = [jnp.concatenate(firsts, axis=0)]
        for ref in table_refs[1:]:
            keys = ref[head, :]
            scores.append(lax.dot_general(queries, keys, against, preferred_element_type=f32))
        return scores

    def head_result(h, scores):
        head = slice(h * CELLS, (h + 1) * CELLS)
        largest = scores[0]
        for part in scores[1:]:
            largest = jnp.maximum(largest, part)
        largest = jnp.max(largest, axis=1, keepdims=True)
        summed = None
        for index, part in enumerate(scores):
            weights = jnp.exp2((part - largest) * factor).astype(bf16)
            if index == 0:
                products = []
                for g, ref in enumerate(first_refs):
                    values = jnp.concatenate([ref[head, :], ones], axis=1)
                    rows = weights[g * CELLS : (g + 1) * CELLS]
                    products.append(jnp.dot(rows, values, preferred_element_type=f32))
                summed = jnp.concatenate(products, axis=0)
            else:
                values = jnp.concatenate([table_refs[index][head, :], ones], axis=1)
                summed = summed + jnp.dot(weights, values, preferred_element_type=f32)
        return summed[:, 0:LANES] / summed[:, LANES:]

    results = []
    scores = head_scores(0)
    for h in range(SET_HEADS):
        following = head_scores(h + 1) if h + 1 < SET_HEADS else None
        results.append(head_result(h, scores))
        scores = following
    for g, out_ref in enumerate(out_refs):
        rows = slice(g * CELLS, (g + 1) * CELLS)
        for t in range(2):
            both = jnp.where(low_half, results[2 * t + 1][rows], results[2 * t][rows])
            out_ref[t * CELLS : (t + 1) * CELLS, :] = turn(both).astype(bf16)
        half = lax.shift_right_logical(iota((CELLS // 2, LANES), 1), 6)
        out_ref[2 * CELLS :, :] = fold(turn(results[4][rows]), half == parity)


def assemble_kernel(place_ref, *refs):
    *in_refs, out_ref, sets_ref = refs
    place = place_ref[0]
    for k, ref in enumerate(in_refs):
        sets_ref[lax.rem(place + k, 4)] = ref[...]
    for j in range(4):
        for t in range(2):
            low = (2 * j + t) * LANES
            out_ref[:, low : low + LANES] = sets_ref[j, t * CELLS : (t + 1) * CELLS, :]
    low_half = iota((CELLS, LANES), 1) < HEAD_DIM
    for t in range(2):
        low = (8 + t) * LANES
        both = [unfold(sets_ref[2 * t + i, 2 * CELLS :, :]) for i in range(2)]
        out_ref[:, low : low + LANES] = jnp.where(low_half, *both).astype(bf16)


def call(kernel, ins, outs, *args, scratch=(), limit=24):
    return pl.pallas_call(
        kernel,
        in_specs=ins,
        out_specs=[VMEM] * len(outs),
        out_shape=[jax.ShapeDtypeStruct(shape, kind) for shape, kind in outs],
        scratch_shapes=list(scratch),
        compiler_params=pltpu.CompilerParams(vmem_limit_bytes=limit * 1024 * 1024),
        cost_estimate=pl.CostEstimate(flops=1, bytes_accessed=1, transcendentals=0),
    )(*args)


def permute(array, place):
    pairs = []
    for source in range(128):
        z, y, x, core = place(source // 32, source // 8 % 4, source // 2 % 4, source % 2)
        pairs.append((source, z % 4 * 32 + y % 4 * 8 + x % 4 * 2 + core % 2))
    return lax.ppermute(array, "patch", pairs)


def shift(array, axis, step):
    def place(*places):
        return [at + step * (name == axis) for at, name in zip(places, ("z", "y", "x", "core"))]

    return permute(array, place)


def after(array, *others):
    return lax.optimization_barrier((array, *others))[0]


def per_device(tokens, stale_keys, norm_gain, norm_bias, query_weight, pair_weight):
    place = (lax.axis_index("patch") // 2 % 4).astype(jnp.int32).reshape(1)
    table = ((SET_HEADS * CELLS, LANES), bf16)
    answer = ((ANSWER_ROWS, LANES), bf16)
    stats, tokens = call(
        local_kernel,
        [VMEM],
        [((8, LANES), f32), ((CELLS, WIDTH), bf16)],
        tokens[0],
    )
    (sets,) = call(
        sets_kernel, [VMEM, VMEM], [((4, SET_ROWS, LANES), bf16)], stats, stale_keys[0]
    )
    other = shift(stats, "core", 1)
    messages = call(
        x_kernel,
        [SMEM, VMEM, VMEM, VMEM],
        [((SET_ROWS + ROWS, LANES), bf16)] * 4,
        place,
        stats,
        other,
        sets,
    )
    received = [messages[0]] + [shift(messages[k], "x", k) for k in X_ORDER[1:]]
    norm_gain, norm_bias, _ = lax.optimization_barrier((norm_gain, norm_bias, messages[0]))
    (affine,) = call(affine_kernel, [VMEM] * 2, [((2, WIDTH), f32)], norm_gain, norm_bias)
    received, affine = lax.optimization_barrier((received, affine))
    (part,) = call(z_kernel, [VMEM] * 4, [((4 * SET_ROWS + ROWS, LANES), bf16)], *received)
    parts = [part] + [shift(part, "z", k) for k in (2, 3, 1)]
    weights = [part]
    for weight, limit in ((query_weight, 49), (pair_weight, 43)):
        weight = after(weight, weights[0])
        loaded = call(
            load_kernel,
            [HBM],
            [(weight.shape, bf16)],
            weight,
            scratch=[pltpu.SemaphoreType.DMA],
            limit=limit,
        )
        weights = [*loaded, *weights]
    weights = weights[1::-1]
    parts, weights = lax.optimization_barrier((parts, weights))
    (stats,) = call(stats_kernel, [VMEM] * 4, [((8, LANES), f32)], *parts)
    all_stats = [stats] + [shift(stats, "y", k) for k in (1, 2, 3)]
    (piece,) = call(piece_kernel, [VMEM] * 5, [table], stats, *parts)
    pieces = [piece, shift(piece, "y", 1), shift(piece, "y", 3)]
    pieces.append(shift(after(piece, *all_stats), "y", 2))
    *queries, fresh = call(
        project_kernel,
        [SMEM] + [VMEM] * 8,
        [((ANSWER_ROWS + SET_ROWS, LANES), bf16)] * 4 + [((ROWS, 2 * WIDTH), bf16)],
        place,
        tokens,
        *all_stats,
        affine,
        *weights,
        scratch=[
            pltpu.VMEM((4, SET_ROWS, LANES), bf16),
            pltpu.VMEM((2, CELLS, LANES), bf16),
        ],
    )
    asked = {0: queries[0]}
    for k in (1, 2, 3):
        asked[k] = shift(after(queries[k], pieces[1]) if k == 3 else queries[k], "x", k)
    tables = pieces + [shift(after(block, asked[1]), "core", 1) for block in pieces]
    results = [None] * 4
    for sources in ((2, 1), (3,), (0,)):
        answers = call(
            functools.partial(attend_kernel, sources),
            [SMEM] + [VMEM] * (len(sources) + 8),
            [answer] * len(sources),
            place,
            *[asked[k] for k in sources],
            *tables,
            scratch=[pltpu.VMEM(*table)] * len(sources),
            limit=40,
        )
        for k, block in zip(sources, answers):
            results[k] = shift(block, "x", -k) if k else block
    (attended,) = call(
        assemble_kernel,
        [SMEM] + [VMEM] * 4,
        [((CELLS, WIDTH), bf16)],
        place,
        *results,
        scratch=[pltpu.VMEM((4, ANSWER_ROWS, LANES), bf16)],
    )
    return (attended[None], fresh[None])


def solution(mesh):
    return jax.shard_map(
        per_device,
        mesh=mesh,
        in_specs=(P("cfg", "patch", None), P("cfg", "patch", None), P(), P(), P(), P()),
        out_specs=(P("cfg", "patch", None), P("cfg", "patch", None)),
        check_vma=False,
    )
```

```python
import functools

import jax
import jax.numpy as jnp
from jax import lax
from jax.experimental import pallas as pl
from jax.experimental.pallas import tpu as pltpu
from jax.sharding import PartitionSpec as P

HEADS = 20
HEAD_DIM = 64
GROUPS = 32
POOL = 4
WIDTH = 1280
CELLS = 256
ROWS = 16
GROUP_WIDTH = WIDTH // GROUPS
LANES = 128
SET_HEADS = 5
SET_ROWS = SET_HEADS * ROWS
ANSWER_ROWS = SET_HEADS * CELLS // 2
epsilon = 1e-05

f32 = jnp.float32
bf16 = jnp.bfloat16
VMEM = pl.BlockSpec(memory_space=pltpu.VMEM)
SMEM = pl.BlockSpec(memory_space=pltpu.SMEM)
HBM = pl.BlockSpec(memory_space=pltpu.HBM)


def iota(shape, axis):
    return lax.broadcasted_iota(jnp.int32, shape, axis)


def group_of_channel():
    low = iota((WIDTH, LANES), 1) * GROUP_WIDTH
    channel = iota((WIDTH, LANES), 0)
    return ((channel >= low) & (channel < low + GROUP_WIDTH)).astype(f32).astype(bf16)


def channel_of_group():
    low = iota((LANES, WIDTH), 0) * GROUP_WIDTH
    channel = iota((LANES, WIDTH), 1)
    return ((channel >= low) & (channel < low + GROUP_WIDTH)).astype(f32).astype(bf16)


def split_rows(*rows):
    width = rows[0].shape[1]
    row = iota((ROWS, width), 0)
    split = jnp.zeros((ROWS, width), f32)
    for i, rest in enumerate(rows):
        for part in range(3):
            rounded = rest.astype(bf16).astype(f32)
            split = jnp.where(row == 3 * i + part, rounded, split)
            rest = rest - rounded
    return split.astype(bf16)


def join_rows(split, i):
    parts = split[3 * i : 3 * i + 3].astype(f32)
    return parts[0:1] + parts[1:2] + parts[2:3]


def select_dot(matrix, *rows):
    products = jnp.dot(split_rows(*rows), matrix, preferred_element_type=f32)
    return [join_rows(products, i) for i in range(len(rows))]


def combine(parts, entries):
    mean = sum(part[0:1] for part in parts) / len(parts)
    squares = sum(part[1:2] for part in parts)
    apart = sum((part[0:1] - mean) * (part[0:1] - mean) for part in parts)
    return mean, squares + entries * apart


def stack_stats(mean, squares):
    row = iota((8, LANES), 0)
    return jnp.where(row == 0, mean, jnp.where(row == 1, squares, 0.0))


def decode(rows):
    split = rows.astype(f32)
    return jnp.concatenate([join_rows(split, 0), join_rows(split, 1)], axis=0)


def head_tiles(pairs):
    lane = iota((ROWS, LANES), 1)
    even, odd = [], []
    for t in range(WIDTH // LANES):
        keys = pairs[:, t * LANES : (t + 1) * LANES].astype(f32)
        values = pairs[:, WIDTH + t * LANES : WIDTH + (t + 1) * LANES].astype(f32)
        turned = pltpu.roll(values, HEAD_DIM, 1)
        even.append(jnp.where(lane < HEAD_DIM, keys, turned).astype(bf16))
        odd.append(jnp.where(lane < HEAD_DIM, turned, keys).astype(bf16))
    sets = []
    for j in range(4):
        last = (even if j % 2 == 0 else odd)[8 + j // 2]
        sets.append(
            jnp.concatenate(
                [even[2 * j], odd[2 * j], even[2 * j + 1], odd[2 * j + 1], last], axis=0
            )
        )
    return sets


def turn(block):
    return pltpu.roll(block.astype(f32), HEAD_DIM, 1)


def fold(block, mask):
    half = CELLS // 2
    return jnp.where(mask, block[0:half].astype(f32), turn(block[half:])).astype(bf16)


def unfold(block):
    return jnp.concatenate([block.astype(f32), turn(block)], axis=0)


def local_kernel(tokens_ref, stats_ref, kept_ref):
    tokens = tokens_ref[...]
    kept_ref[...] = tokens
    values = tokens.astype(f32)
    (mean,) = select_dot(group_of_channel(), jnp.sum(values, axis=0, keepdims=True))
    mean = mean / (CELLS * GROUP_WIDTH)
    (center,) = select_dot(channel_of_group(), mean)
    shifted = values - center
    (squares,) = select_dot(
        group_of_channel(), jnp.sum(shifted * shifted, axis=0, keepdims=True)
    )
    stats_ref[...] = stack_stats(mean, squares)


def sets_kernel(stats_ref, stale_ref, sets_ref):
    for j, block in enumerate(head_tiles(stale_ref[...])):
        sets_ref[j] = block


def x_kernel(place_ref, own_ref, other_ref, sets_ref, *out_refs):
    mean, squares = combine([own_ref[...], other_ref[...]], CELLS * GROUP_WIDTH)
    coded = split_rows(mean, squares)
    place = place_ref[0]
    for k, out_ref in enumerate(out_refs):
        out_ref[0:SET_ROWS, :] = sets_ref[lax.rem(place + k, 4)]
        out_ref[SET_ROWS:, :] = coded


def affine_kernel(gain_ref, bias_ref, out_ref):
    out_ref[0:1, :] = gain_ref[...].reshape(1, WIDTH)
    out_ref[1:2, :] = bias_ref[...].reshape(1, WIDTH)


def z_kernel(*refs):
    *in_refs, out_ref = refs
    stats = [decode(ref[SET_ROWS:, :]) for ref in in_refs]
    mean, squares = combine(stats, 2 * CELLS * GROUP_WIDTH)
    for k, ref in enumerate(in_refs):
        for h in range(SET_HEADS):
            low = h * 4 * ROWS + k * ROWS
            out_ref[low : low + ROWS, :] = ref[h * ROWS : (h + 1) * ROWS, :]
    out_ref[4 * SET_ROWS :, :] = split_rows(mean, squares)


def stats_kernel(*refs):
    *in_refs, stats_ref = refs
    stats = [decode(ref[4 * SET_ROWS :, :]) for ref in in_refs]
    mean, squares = combine(stats, 8 * CELLS * GROUP_WIDTH)
    stats_ref[...] = stack_stats(mean, squares)


def piece_kernel(stats_ref, *refs):
    *in_refs, out_ref = refs
    for k, ref in enumerate(in_refs):
        for h in range(SET_HEADS):
            low = h * CELLS + k * 4 * ROWS
            out_ref[low : low + 4 * ROWS, :] = ref[h * 4 * ROWS : (h + 1) * 4 * ROWS, :]


def load_kernel(source_hbm, target_ref, arrived):
    copy = pltpu.make_async_copy(source_hbm, target_ref, arrived)
    copy.start()
    copy.wait()


def project_kernel(
    place_ref, tokens_ref, s0, s1, s2, s3, affine_ref, query_ref, pair_ref, *refs
):
    *message_refs, fresh_ref, sets_ref, last_ref = refs
    mean, squares = combine([s0[...], s1[...], s2[...], s3[...]], 32 * CELLS * GROUP_WIDTH)
    spread = squares / (128 * CELLS * GROUP_WIDTH)
    center, inverse = select_dot(channel_of_group(), mean, lax.rsqrt(spread + epsilon))
    scaled = (tokens_ref[...].astype(f32) - center) * inverse
    normed = (scaled * affine_ref[0:1] + affine_ref[1:2]).astype(bf16)

    square = iota((ROWS, CELLS), 0)
    cell = iota((ROWS, CELLS), 1)
    cell_square = lax.shift_right_logical(lax.bitwise_and(cell, 63), 2)
    pool = jnp.where(cell_square == square, 1.0 / (POOL * POOL), 0.0).astype(bf16)
    pooled = jnp.dot(pool, normed, preferred_element_type=f32).astype(bf16)

    place = place_ref[0]
    last = jnp.dot(normed, query_ref[:, 1024:], preferred_element_type=f32).astype(bf16)
    last_ref[0] = last[:, 0:LANES]
    last_ref[1] = last[:, LANES:]
    lane_half = lax.shift_right_logical(iota((CELLS // 2, LANES), 1), 6)
    for k in (2, 1, 3, 0):
        j = lax.rem(place + k, 4)
        columns = pl.ds(pl.multiple_of(j * 256, 256), 256)
        block = jnp.dot(normed, query_ref[:, columns], preferred_element_type=f32).astype(bf16)
        message_refs[k][0:CELLS, :] = block[:, 0:LANES]
        message_refs[k][CELLS : 2 * CELLS, :] = block[:, LANES:]
        mask = lane_half == lax.bitwise_and(j, 1)
        message_refs[k][2 * CELLS : ANSWER_ROWS, :] = fold(
            last_ref[lax.shift_right_logical(j, 1)], mask
        )

    fresh = jnp.dot(pooled, pair_ref[...], preferred_element_type=f32).astype(bf16)
    fresh_ref[...] = fresh
    for j, block in enumerate(head_tiles(fresh)):
        sets_ref[j] = block
    for k in range(4):
        message_refs[k][ANSWER_ROWS:, :] = sets_ref[lax.rem(place + k, 4)]


def attend_kernel(sources, place_ref, *refs):
    count = len(sources)
    message_refs, table_refs = refs[:count], refs[count : count + 8]
    out_refs, first_refs = refs[count + 8 : 2 * count + 8], refs[2 * count + 8 :]
    for source, message_ref, first_ref in zip(sources, message_refs, first_refs):
        first_ref[...] = table_refs[0][...]
        for h in range(SET_HEADS):
            low = h * CELLS + source * ROWS
            fresh = message_ref[ANSWER_ROWS + h * ROWS : ANSWER_ROWS + (h + 1) * ROWS, :]
            first_ref[low : low + ROWS, :] = fresh
    lane = iota((CELLS, LANES), 1)
    low_half = lane < HEAD_DIM
    parity = lax.bitwise_and(place_ref[0], 1)
    factor = HEAD_DIM ** (-0.5) * 1.4426950408889634
    against = (((1,), (1,)), ((), ()))
    ones = jnp.ones((CELLS, LANES), bf16)

    def head_scores(h):
        if h < 4:
            mask = low_half if h % 2 == 0 else jnp.logical_not(low_half)
        else:
            mask = lax.shift_right_logical(lane, 6) == parity
        groups = []
        for message_ref in message_refs:
            if h < 4:
                queries = message_ref[(h // 2) * CELLS : (h // 2 + 1) * CELLS, :].astype(f32)
            else:
                queries = unfold(message_ref[2 * CELLS : ANSWER_ROWS, :])
            groups.append(jnp.where(mask, queries, 0.0).astype(bf16))
        queries = jnp.concatenate(groups, axis=0) if count > 1 else groups[0]
        head = slice(h * CELLS, (h + 1) * CELLS)
        firsts = [
            lax.dot_general(group, ref[head, :], against, preferred_element_type=f32)
            for group, ref in zip(groups, first_refs)
        ]
        scores = [jnp.concatenate(firsts, axis=0)]
        for ref in table_refs[1:]:
            keys = ref[head, :]
            scores.append(lax.dot_general(queries, keys, against, preferred_element_type=f32))
        return scores

    def head_result(h, scores):
        head = slice(h * CELLS, (h + 1) * CELLS)
        largest = scores[0]
        for part in scores[1:]:
            largest = jnp.maximum(largest, part)
        largest = jnp.max(largest, axis=1, keepdims=True)
        summed = None
        for index, part in enumerate(scores):
            weights = jnp.exp2((part - largest) * factor).astype(bf16)
            if index == 0:
                products = []
                for g, ref in enumerate(first_refs):
                    values = jnp.concatenate([ref[head, :], ones], axis=1)
                    rows = weights[g * CELLS : (g + 1) * CELLS]
                    products.append(jnp.dot(rows, values, preferred_element_type=f32))
                summed = jnp.concatenate(products, axis=0)
            else:
                values = jnp.concatenate([table_refs[index][head, :], ones], axis=1)
                summed = summed + jnp.dot(weights, values, preferred_element_type=f32)
        return summed[:, 0:LANES] / summed[:, LANES:]

    results = []
    scores = head_scores(0)
    for h in range(SET_HEADS):
        following = head_scores(h + 1) if h + 1 < SET_HEADS else None
        results.append(head_result(h, scores))
        scores = following
    for g, out_ref in enumerate(out_refs):
        rows = slice(g * CELLS, (g + 1) * CELLS)
        for t in range(2):
            both = jnp.where(low_half, results[2 * t + 1][rows], results[2 * t][rows])
            out_ref[t * CELLS : (t + 1) * CELLS, :] = turn(both).astype(bf16)
        half = lax.shift_right_logical(iota((CELLS // 2, LANES), 1), 6)
        out_ref[2 * CELLS :, :] = fold(turn(results[4][rows]), half == parity)


def assemble_kernel(place_ref, *refs):
    *in_refs, out_ref, sets_ref = refs
    place = place_ref[0]
    for k, ref in enumerate(in_refs):
        sets_ref[lax.rem(place + k, 4)] = ref[...]
    for j in range(4):
        for t in range(2):
            low = (2 * j + t) * LANES
            out_ref[:, low : low + LANES] = sets_ref[j, t * CELLS : (t + 1) * CELLS, :]
    low_half = iota((CELLS, LANES), 1) < HEAD_DIM
    for t in range(2):
        low = (8 + t) * LANES
        both = [unfold(sets_ref[2 * t + i, 2 * CELLS :, :]) for i in range(2)]
        out_ref[:, low : low + LANES] = jnp.where(low_half, *both).astype(bf16)


def call(kernel, ins, outs, *args, scratch=(), limit=24):
    return pl.pallas_call(
        kernel,
        in_specs=ins,
        out_specs=[VMEM] * len(outs),
        out_shape=[jax.ShapeDtypeStruct(shape, kind) for shape, kind in outs],
        scratch_shapes=list(scratch),
        compiler_params=pltpu.CompilerParams(vmem_limit_bytes=limit * 1024 * 1024),
        cost_estimate=pl.CostEstimate(flops=1, bytes_accessed=1, transcendentals=0),
    )(*args)


def permute(array, place):
    pairs = []
    for source in range(128):
        z, y, x, core = place(source // 32, source // 8 % 4, source // 2 % 4, source % 2)
        pairs.append((source, z % 4 * 32 + y % 4 * 8 + x % 4 * 2 + core % 2))
    return lax.ppermute(array, "patch", pairs)


def shift(array, axis, step):
    def place(*places):
        return [at + step * (name == axis) for at, name in zip(places, ("z", "y", "x", "core"))]

    return permute(array, place)


def after(array, *others):
    return lax.optimization_barrier((array, *others))[0]


def load(weight, limit):
    return call(
        load_kernel,
        [HBM],
        [(weight.shape, bf16)],
        weight,
        scratch=[pltpu.SemaphoreType.DMA],
        limit=limit,
    )[0]


def per_device(tokens, stale_keys, norm_gain, norm_bias, query_weight, pair_weight):
    place = (lax.axis_index("patch") // 2 % 4).astype(jnp.int32).reshape(1)
    table = ((SET_HEADS * CELLS, LANES), bf16)
    answer = ((ANSWER_ROWS, LANES), bf16)
    stats, tokens = call(
        local_kernel,
        [VMEM],
        [((8, LANES), f32), ((CELLS, WIDTH), bf16)],
        tokens[0],
    )
    (sets,) = call(
        sets_kernel, [VMEM, VMEM], [((4, SET_ROWS, LANES), bf16)], stats, stale_keys[0]
    )
    other = shift(stats, "core", 1)
    messages = call(
        x_kernel,
        [SMEM, VMEM, VMEM, VMEM],
        [((SET_ROWS + ROWS, LANES), bf16)] * 4,
        place,
        stats,
        other,
        sets,
    )
    received = [messages[0]] + [shift(messages[k], "x", k) for k in (1, 2, 3)]
    norm_gain, norm_bias, query_weight, _ = lax.optimization_barrier(
        (norm_gain, norm_bias, query_weight, messages[0])
    )
    (affine,) = call(affine_kernel, [VMEM] * 2, [((2, WIDTH), f32)], norm_gain, norm_bias)
    query_weight = load(query_weight, 49)
    received, affine, query_weight = lax.optimization_barrier((received, affine, query_weight))
    (part,) = call(z_kernel, [VMEM] * 4, [((4 * SET_ROWS + ROWS, LANES), bf16)], *received)
    parts = [part] + [shift(part, "z", k) for k in (2, 3, 1)]
    weights = [query_weight, load(after(pair_weight, part), 43)]
    parts, weights = lax.optimization_barrier((parts, weights))
    (stats,) = call(stats_kernel, [VMEM] * 4, [((8, LANES), f32)], *parts)
    all_stats = [stats] + [shift(stats, "y", k) for k in (1, 2, 3)]
    (piece,) = call(piece_kernel, [VMEM] * 5, [table], stats, *parts)
    pieces = [piece, shift(piece, "y", 1), shift(piece, "y", 3)]
    pieces.append(shift(after(piece, *all_stats), "y", 2))
    *queries, fresh = call(
        project_kernel,
        [SMEM] + [VMEM] * 8,
        [((ANSWER_ROWS + SET_ROWS, LANES), bf16)] * 4 + [((ROWS, 2 * WIDTH), bf16)],
        place,
        tokens,
        *all_stats,
        affine,
        *weights,
        scratch=[
            pltpu.VMEM((4, SET_ROWS, LANES), bf16),
            pltpu.VMEM((2, CELLS, LANES), bf16),
        ],
    )
    asked = {0: queries[0]}
    for k in (1, 2, 3):
        asked[k] = shift(after(queries[k], pieces[1]) if k == 3 else queries[k], "x", k)
    tables = pieces + [shift(after(block, asked[1]), "core", 1) for block in pieces]
    results = [None] * 4
    for sources in ((2, 1), (3,), (0,)):
        answers = call(
            functools.partial(attend_kernel, sources),
            [SMEM] + [VMEM] * (len(sources) + 8),
            [answer] * len(sources),
            place,
            *[asked[k] for k in sources],
            *tables,
            scratch=[pltpu.VMEM(*table)] * len(sources),
            limit=40,
        )
        for k, block in zip(sources, answers):
            results[k] = shift(block, "x", -k) if k else block
    (attended,) = call(
        assemble_kernel,
        [SMEM] + [VMEM] * 4,
        [((CELLS, WIDTH), bf16)],
        place,
        *results,
        scratch=[pltpu.VMEM((4, ANSWER_ROWS, LANES), bf16)],
    )
    return (attended[None], fresh[None])


def solution(mesh):
    return jax.shard_map(
        per_device,
        mesh=mesh,
        in_specs=(P("cfg", "patch", None), P("cfg", "patch", None), P(), P(), P(), P()),
        out_specs=(P("cfg", "patch", None), P("cfg", "patch", None)),
        check_vma=False,
    )
```

```python
import functools

import jax
import jax.numpy as jnp
from jax import lax
from jax.experimental import pallas as pl
from jax.experimental.pallas import tpu as pltpu
from jax.sharding import PartitionSpec as P

HEADS = 20
HEAD_DIM = 64
GROUPS = 32
POOL = 4
WIDTH = 1280
CELLS = 256
ROWS = 16
GROUP_WIDTH = WIDTH // GROUPS
LANES = 128
SET_HEADS = 5
SET_ROWS = SET_HEADS * ROWS
ANSWER_ROWS = SET_HEADS * CELLS // 2
epsilon = 1e-05

f32 = jnp.float32
bf16 = jnp.bfloat16
VMEM = pl.BlockSpec(memory_space=pltpu.VMEM)
SMEM = pl.BlockSpec(memory_space=pltpu.SMEM)
HBM = pl.BlockSpec(memory_space=pltpu.HBM)


def iota(shape, axis):
    return lax.broadcasted_iota(jnp.int32, shape, axis)


def group_of_channel():
    low = iota((WIDTH, LANES), 1) * GROUP_WIDTH
    channel = iota((WIDTH, LANES), 0)
    return ((channel >= low) & (channel < low + GROUP_WIDTH)).astype(f32).astype(bf16)


def channel_of_group():
    low = iota((LANES, WIDTH), 0) * GROUP_WIDTH
    channel = iota((LANES, WIDTH), 1)
    return ((channel >= low) & (channel < low + GROUP_WIDTH)).astype(f32).astype(bf16)


def split_rows(*rows):
    width = rows[0].shape[1]
    row = iota((ROWS, width), 0)
    split = jnp.zeros((ROWS, width), f32)
    for i, rest in enumerate(rows):
        for part in range(3):
            rounded = rest.astype(bf16).astype(f32)
            split = jnp.where(row == 3 * i + part, rounded, split)
            rest = rest - rounded
    return split.astype(bf16)


def join_rows(split, i):
    parts = split[3 * i : 3 * i + 3].astype(f32)
    return parts[0:1] + parts[1:2] + parts[2:3]


def select_dot(matrix, *rows):
    products = jnp.dot(split_rows(*rows), matrix, preferred_element_type=f32)
    return [join_rows(products, i) for i in range(len(rows))]


def combine(parts, entries):
    mean = sum(part[0:1] for part in parts) / len(parts)
    squares = sum(part[1:2] for part in parts)
    apart = sum((part[0:1] - mean) * (part[0:1] - mean) for part in parts)
    return mean, squares + entries * apart


def stack_stats(mean, squares):
    row = iota((8, LANES), 0)
    return jnp.where(row == 0, mean, jnp.where(row == 1, squares, 0.0))


def decode(rows):
    split = rows.astype(f32)
    return jnp.concatenate([join_rows(split, 0), join_rows(split, 1)], axis=0)


def head_tiles(pairs):
    lane = iota((ROWS, LANES), 1)
    even, odd = [], []
    for t in range(WIDTH // LANES):
        keys = pairs[:, t * LANES : (t + 1) * LANES].astype(f32)
        values = pairs[:, WIDTH + t * LANES : WIDTH + (t + 1) * LANES].astype(f32)
        turned = pltpu.roll(values, HEAD_DIM, 1)
        even.append(jnp.where(lane < HEAD_DIM, keys, turned).astype(bf16))
        odd.append(jnp.where(lane < HEAD_DIM, turned, keys).astype(bf16))
    sets = []
    for j in range(4):
        last = (even if j % 2 == 0 else odd)[8 + j // 2]
        sets.append(
            jnp.concatenate(
                [even[2 * j], odd[2 * j], even[2 * j + 1], odd[2 * j + 1], last], axis=0
            )
        )
    return sets


def turn(block):
    return pltpu.roll(block.astype(f32), HEAD_DIM, 1)


def fold(block, mask):
    half = CELLS // 2
    return jnp.where(mask, block[0:half].astype(f32), turn(block[half:])).astype(bf16)


def unfold(block):
    return jnp.concatenate([block.astype(f32), turn(block)], axis=0)


def local_kernel(tokens_ref, stats_ref, kept_ref):
    tokens = tokens_ref[...]
    kept_ref[...] = tokens
    values = tokens.astype(f32)
    (mean,) = select_dot(group_of_channel(), jnp.sum(values, axis=0, keepdims=True))
    mean = mean / (CELLS * GROUP_WIDTH)
    (center,) = select_dot(channel_of_group(), mean)
    shifted = values - center
    (squares,) = select_dot(
        group_of_channel(), jnp.sum(shifted * shifted, axis=0, keepdims=True)
    )
    stats_ref[...] = stack_stats(mean, squares)


def sets_kernel(stats_ref, stale_ref, sets_ref):
    for j, block in enumerate(head_tiles(stale_ref[...])):
        sets_ref[j] = block


def x_kernel(place_ref, own_ref, other_ref, sets_ref, *out_refs):
    mean, squares = combine([own_ref[...], other_ref[...]], CELLS * GROUP_WIDTH)
    coded = split_rows(mean, squares)
    place = place_ref[0]
    for k, out_ref in enumerate(out_refs):
        out_ref[0:SET_ROWS, :] = sets_ref[lax.rem(place + k, 4)]
        out_ref[SET_ROWS:, :] = coded


def affine_kernel(gain_ref, bias_ref, out_ref):
    out_ref[0:1, :] = gain_ref[...].reshape(1, WIDTH)
    out_ref[1:2, :] = bias_ref[...].reshape(1, WIDTH)


def z_kernel(*refs):
    *in_refs, out_ref = refs
    stats = [decode(ref[SET_ROWS:, :]) for ref in in_refs]
    mean, squares = combine(stats, 2 * CELLS * GROUP_WIDTH)
    for k, ref in enumerate(in_refs):
        for h in range(SET_HEADS):
            low = h * 4 * ROWS + k * ROWS
            out_ref[low : low + ROWS, :] = ref[h * ROWS : (h + 1) * ROWS, :]
    out_ref[4 * SET_ROWS :, :] = split_rows(mean, squares)


def stats_kernel(*refs):
    *in_refs, stats_ref = refs
    stats = [decode(ref[4 * SET_ROWS :, :]) for ref in in_refs]
    mean, squares = combine(stats, 8 * CELLS * GROUP_WIDTH)
    stats_ref[...] = stack_stats(mean, squares)


def piece_kernel(stats_ref, *refs):
    *in_refs, out_ref = refs
    for k, ref in enumerate(in_refs):
        for h in range(SET_HEADS):
            low = h * CELLS + k * 4 * ROWS
            out_ref[low : low + 4 * ROWS, :] = ref[h * 4 * ROWS : (h + 1) * 4 * ROWS, :]


def load_kernel(source_hbm, target_ref, arrived):
    copy = pltpu.make_async_copy(source_hbm, target_ref, arrived)
    copy.start()
    copy.wait()


def project_kernel(
    place_ref, tokens_ref, s0, s1, s2, s3, affine_ref, query_ref, pair_ref, *refs
):
    *message_refs, fresh_ref, sets_ref, last_ref = refs
    mean, squares = combine([s0[...], s1[...], s2[...], s3[...]], 32 * CELLS * GROUP_WIDTH)
    spread = squares / (128 * CELLS * GROUP_WIDTH)
    center, inverse = select_dot(channel_of_group(), mean, lax.rsqrt(spread + epsilon))
    scaled = (tokens_ref[...].astype(f32) - center) * inverse
    normed = (scaled * affine_ref[0:1] + affine_ref[1:2]).astype(bf16)

    square = iota((ROWS, CELLS), 0)
    cell = iota((ROWS, CELLS), 1)
    cell_square = lax.shift_right_logical(lax.bitwise_and(cell, 63), 2)
    pool = jnp.where(cell_square == square, 1.0 / (POOL * POOL), 0.0).astype(bf16)
    pooled = jnp.dot(pool, normed, preferred_element_type=f32).astype(bf16)

    place = place_ref[0]
    last = jnp.dot(normed, query_ref[:, 1024:], preferred_element_type=f32).astype(bf16)
    last_ref[0] = last[:, 0:LANES]
    last_ref[1] = last[:, LANES:]
    lane_half = lax.shift_right_logical(iota((CELLS // 2, LANES), 1), 6)
    for k in (2, 1, 3, 0):
        j = lax.rem(place + k, 4)
        columns = pl.ds(pl.multiple_of(j * 256, 256), 256)
        block = jnp.dot(normed, query_ref[:, columns], preferred_element_type=f32).astype(bf16)
        message_refs[k][0:CELLS, :] = block[:, 0:LANES]
        message_refs[k][CELLS : 2 * CELLS, :] = block[:, LANES:]
        mask = lane_half == lax.bitwise_and(j, 1)
        message_refs[k][2 * CELLS : ANSWER_ROWS, :] = fold(
            last_ref[lax.shift_right_logical(j, 1)], mask
        )

    fresh = jnp.dot(pooled, pair_ref[...], preferred_element_type=f32).astype(bf16)
    fresh_ref[...] = fresh
    for j, block in enumerate(head_tiles(fresh)):
        sets_ref[j] = block
    for k in range(4):
        message_refs[k][ANSWER_ROWS:, :] = sets_ref[lax.rem(place + k, 4)]


def attend_kernel(sources, place_ref, *refs):
    count = len(sources)
    message_refs, table_refs = refs[:count], refs[count : count + 8]
    out_refs, first_refs = refs[count + 8 : 2 * count + 8], refs[2 * count + 8 :]
    for source, message_ref, first_ref in zip(sources, message_refs, first_refs):
        first_ref[...] = table_refs[0][...]
        for h in range(SET_HEADS):
            low = h * CELLS + source * ROWS
            fresh = message_ref[ANSWER_ROWS + h * ROWS : ANSWER_ROWS + (h + 1) * ROWS, :]
            first_ref[low : low + ROWS, :] = fresh
    lane = iota((CELLS, LANES), 1)
    low_half = lane < HEAD_DIM
    parity = lax.bitwise_and(place_ref[0], 1)
    factor = HEAD_DIM ** (-0.5) * 1.4426950408889634
    against = (((1,), (1,)), ((), ()))
    ones = jnp.ones((CELLS, LANES), bf16)

    def head_scores(h):
        if h < 4:
            mask = low_half if h % 2 == 0 else jnp.logical_not(low_half)
        else:
            mask = lax.shift_right_logical(lane, 6) == parity
        groups = []
        for message_ref in message_refs:
            if h < 4:
                queries = message_ref[(h // 2) * CELLS : (h // 2 + 1) * CELLS, :].astype(f32)
            else:
                queries = unfold(message_ref[2 * CELLS : ANSWER_ROWS, :])
            groups.append(jnp.where(mask, queries, 0.0).astype(bf16))
        queries = jnp.concatenate(groups, axis=0) if count > 1 else groups[0]
        head = slice(h * CELLS, (h + 1) * CELLS)
        firsts = [
            lax.dot_general(group, ref[head, :], against, preferred_element_type=f32)
            for group, ref in zip(groups, first_refs)
        ]
        scores = [jnp.concatenate(firsts, axis=0)]
        for ref in table_refs[1:]:
            keys = ref[head, :]
            scores.append(lax.dot_general(queries, keys, against, preferred_element_type=f32))
        return scores

    def head_result(h, scores):
        head = slice(h * CELLS, (h + 1) * CELLS)
        largest = scores[0]
        for part in scores[1:]:
            largest = jnp.maximum(largest, part)
        largest = jnp.max(largest, axis=1, keepdims=True)
        summed = None
        for index, part in enumerate(scores):
            weights = jnp.exp2((part - largest) * factor).astype(bf16)
            if index == 0:
                products = []
                for g, ref in enumerate(first_refs):
                    values = jnp.concatenate([ref[head, :], ones], axis=1)
                    rows = weights[g * CELLS : (g + 1) * CELLS]
                    products.append(jnp.dot(rows, values, preferred_element_type=f32))
                summed = jnp.concatenate(products, axis=0)
            else:
                values = jnp.concatenate([table_refs[index][head, :], ones], axis=1)
                summed = summed + jnp.dot(weights, values, preferred_element_type=f32)
        return summed[:, 0:LANES] / summed[:, LANES:]

    results = []
    scores = head_scores(0)
    for h in range(SET_HEADS):
        following = head_scores(h + 1) if h + 1 < SET_HEADS else None
        results.append(head_result(h, scores))
        scores = following
    for g, out_ref in enumerate(out_refs):
        rows = slice(g * CELLS, (g + 1) * CELLS)
        for t in range(2):
            both = jnp.where(low_half, results[2 * t + 1][rows], results[2 * t][rows])
            out_ref[t * CELLS : (t + 1) * CELLS, :] = turn(both).astype(bf16)
        half = lax.shift_right_logical(iota((CELLS // 2, LANES), 1), 6)
        out_ref[2 * CELLS :, :] = fold(turn(results[4][rows]), half == parity)


def assemble_kernel(place_ref, *refs):
    *in_refs, out_ref, sets_ref = refs
    place = place_ref[0]
    for k, ref in enumerate(in_refs):
        sets_ref[lax.rem(place + k, 4)] = ref[...]
    for j in range(4):
        for t in range(2):
            low = (2 * j + t) * LANES
            out_ref[:, low : low + LANES] = sets_ref[j, t * CELLS : (t + 1) * CELLS, :]
    low_half = iota((CELLS, LANES), 1) < HEAD_DIM
    for t in range(2):
        low = (8 + t) * LANES
        both = [unfold(sets_ref[2 * t + i, 2 * CELLS :, :]) for i in range(2)]
        out_ref[:, low : low + LANES] = jnp.where(low_half, *both).astype(bf16)


def call(kernel, ins, outs, *args, scratch=(), limit=24):
    return pl.pallas_call(
        kernel,
        in_specs=ins,
        out_specs=[VMEM] * len(outs),
        out_shape=[jax.ShapeDtypeStruct(shape, kind) for shape, kind in outs],
        scratch_shapes=list(scratch),
        compiler_params=pltpu.CompilerParams(vmem_limit_bytes=limit * 1024 * 1024),
        cost_estimate=pl.CostEstimate(flops=1, bytes_accessed=1, transcendentals=0),
    )(*args)


def permute(array, place):
    pairs = []
    for source in range(128):
        z, y, x, core = place(source // 32, source // 8 % 4, source // 2 % 4, source % 2)
        pairs.append((source, z % 4 * 32 + y % 4 * 8 + x % 4 * 2 + core % 2))
    return lax.ppermute(array, "patch", pairs)


def shift(array, axis, step):
    def place(*places):
        return [at + step * (name == axis) for at, name in zip(places, ("z", "y", "x", "core"))]

    return permute(array, place)


def after(array, *others):
    return lax.optimization_barrier((array, *others))[0]


def per_device(tokens, stale_keys, norm_gain, norm_bias, query_weight, pair_weight):
    place = (lax.axis_index("patch") // 2 % 4).astype(jnp.int32).reshape(1)
    table = ((SET_HEADS * CELLS, LANES), bf16)
    answer = ((ANSWER_ROWS, LANES), bf16)
    stats, tokens = call(
        local_kernel,
        [VMEM],
        [((8, LANES), f32), ((CELLS, WIDTH), bf16)],
        tokens[0],
    )
    (sets,) = call(
        sets_kernel, [VMEM, VMEM], [((4, SET_ROWS, LANES), bf16)], stats, stale_keys[0]
    )
    other = shift(stats, "core", 1)
    messages = call(
        x_kernel,
        [SMEM, VMEM, VMEM, VMEM],
        [((SET_ROWS + ROWS, LANES), bf16)] * 4,
        place,
        stats,
        other,
        sets,
    )
    received = [messages[0]] + [shift(messages[k], "x", k) for k in (1, 2, 3)]
    norm_gain, norm_bias, _ = lax.optimization_barrier((norm_gain, norm_bias, messages[0]))
    (affine,) = call(affine_kernel, [VMEM] * 2, [((2, WIDTH), f32)], norm_gain, norm_bias)
    received, affine = lax.optimization_barrier((received, affine))
    (part,) = call(z_kernel, [VMEM] * 4, [((4 * SET_ROWS + ROWS, LANES), bf16)], *received)
    parts = [part] + [shift(part, "z", k) for k in (2, 3, 1)]
    weights = [part]
    for weight, limit in ((query_weight, 49), (pair_weight, 43)):
        weight = after(weight, weights[0])
        loaded = call(
            load_kernel,
            [HBM],
            [(weight.shape, bf16)],
            weight,
            scratch=[pltpu.SemaphoreType.DMA],
            limit=limit,
        )
        weights = [*loaded, *weights]
    weights = weights[1::-1]
    parts, weights = lax.optimization_barrier((parts, weights))
    (stats,) = call(stats_kernel, [VMEM] * 4, [((8, LANES), f32)], *parts)
    all_stats = [stats] + [shift(stats, "y", k) for k in (1, 2, 3)]
    (piece,) = call(piece_kernel, [VMEM] * 5, [table], stats, *parts)
    pieces = [piece, shift(piece, "y", 1), shift(piece, "y", 2)]
    pieces.append(shift(after(piece, *all_stats), "y", 3))
    *queries, fresh = call(
        project_kernel,
        [SMEM] + [VMEM] * 8,
        [((ANSWER_ROWS + SET_ROWS, LANES), bf16)] * 4 + [((ROWS, 2 * WIDTH), bf16)],
        place,
        tokens,
        *all_stats,
        affine,
        *weights,
        scratch=[
            pltpu.VMEM((4, SET_ROWS, LANES), bf16),
            pltpu.VMEM((2, CELLS, LANES), bf16),
        ],
    )
    asked = {0: queries[0]}
    for k in (1, 2, 3):
        asked[k] = shift(after(queries[k], pieces[1]) if k == 3 else queries[k], "x", k)
    tables = pieces + [shift(after(block, asked[1]), "core", 1) for block in pieces]
    results = [None] * 4
    for sources in ((2, 1), (3,), (0,)):
        answers = call(
            functools.partial(attend_kernel, sources),
            [SMEM] + [VMEM] * (len(sources) + 8),
            [answer] * len(sources),
            place,
            *[asked[k] for k in sources],
            *tables,
            scratch=[pltpu.VMEM(*table)] * len(sources),
            limit=40,
        )
        for k, block in zip(sources, answers):
            results[k] = shift(block, "x", -k) if k else block
    (attended,) = call(
        assemble_kernel,
        [SMEM] + [VMEM] * 4,
        [((CELLS, WIDTH), bf16)],
        place,
        *results,
        scratch=[pltpu.VMEM((4, ANSWER_ROWS, LANES), bf16)],
    )
    return (attended[None], fresh[None])


def solution(mesh):
    return jax.shard_map(
        per_device,
        mesh=mesh,
        in_specs=(P("cfg", "patch", None), P("cfg", "patch", None), P(), P(), P(), P()),
        out_specs=(P("cfg", "patch", None), P("cfg", "patch", None)),
        check_vma=False,
    )
```
